128 devices in a mesh: seq: 64 (over z, y, x_hi, core), head: 2 (over x_lo).
Axes of the slice: x: 4 (x_hi: 2, x_lo: 2; x = x_hi * 2 + x_lo), y: 4, z: 4, core: 2. Of those that a mesh axis runs over, the one named last changes fastest.
Arguments:
- queries: bfloat16 [6144, 2560], P('seq', 'head'), may hold values from -20 to 20
- keys: bfloat16 [6144, 2560], P('seq', 'head'), may hold values from -5 to 5
- values: bfloat16 [6144, 2560], P('seq', 'head'), may hold values from -6 to 6
- queries_tan: bfloat16 [6144, 2560], P('seq', 'head'), may hold values from -6 to 6
- keys_tan: bfloat16 [6144, 2560], P('seq', 'head'), may hold values from -6 to 6
- values_tan: bfloat16 [6144, 2560], P('seq', 'head'), may hold values from -6 to 6
- segments: int32 [6144], P('seq'), may hold values from 0 to 1, as said below
- positions: int32 [6144], P('seq'), may hold values from 0 to 3839, as said below
- out_weight: bfloat16 [2560, 5120], P('head'), may hold values from -0.125 to 0.125
- residual: float32 [6144, 5120], P('seq', 'head'), may hold values from -30 to 30
- residual_tan: float32 [6144, 5120], P('seq', 'head'), may hold values from -6 to 6
- gate: float32 [2, 5120], replicated, may hold values from -3 to 3
- gate_tan: float32 [2, 5120], replicated, may hold values from -3 to 3
- mod_scale: float32 [2, 5120], replicated, may hold values from -2 to 2
- mod_scale_tan: float32 [2, 5120], replicated, may hold values from -2 to 2
- mod_shift: float32 [2, 5120], replicated, may hold values from -2 to 2
- mod_shift_tan: float32 [2, 5120], replicated, may hold values from -2 to 2
Outputs:
- resid_out: float32 [6144, 5120], P('seq', 'head')
- resid_tan_out: float32 [6144, 5120], P('seq', 'head')
- ffn_in: bfloat16 [6144, 5120], P('seq')
- ffn_in_tan: bfloat16 [6144, 5120], P('seq')
The draws below stay inside these ranges and needn't reach their ends.
Inputs may be any that keep to these rules, and one draw needn't show every extreme that they name: `segments`: 0 and 1 name the two clips; each clip is one run of consecutive tokens when the last token is taken as followed by the first; one of the two clips holds exactly 3840 tokens and the other the rest. Within each clip the positions of its tokens are a permutation of 0 to the clip's length minus 1.
All inputs are finite; a program needn't handle non-finite values.
Results may differ from the reference program's by a relative error of at most 0.029.
Values may be sent and summed in bfloat16 or wider, within the bound.
No kernel may reach another device: no remote copies, remote signals or barrier semaphores. Data moves between devices by JAX's collectives and lax.ppermute only.
A program may use at most 320 MiB of HBM per device.

```python
import math
import jax
import jax.numpy as jnp
from jax import lax

D = 5120
HEADS = 20
HEAD_DIM = 128
CLIPS = 2
TOK_DEV = 96
TOKENS = 6144


def clip_layout(key):
    split_key = jax.random.fold_in(key, 7)
    order_key = jax.random.fold_in(key, 8)
    start_key = jax.random.fold_in(key, 9)
    longer = 5 * TOKENS // 8
    long_one = jax.random.randint(split_key, (), 0, 2).astype(jnp.int32)
    start_at = jax.random.randint(start_key, (), 0, TOKENS).astype(jnp.int32)
    index_rows = jnp.arange(TOKENS, dtype=jnp.int32)
    in_long = (jnp.mod(index_rows - start_at, TOKENS) < longer).astype(jnp.int32)
    clip_ids = jnp.where(in_long == 1, long_one, 1 - long_one).astype(jnp.int32)
    zero_count = jnp.sum((clip_ids == 0).astype(jnp.int32)).astype(jnp.int32)
    shuffled = jax.random.permutation(order_key, TOKENS).astype(jnp.int32)
    score_keys = clip_ids * TOKENS + shuffled
    sorted_order = jnp.argsort(score_keys)
    ranking = jnp.argsort(sorted_order).astype(jnp.int32)
    return (clip_ids, (ranking - clip_ids * zero_count).astype(jnp.int32))


def draw_segments(key, part):
    clip_ids, position = clip_layout(key)
    return clip_ids


def draw_positions(key, part):
    clip_ids, position = clip_layout(key)
    return position


def draw_queries(key, part):
    key = jax.random.fold_in(key, 51)
    scale_key, value_key = jax.random.split(key)
    row_scale = jnp.exp(jax.random.uniform(scale_key, (TOKENS, 1), minval=math.log(0.4), maxval=math.log(2.0)))
    base = jnp.clip(jax.random.normal(value_key, (TOKENS, HEADS * HEAD_DIM)), -3.0, 3.0) * row_scale
    return base.astype(jnp.bfloat16)


def draw_keys(key, part):
    key = jax.random.fold_in(key, 61)
    base = jnp.clip(jax.random.normal(key, (TOKENS, HEADS * HEAD_DIM)), -3.0, 3.0) * 1.6
    return base.astype(jnp.bfloat16)


def draw_residual(key, part):
    key = jax.random.fold_in(key, 71)
    row_key, column_key, value_key = jax.random.split(key, 3)
    row_scale = jnp.exp(jax.random.uniform(row_key, (TOKENS, 1), minval=math.log(0.3), maxval=math.log(3.0)))
    column_rise = 0.5 + jnp.arange(D, dtype=jnp.float32)[None, :] / (D - 1)
    column_scale = jnp.exp(jax.random.uniform(column_key, (1, D), minval=-0.5, maxval=0.5)) * column_rise
    base = jnp.clip(jax.random.normal(value_key, (TOKENS, D)), -4.0, 4.0)
    return (base * row_scale * column_scale).astype(jnp.float32)


def steps_of(stream_key, extent, cuts, least, largest):
    def one(axis_at, parts):
        steps = jax.random.uniform(jax.random.fold_in(jax.random.fold_in(stream_key, 6), axis_at), (parts,), jnp.float32, least / len(cuts), largest / len(cuts))
        return jnp.repeat(jnp.exp(steps), extent[axis_at] // parts).reshape((-1,) + (1,) * (len(extent) - axis_at - 1))

    gain = one(*cuts[0])
    for cut in cuts[1:]:
        gain = gain * one(*cut)
    return gain


def noise(rng, shape, scale, bound, cuts=(), kind=jnp.bfloat16):
    values = scale * jax.random.normal(rng, shape, jnp.float32)
    if cuts:
        values = values * steps_of(rng, shape, cuts, -0.22, 0.18)
    return jnp.clip(values, -bound, bound).astype(kind)


def setup_inputs(seed: int = 0) -> dict:
    key_list = jax.random.split(jax.random.key(seed), 18)
    queries = draw_queries(jax.random.fold_in(key_list[17], 71), 0)
    keys = draw_keys(jax.random.fold_in(key_list[17], 71), 0)
    values = noise(key_list[2], (TOKENS, HEADS * HEAD_DIM), 1.0, 6.0, ((0, 64), (1, 2)))
    queries_tan = noise(key_list[3], (TOKENS, HEADS * HEAD_DIM), 1.0, 6.0, ((0, 64), (1, 2)))
    keys_tan = noise(key_list[4], (TOKENS, HEADS * HEAD_DIM), 1.0, 6.0, ((0, 64), (1, 2)))
    values_tan = noise(key_list[5], (TOKENS, HEADS * HEAD_DIM), 1.0, 6.0, ((0, 64), (1, 2)))
    segments = draw_segments(jax.random.fold_in(key_list[17], 71), 0)
    positions = draw_positions(jax.random.fold_in(key_list[17], 71), 0)
    out_weight = noise(key_list[8], (HEADS * HEAD_DIM, D), (HEADS * HEAD_DIM) ** -0.5, 0.125, ((0, 2),))
    residual = draw_residual(jax.random.fold_in(key_list[17], 71), 0)
    residual_tan = noise(key_list[10], (TOKENS, D), 1.0, 6.0, ((0, 64), (1, 2)), jnp.float32)
    gate = noise(key_list[11], (CLIPS, D), 1.0, 3.0, (), jnp.float32)
    gate_tan = noise(key_list[12], (CLIPS, D), 1.0, 3.0, (), jnp.float32)
    mod_scale = noise(key_list[13], (CLIPS, D), 0.5, 2.0, (), jnp.float32)
    mod_scale_tan = noise(key_list[14], (CLIPS, D), 0.5, 2.0, (), jnp.float32)
    mod_shift = noise(key_list[15], (CLIPS, D), 0.5, 2.0, (), jnp.float32)
    mod_shift_tan = noise(key_list[16], (CLIPS, D), 0.5, 2.0, (), jnp.float32)
    return {"queries": queries, "keys": keys, "values": values, "queries_tan": queries_tan, "keys_tan": keys_tan, "values_tan": values_tan, "segments": segments, "positions": positions, "out_weight": out_weight, "residual": residual, "residual_tan": residual_tan, "gate": gate, "gate_tan": gate_tan, "mod_scale": mod_scale, "mod_scale_tan": mod_scale_tan, "mod_shift": mod_shift, "mod_shift_tan": mod_shift_tan}


neg_fill = -1e+30
norm_eps = 1e-06
rope_base = 10000.0

def rotary(flat_rows, position, head_width):
    token_count = flat_rows.shape[0]
    head_count = flat_rows.shape[1] // head_width
    half_width = head_width // 2
    per_head = flat_rows.astype(jnp.float32).reshape(token_count, head_count, head_width)
    frequency = rope_base ** (-jnp.arange(half_width, dtype=jnp.float32) / half_width)
    angles = position.astype(jnp.float32)[:, None] * frequency[None, :]
    cosine = jnp.cos(angles)[:, None, :]
    sine_part = jnp.sin(angles)[:, None, :]
    first_half = per_head[..., :half_width]
    second_half = per_head[..., half_width:]
    turned = jnp.concatenate([first_half * cosine - second_half * sine_part, first_half * sine_part + second_half * cosine], axis=-1)
    return turned.reshape(token_count, head_count * head_width).astype(jnp.bfloat16)

def pick_clip(clip_table, segments):
    return jnp.where(segments[:, None] == 1, clip_table[1][None, :], clip_table[0][None, :])

def moments(resid_rows, resid_tan_rows):
    return (lax.optimization_barrier(jnp.sum(resid_rows, axis=1)), lax.optimization_barrier(jnp.sum(resid_rows * resid_rows, axis=1)), lax.optimization_barrier(jnp.sum(resid_tan_rows, axis=1)), lax.optimization_barrier(jnp.sum(resid_rows * resid_tan_rows, axis=1)))

def finish_norm(resid_rows, resid_tan_rows, moment_sums, width, scale_rows, scale_tan_rows, shift_rows, shift_tan_rows):
    first_sum, square_sum, tan_sum, cross_sum = moment_sums
    mean_rows = first_sum / width
    rstd = lax.rsqrt(square_sum / width - mean_rows * mean_rows + norm_eps)
    mean_tan = tan_sum / width
    cov_rows = cross_sum / width - mean_rows * mean_tan
    centered = resid_rows - mean_rows[:, None]
    normed = centered * rstd[:, None]
    normed_tan = (resid_tan_rows - mean_tan[:, None]) * rstd[:, None] - centered * (rstd * rstd * rstd * cov_rows)[:, None]
    ffn_rows = (normed * (1.0 + scale_rows) + shift_rows).astype(jnp.bfloat16)
    ffn_tan_rows = (normed_tan * (1.0 + scale_rows) + normed * scale_tan_rows + shift_tan_rows).astype(jnp.bfloat16)
    return (ffn_rows, ffn_tan_rows)

def head_attention(head_items, segments):
    query_head, key_head, value_head, query_tan, key_tan, value_tan = head_items
    score_scale = 1.0 / math.sqrt(HEAD_DIM)
    block_count = TOKENS // TOK_DEV

    def query_block(block_items):
        query_rows, query_tan_rows, query_segments = block_items
        scores = jnp.dot(query_rows, key_head.T, preferred_element_type=jnp.float32) * score_scale
        score_tan = (jnp.dot(query_tan_rows, key_head.T, preferred_element_type=jnp.float32) + jnp.dot(query_rows, key_tan.T, preferred_element_type=jnp.float32)) * score_scale
        allowed = query_segments[:, None] == segments[None, :]
        row_top = lax.optimization_barrier(jnp.max(jnp.where(allowed, scores, neg_fill), axis=1, keepdims=True))
        raised = jnp.where(allowed, jnp.exp(scores - row_top), 0.0)
        weights = raised / lax.optimization_barrier(jnp.sum(raised, axis=1, keepdims=True))
        drift = lax.optimization_barrier(jnp.sum(weights * score_tan, axis=1, keepdims=True))
        weights_low = weights.astype(jnp.bfloat16)
        shifted_low = (weights * (score_tan - drift)).astype(jnp.bfloat16)
        attended = jnp.dot(weights_low, value_head, preferred_element_type=jnp.float32)
        attended_tan = jnp.dot(shifted_low, value_head, preferred_element_type=jnp.float32) + jnp.dot(weights_low, value_tan, preferred_element_type=jnp.float32)
        return (attended.astype(jnp.bfloat16), attended_tan.astype(jnp.bfloat16))
    outputs = lax.map(query_block, (query_head.reshape(block_count, TOK_DEV, HEAD_DIM), query_tan.reshape(block_count, TOK_DEV, HEAD_DIM), segments.reshape(block_count, TOK_DEV)))
    return (outputs[0].reshape(TOKENS, HEAD_DIM), outputs[1].reshape(TOKENS, HEAD_DIM))

def by_heads(flat_rows):
    return flat_rows.reshape(TOKENS, HEADS, HEAD_DIM).transpose(1, 0, 2)

def from_heads(stacked):
    return stacked.transpose(1, 0, 2).reshape(TOKENS, HEADS * HEAD_DIM)

def reference(queries, keys, values, queries_tan, keys_tan, values_tan, segments, positions, out_weight, residual, residual_tan, gate, gate_tan, mod_scale, mod_scale_tan, mod_shift, mod_shift_tan):
    rotated_queries = rotary(queries, positions, HEAD_DIM)
    rotated_keys = rotary(keys, positions, HEAD_DIM)
    rotated_queries_tan = rotary(queries_tan, positions, HEAD_DIM)
    rotated_keys_tan = rotary(keys_tan, positions, HEAD_DIM)

    def one_head(head_items):
        return head_attention(head_items, segments)
    head_outputs = lax.map(one_head, (by_heads(rotated_queries), by_heads(rotated_keys), by_heads(values), by_heads(rotated_queries_tan), by_heads(rotated_keys_tan), by_heads(values_tan)))
    attended = from_heads(head_outputs[0])
    attended_tan = from_heads(head_outputs[1])
    projected = jnp.dot(attended, out_weight, preferred_element_type=jnp.float32)
    projected_tan = jnp.dot(attended_tan, out_weight, preferred_element_type=jnp.float32)
    gate_rows = pick_clip(gate, segments)
    resid_out = residual + gate_rows * projected
    resid_tan_out = residual_tan + pick_clip(gate_tan, segments) * projected + gate_rows * projected_tan
    ffn_in, ffn_in_tan = finish_norm(resid_out, resid_tan_out, moments(resid_out, resid_tan_out), D, pick_clip(mod_scale, segments), pick_clip(mod_scale_tan, segments), pick_clip(mod_shift, segments), pick_clip(mod_shift_tan, segments))
    return (resid_out, resid_tan_out, ffn_in, ffn_in_tan)
```

```python
import math

import jax
import jax.numpy as jnp
from jax import lax
from jax.experimental import pallas as pl
from jax.experimental.pallas import tpu as pltpu
from jax.sharding import Mesh, PartitionSpec as P

D = 5120
HD = 128
NH = 10
ROWS = 96
THIRD = 32
CHIPS = 32
PARTS = 3
MSG = 240
KEYS = CHIPS * ROWS
QUERIES = CHIPS * THIRD
HALF = D // 2

QB = 8
KB = 4
QR = QB * THIRD
KR = KB * ROWS
NQ = CHIPS // QB
NK = CHIPS // KB

neg_fill = -1e30
norm_eps = 1e-06
rope_base = 10000.0
score_scale = 1.0 / math.sqrt(HD)
exp_scale = score_scale * math.log2(math.e)

f32 = jnp.float32
bf16 = jnp.bfloat16
VMEM = pl.BlockSpec(memory_space=pltpu.VMEM)


def params(**kw):
    return pltpu.CompilerParams(vmem_limit_bytes=56 * 2**20, **kw)


def pack_kernel(q_ref, k_ref, v_ref, qt_ref, kt_ref, vt_ref, cos_ref, sin_ref, seg_ref, out_ref):
    cos = cos_ref[...]
    sin = sin_ref[...]

    def rot(ref, cols):
        x = ref[:, cols].astype(f32)
        return (x * cos + jnp.roll(x, HD // 2, axis=1) * sin).astype(bf16)

    for h in range(NH):
        cols = slice(h * HD, (h + 1) * HD)
        k, kt = rot(k_ref, cols), rot(kt_ref, cols)
        q, qt = rot(q_ref, cols), rot(qt_ref, cols)
        v, vt = v_ref[:, cols], vt_ref[:, cols]
        for t in range(PARTS):
            s = h * PARTS + t
            mine = slice(t * THIRD, (t + 1) * THIRD)
            out_ref[s, 0:96, 0:128] = k
            out_ref[s, 0:96, 128:256] = kt
            out_ref[s, 96:192, 0:128] = v
            out_ref[s, 96:192, 128:256] = vt
            out_ref[s, 192:224, 0:128] = qt[mine]
            out_ref[s, 192:224, 128:256] = q[mine]
            out_ref[s, 224:240, :] = seg_ref[t]
    for s in range(NH * PARTS, CHIPS):
        out_ref[s] = jnp.zeros((MSG, 256), bf16)


def attn_kernel(q_ref, kv_ref, kseg_ref, out_ref, stat_ref, s_ref, acc_ref, acct_ref, m_ref, l_ref, d_ref, flag_ref):
    for kb in range(NK):
        row = kseg_ref[kb]
        flag_ref[0, kb] = jnp.min(row)
        flag_ref[1, kb] = jnp.max(row)

    eye = lax.broadcasted_iota(jnp.int32, (THIRD, HD), 0) == lax.broadcasted_iota(jnp.int32, (THIRD, HD), 1)
    lane = lax.broadcasted_iota(jnp.int32, (QR, HD), 1)
    nt = (((1,), (1,)), ((), ()))

    @pl.loop(0, NQ)
    def _(g):
        qq = q_ref[pl.ds(g * QB, QB), 0:THIRD, :].reshape(QR, 256)
        q = qq[:, 128:256]
        cols = []
        for i in range(QB):
            tile = q_ref[g * QB + i, 32:48, 0:128].astype(f32)
            cols.append(jnp.sum(jnp.where(eye, tile[1:2, :], 0.0), axis=1, keepdims=True))
        qseg = jnp.concatenate(cols, axis=0)
        qmin, qmax = jnp.min(qseg), jnp.max(qseg)
        m_ref[...] = jnp.full((QR, HD), neg_fill, f32)
        l_ref[...] = jnp.zeros((QR, HD), f32)
        d_ref[...] = jnp.zeros((QR, HD), f32)
        acc_ref[...] = jnp.zeros((QR, 256), f32)
        acct_ref[...] = jnp.zeros((QR, HD), f32)

        @pl.loop(0, NK)
        def _(kb):
            @pl.when((flag_ref[0, kb] <= qmax) & (flag_ref[1, kb] >= qmin))
            def _():
                k = kv_ref[pl.ds(kb * KB, KB), 0:96, 0:128].reshape(KR, HD)
                s = lax.dot_general(q, k, nt, preferred_element_type=f32)
                s = jnp.where(qseg == kseg_ref[kb], s, neg_fill)
                s_ref[kb] = s
                m = m_ref[...]
                for j in range(KR // HD):
                    m = jnp.maximum(m, s[:, j * HD : (j + 1) * HD])
                m_ref[...] = m

        top = jnp.max(m_ref[...], axis=1, keepdims=True)

        @pl.loop(0, NK)
        def _(kb):
            @pl.when((flag_ref[0, kb] <= qmax) & (flag_ref[1, kb] >= qmin))
            def _():
                kk = kv_ref[pl.ds(kb * KB, KB), 0:96, :].reshape(KR, 256)
                vv = kv_ref[pl.ds(kb * KB, KB), 96:192, :].reshape(KR, 256)
                st = lax.dot_general(qq, kk, nt, preferred_element_type=f32)
                p = jnp.exp2((s_ref[kb] - top) * exp_scale)
                pt = p * st
                l, d = l_ref[...], d_ref[...]
                for j in range(KR // HD):
                    l = l + p[:, j * HD : (j + 1) * HD]
                    d = d + pt[:, j * HD : (j + 1) * HD]
                l_ref[...] = l
                d_ref[...] = d
                acc_ref[...] += jnp.dot(p.astype(bf16), vv, preferred_element_type=f32)
                acct_ref[...] += jnp.dot(pt.astype(bf16), vv[:, 0:128], preferred_element_type=f32)

        total = jnp.sum(l_ref[...], axis=1, keepdims=True)
        inv = 1.0 / total
        drift = jnp.sum(d_ref[...], axis=1, keepdims=True) * inv * score_scale
        o = acc_ref[:, 0:128] * inv
        t = (acct_ref[...] * score_scale + acc_ref[:, 128:256]) * inv - drift * o
        out_ref[pl.ds(g * QB, QB), 0:32, :] = o.astype(bf16).reshape(QB, THIRD, HD)
        out_ref[pl.ds(g * QB, QB), 32:64, :] = t.astype(bf16).reshape(QB, THIRD, HD)
        lse = top * exp_scale + jnp.log2(total)
        stats = jnp.where(lane == 0, lse, jnp.where(lane == 1, drift, 0.0))
        stat_ref[g] = jnp.transpose(stats)[0:8, :]


def combine_kernel(a_ref, sa_ref, b_ref, sb_ref, out_ref):
    def cols(ref, g):
        tile = jnp.concatenate([ref[g], jnp.zeros((HD - 8, QR), f32)], axis=0)
        tile = jnp.transpose(tile)
        return tile[:, 0:1], tile[:, 1:2]

    for g in range(NQ):
        rows = slice(g * QB, (g + 1) * QB)
        (la, da), (lb, db) = cols(sa_ref, g), cols(sb_ref, g)
        top = jnp.maximum(la, lb)
        wa, wb = jnp.exp2(la - top), jnp.exp2(lb - top)
        inv = 1.0 / (wa + wb)
        wa, wb = wa * inv, wb * inv
        drift = wa * da + wb * db
        oa = a_ref[rows, 0:32, :].astype(f32).reshape(QR, HD)
        ta = a_ref[rows, 32:64, :].astype(f32).reshape(QR, HD)
        ob = b_ref[rows, 0:32, :].astype(f32).reshape(QR, HD)
        tb = b_ref[rows, 32:64, :].astype(f32).reshape(QR, HD)
        o = wa * oa + wb * ob
        t = wa * (ta + (da - drift) * oa) + wb * (tb + (db - drift) * ob)
        out_ref[rows, 0:32, :] = o.astype(bf16).reshape(QB, THIRD, HD)
        out_ref[rows, 32:64, :] = t.astype(bf16).reshape(QB, THIRD, HD)


CT = 512


def project_kernel(side_ref, x_ref, w_ref, seg_ref, gate_ref, gate_tan_ref, *refs, own):
    if own:
        resid_ref, resid_tan_ref, keep_ref, send_ref, lhs_ref = refs
    else:
        keep_ref, send_ref, lhs_ref = refs

    @pl.when(pl.program_id(0) == 0)
    def _():
        for h in range(NH):
            for t in range(PARTS):
                s = h * PARTS + t
                lhs_ref[t * 32 : t * 32 + 32, h * HD : (h + 1) * HD] = x_ref[s, 0:32, :]
                lhs_ref[96 + t * 32 : 128 + t * 32, h * HD : (h + 1) * HD] = x_ref[s, 32:64, :]

    out = jnp.dot(lhs_ref[...], w_ref[...], preferred_element_type=f32)
    one = seg_ref[...] == 1.0
    gate = jnp.where(one, gate_ref[1:2, :], gate_ref[0:1, :])
    gate_tan = jnp.where(one, gate_tan_ref[1:2, :], gate_tan_ref[0:1, :])
    a = gate * out[0:96]
    b = gate_tan * out[0:96] + gate * out[96:192]
    if own:
        a = a + resid_ref[...]
        b = b + resid_tan_ref[...]
    keep_ref[0] = a
    keep_ref[1] = b
    send_ref[0] = a.astype(bf16)
    send_ref[1] = b.astype(bf16)


def project(side, x, w, seg, gate, gate_tan, resid, resid_tan, own):
    steps = HALF // CT
    table = pl.BlockSpec((2, CT), lambda j, s: (0, s[0] * steps + j))
    here = pl.BlockSpec((2, ROWS, CT), lambda j, s: (0, 0, j))
    rows = pl.BlockSpec((ROWS, CT), lambda j, s: (0, j))
    return pl.pallas_call(
        lambda *refs: project_kernel(*refs, own=own),
        grid_spec=pltpu.PrefetchScalarGridSpec(
            num_scalar_prefetch=1,
            grid=(steps,),
            in_specs=[
                pl.BlockSpec((CHIPS, 64, HD), lambda j, s: (0, 0, 0)),
                pl.BlockSpec((NH * HD, CT), lambda j, s: (0, s[0] * steps + j)),
                pl.BlockSpec((ROWS, 1), lambda j, s: (0, 0)),
                table,
                table,
            ]
            + [rows, rows] * own,
            out_specs=[here, here],
            scratch_shapes=[pltpu.VMEM((2 * ROWS, NH * HD), bf16)],
        ),
        out_shape=[
            jax.ShapeDtypeStruct((2, ROWS, HALF), f32),
            jax.ShapeDtypeStruct((2, ROWS, HALF), bf16),
        ],
        compiler_params=params(),
        cost_estimate=pl.CostEstimate(flops=2 * 192 * 1280 * HALF, bytes_accessed=12 * 2**20, transcendentals=0),
    )(side, x, w, seg, gate, gate_tan, *([resid, resid_tan] if own else []))


FT = 32


def final_kernel(
    side_ref, mine_ref, other_ref, got_mine_ref, got_other_ref, seg_ref, scale_ref, scale_tan_ref, shift_ref, shift_tan_ref,
    resid_ref, resid_tan_ref, ffn_ref, ffn_tan_ref,
):
    a = (mine_ref[0] + got_mine_ref[0].astype(f32), other_ref[0] + got_other_ref[0].astype(f32))
    b = (mine_ref[1] + got_mine_ref[1].astype(f32), other_ref[1] + got_other_ref[1].astype(f32))
    resid_ref[...] = a[0]
    resid_tan_ref[...] = b[0]

    def total(x, y):
        return (jnp.sum(x, axis=1, keepdims=True) + jnp.sum(y, axis=1, keepdims=True)) / D

    mean = total(a[0], a[1])
    rstd = lax.rsqrt(total(a[0] * a[0], a[1] * a[1]) - mean * mean + norm_eps)
    mean_tan = total(b[0], b[1])
    cov = total(a[0] * b[0], a[1] * b[1]) - mean * mean_tan
    slope = rstd * rstd * rstd * cov
    one = seg_ref[...] == 1.0
    side = side_ref[0]
    for i in range(2):
        at = pl.multiple_of((side if i == 0 else 1 - side) * HALF, HALF)
        cols = pl.ds(at, HALF)

        def pick(ref):
            return jnp.where(one, ref[1:2, cols], ref[0:1, cols])

        centered = a[i] - mean
        normed = centered * rstd
        normed_tan = (b[i] - mean_tan) * rstd - centered * slope
        scale = 1.0 + pick(scale_ref)
        ffn_ref[:, cols] = (normed * scale + pick(shift_ref)).astype(bf16)
        ffn_tan_ref[:, cols] = (normed_tan * scale + normed * pick(scale_tan_ref) + pick(shift_tan_ref)).astype(bf16)


def finish(side, mine, other, got_mine, got_other, seg, scale, scale_tan, shift, shift_tan):
    pair = pl.BlockSpec((2, FT, HALF), lambda j, s: (0, j, 0))
    table = pl.BlockSpec((2, D), lambda j, s: (0, 0))
    half = pl.BlockSpec((FT, HALF), lambda j, s: (j, 0))
    full = pl.BlockSpec((FT, D), lambda j, s: (j, 0))
    return pl.pallas_call(
        final_kernel,
        grid_spec=pltpu.PrefetchScalarGridSpec(
            num_scalar_prefetch=1,
            grid=(ROWS // FT,),
            in_specs=[pair] * 4 + [pl.BlockSpec((FT, 1), lambda j, s: (j, 0))] + [table] * 4,
            out_specs=[half, half, full, full],
        ),
        out_shape=[
            jax.ShapeDtypeStruct((ROWS, HALF), f32),
            jax.ShapeDtypeStruct((ROWS, HALF), f32),
            jax.ShapeDtypeStruct((ROWS, D), bf16),
            jax.ShapeDtypeStruct((ROWS, D), bf16),
        ],
        compiler_params=params(),
    )(side, mine, other, got_mine, got_other, seg, scale, scale_tan, shift, shift_tan)


def attend(q, kv, kseg):
    return pl.pallas_call(
        attn_kernel,
        in_specs=[VMEM] * 3,
        out_specs=[VMEM] * 2,
        out_shape=[
            jax.ShapeDtypeStruct((CHIPS, 64, HD), bf16),
            jax.ShapeDtypeStruct((NQ, 8, QR), f32),
        ],
        scratch_shapes=[
            pltpu.VMEM((NK, QR, KR), f32),
            pltpu.VMEM((QR, 256), f32),
            pltpu.VMEM((QR, HD), f32),
            pltpu.VMEM((QR, HD), f32),
            pltpu.VMEM((QR, HD), f32),
            pltpu.VMEM((QR, HD), f32),
            pltpu.SMEM((2, NK), f32),
        ],
        compiler_params=params(),
        cost_estimate=pl.CostEstimate(
            flops=12 * QUERIES * KEYS * HD, bytes_accessed=6 * 2**20, transcendentals=QUERIES * KEYS
        ),
    )(q, kv, kseg)


def body(
    queries, keys, values, queries_tan, keys_tan, values_tan, segments, positions, out_weight,
    residual, residual_tan, gate, gate_tan, mod_scale, mod_scale_tan, mod_shift, mod_shift_tan,
):
    frequency = rope_base ** (-jnp.arange(HD // 2, dtype=f32) / (HD // 2))
    angles = positions.astype(f32)[:, None] * jnp.concatenate([frequency, frequency])[None, :]
    sign = jnp.where(jnp.arange(HD) < HD // 2, -1.0, 1.0).astype(f32)
    cosine, sine = jnp.cos(angles), jnp.sin(angles) * sign[None, :]
    clips = segments.astype(bf16)
    rows = jnp.stack([jnp.zeros((PARTS, 256), bf16).at[:, :ROWS].set(clips[None, :]),
                      jnp.zeros((PARTS, 256), bf16).at[:, :THIRD].set(clips.reshape(PARTS, THIRD))], axis=1)
    tiles = jnp.zeros((PARTS, 16, 256), bf16).at[:, 0:2].set(rows)

    with jax.named_scope("pack"):
        message = pl.pallas_call(
            pack_kernel,
            in_specs=[VMEM] * 9,
            out_specs=VMEM,
            out_shape=jax.ShapeDtypeStruct((CHIPS, MSG, 256), bf16),
            compiler_params=params(),
        )(queries, keys, values, queries_tan, keys_tan, values_tan, cosine, sine, tiles)
    with jax.named_scope("spread"):
        arrived = lax.all_to_all(message, ("z", "y", "x"), 0, 0, tiled=True)
    with jax.named_scope("attend"):
        swap = [(0, 1), (1, 0)]
        asked = lax.slice_in_dim(arrived, 192, MSG, axis=1)
        asked_there = lax.ppermute(asked, "c", swap)
        kseg = arrived[:, 224, :ROWS].astype(f32).reshape(NK, 1, KR)
        part, stats = attend(asked, arrived, kseg)
        part_there, stats_there = attend(asked_there, arrived, kseg)
        part_back = lax.ppermute(part_there, "c", swap)
        stats_back = lax.ppermute(stats_there, "c", swap)
        answer = pl.pallas_call(
            combine_kernel,
            in_specs=[VMEM] * 4,
            out_specs=VMEM,
            out_shape=jax.ShapeDtypeStruct((CHIPS, 64, HD), bf16),
            compiler_params=params(),
        )(part, stats, part_back, stats_back)
    with jax.named_scope("collect"):
        attended = lax.all_to_all(answer, ("z", "y", "x"), 0, 0, tiled=True)
    with jax.named_scope("project"):
        side = lax.axis_index("head").astype(jnp.int32).reshape(1)
        seg = segments.astype(f32)[:, None]
        swap = [(0, 1), (1, 0)]
        other, other_low = project(1 - side, attended, out_weight, seg, gate, gate_tan, None, None, False)
        got_mine = lax.ppermute(other_low, "head", swap)
        mine, mine_low = project(side, attended, out_weight, seg, gate, gate_tan, residual, residual_tan, True)
        got_other = lax.ppermute(mine_low, "head", swap)
    with jax.named_scope("norm"):
        return tuple(
            finish(side, mine, other, got_mine, got_other, seg, mod_scale, mod_scale_tan, mod_shift, mod_shift_tan)
        )


def solution(mesh):
    fine = Mesh(mesh.devices.reshape(4, 4, 2, 2, 2), ("z", "y", "x", "c", "head"))
    seq = ("z", "y", "x", "c")
    split = P(seq, "head")
    in_specs = (split,) * 6 + (P(seq), P(seq), P("head", None), split, split) + (P(),) * 6
    out_specs = (split, split, P(seq, None), P(seq, None))
    return jax.shard_map(body, mesh=fine, in_specs=in_specs, out_specs=out_specs, check_vma=False)
```

```python
import math

import jax
import jax.numpy as jnp
from jax import lax
from jax.experimental import pallas as pl
from jax.experimental.pallas import tpu as pltpu
from jax.sharding import Mesh, PartitionSpec as P

D = 5120
HD = 128
NH = 10
ROWS = 96
THIRD = 32
CHIPS = 32
PARTS = 3
MSG = 240
HALF = D // 2

ROUNDS = 2
W = THIRD // ROUNDS
SB = 8
KR = SB * ROWS
LONG, SHORT = (21, 3), (13, 2)
RMAX = LONG[0] * 2 * W

neg_fill = -1e30
norm_eps = 1e-06
rope_base = 10000.0
ln2 = math.log(2.0)
exp_scale = math.log2(math.e) / math.sqrt(HD)

f32 = jnp.float32
bf16 = jnp.bfloat16
i32 = jnp.int32
VMEM = pl.BlockSpec(memory_space=pltpu.VMEM)
ANY = pl.BlockSpec(memory_space=pl.ANY)
NT = (((1,), (1,)), ((), ()))


def params(mib):
    return pltpu.CompilerParams(vmem_limit_bytes=mib * 2**20)


def pack_kernel(q_ref, k_ref, v_ref, qt_ref, kt_ref, vt_ref, cos_ref, sin_ref, seg_ref, row_ref, out_ref):
    cos = cos_ref[...]
    sin = sin_ref[...]
    lane = lax.broadcasted_iota(i32, (ROWS, HD), 1)
    clips = jnp.where(lane == 0, seg_ref[...], row_ref[...]).astype(bf16)

    def rot(ref, cols, factor):
        x = ref[:, cols].astype(f32)
        y = x * cos + jnp.roll(x, HD // 2, axis=1) * sin
        return (y if factor is None else y * factor).astype(bf16)

    for h in range(NH):
        cols = slice(h * HD, (h + 1) * HD)
        k, kt = rot(k_ref, cols, None), rot(kt_ref, cols, None)
        q, qt = rot(q_ref, cols, exp_scale), rot(qt_ref, cols, exp_scale)
        v, vt = v_ref[:, cols], vt_ref[:, cols]
        for t in range(PARTS):
            s = h * PARTS + t
            at = t * THIRD
            out_ref[s, 0:96, 0:128] = k
            out_ref[s, 0:96, 128:256] = kt
            out_ref[s, 96:192, 0:128] = v
            out_ref[s, 96:192, 128:256] = vt
            out_ref[s, 192:224, 0:128] = qt[at : at + 32]
            out_ref[s, 192:224, 128:256] = q[at : at + 32]
            out_ref[s, 224:240, 0:128] = clips[at : at + 16]
            out_ref[s, 224:240, 128:256] = clips[at + 16 : at + 32]
    for s in range(NH * PARTS, CHIPS):
        out_ref[s] = jnp.zeros((MSG, 256), bf16)


def bits(tiles):
    rows = jnp.concatenate([t.astype(f32)[0:1, :] for t in tiles], axis=0)
    lane = lax.broadcasted_iota(i32, (CHIPS, HD), 1)
    at = lax.broadcasted_iota(i32, (CHIPS, 1), 0)
    power = jnp.left_shift(jnp.ones((CHIPS, 1), i32), at & 15).astype(f32)
    has0 = 1.0 - jnp.min(jnp.where(lane < 32, 1.0, rows), axis=1, keepdims=True)
    has1 = jnp.max(jnp.where(lane < 32, 0.0, rows), axis=1, keepdims=True)

    def scalar(has):
        low = jnp.sum(jnp.where(at < 16, has * power, 0.0)).astype(i32)
        high = jnp.sum(jnp.where(at < 16, 0.0, has * power)).astype(i32)
        return low | (high << 16)

    return scalar(has0), scalar(has1)


def attn_kernel(qa_ref, qb_ref, kv_ref, tie_ref, oa_ref, ob_ref, s_ref, acc_ref, acct_ref, l_ref, pen_ref, keys_ref, kind_ref, chips_ref, cut_ref, *, turn):
    del tie_ref
    own = bits([kv_ref[j, 224:240, 0:128] for j in range(CHIPS)])
    sib = bits([qb_ref[j, 32:48, 0:128] for j in range(CHIPS)])
    cut_ref[0] = i32(0)
    cut_ref[1] = i32(0)

    def sort(j, carry):
        cuts, counts = carry[0], list(carry[1:])
        has = [(own[c] >> j) & 1 for c in range(2)]
        both = has[0] & has[1]
        cut_ref[jnp.where(both == 1, jnp.minimum(cuts, 1), 2)] = j
        for c in range(2):
            at = jnp.where(has[c] == 1, counts[c], 31 - (j - counts[c]))
            keys_ref[c, at] = j
            kind_ref[c, at] = jnp.where(both == 1, 2 + 2 * c + jnp.minimum(cuts, 1), 1 - has[c])
            counts[c] = counts[c] + has[c]
            any_has = ((own[c] | sib[c]) >> j) & 1
            n = counts[2 + c]
            chips_ref[c, jnp.where(any_has == 1, n, 31 - (j - n))] = j
            counts[2 + c] = n + any_has
        return (cuts + both, *counts)

    zero = i32(0)
    counted = lax.fori_loop(0, CHIPS, sort, (zero,) * 5)
    long_clip = jnp.where(counted[4] > 16, 1, 0)

    lane = lax.broadcasted_iota(i32, (ROWS, HD), 1)
    eye = lane == lax.broadcasted_iota(i32, (ROWS, HD), 0) + 32
    pen_ref[0] = jnp.zeros((ROWS, HD), bf16)
    pen_ref[1] = jnp.where(lane == 0, neg_fill, 0.0).astype(bf16)
    for p in range(2):
        row = kv_ref[cut_ref[p], 224:240, 0:128].astype(f32)[0:1, :]
        col = jnp.sum(jnp.where(eye, row, 0.0), axis=1, keepdims=True)
        pen_ref[2 + p] = jnp.where(lane == 0, col * neg_fill, 0.0).astype(bf16)
        pen_ref[4 + p] = jnp.where(lane == 0, (1.0 - col) * neg_fill, 0.0).astype(bf16)

    rows = slice(turn * W, (turn + 1) * W)
    tag = slice(turn * HD, turn * HD + HD)
    for (chips, blocks), clip in ((LONG, long_clip), (SHORT, 1 - long_clip)):
        R = chips * 2 * W
        listed = [chips_ref[clip, i] for i in range(chips)]
        qq = jnp.concatenate([ref[j, rows, :] for j in listed for ref in (qa_ref, qb_ref)], axis=0)
        one = jnp.where(lax.broadcasted_iota(i32, (R, HD), 1) == 0, 1.0, 0.0).astype(bf16)
        q = jnp.concatenate([qq[:, 128:256], one], axis=1)
        m = jnp.full((R, HD), neg_fill, f32)
        for b in range(blocks):
            pairs = [(keys_ref[clip, b * SB + u], kind_ref[clip, b * SB + u]) for u in range(SB)]
            k = jnp.concatenate([jnp.concatenate([kv_ref[j, 0:96, 0:128], pen_ref[n]], axis=1) for j, n in pairs], axis=0)
            s = lax.dot_general(q, k, NT, preferred_element_type=f32)
            s_ref[b, 0:R] = s
            for j in range(KR // HD):
                m = jnp.maximum(m, s[:, j * HD : (j + 1) * HD])
        top = jnp.max(m, axis=1, keepdims=True)
        for b in range(blocks):
            js = [keys_ref[clip, b * SB + u] for u in range(SB)]
            k = jnp.concatenate([kv_ref[j, 0:96, :] for j in js], axis=0)
            v = jnp.concatenate([kv_ref[j, 96:192, :] for j in js], axis=0)
            v1 = jnp.concatenate([v[:, 0:128], jnp.ones((KR, HD), bf16)], axis=1)
            st = lax.dot_general(qq, k, NT, preferred_element_type=f32)
            p = jnp.exp2(s_ref[b, 0:R] - top)
            pt = (p * st).astype(bf16)
            l = p[:, 0:HD]
            for j in range(1, KR // HD):
                l = l + p[:, j * HD : (j + 1) * HD]
            acc = jnp.dot(p.astype(bf16), v, preferred_element_type=f32)
            acct = jnp.dot(pt, v1, preferred_element_type=f32)
            if b == 0:
                l_ref[0:R], acc_ref[0:R], acct_ref[0:R] = l, acc, acct
            else:
                l_ref[0:R] += l
                acc_ref[0:R] += acc
                acct_ref[0:R] += acct
        total = jnp.sum(l_ref[0:R], axis=1, keepdims=True)
        inv = 1.0 / total
        inv_tan = inv * ln2
        drift = acct_ref[0:R, 128:256] * inv_tan
        o = acc_ref[0:R, 0:128] * inv
        t = acct_ref[0:R, 0:128] * inv_tan + acc_ref[0:R, 128:256] * inv - drift * o
        lse = jnp.broadcast_to(top + jnp.log2(total), (R, HD))
        where = lax.broadcasted_iota(i32, (R, HD), 1)
        pieces = jnp.zeros((R, HD), f32)
        for first, x in ((0, lse), (3, drift)):
            for i in range(3):
                piece = x.astype(bf16).astype(f32)
                pieces = jnp.where(where == first + i, piece, pieces)
                x = x - piece
        whole = [x.astype(bf16) for x in (o, t, pieces)]
        wanted = clip.astype(f32)
        for i, j in enumerate(listed):
            for core, (q_ref, out_ref) in enumerate(((qa_ref, oa_ref), (qb_ref, ob_ref))):
                at = (2 * i + core) * W
                hit = jnp.broadcast_to(q_ref[j, 32:48, tag].astype(f32)[:, 0:1], (W, HD)) == wanted
                for n, x in enumerate(whole):
                    old = out_ref[j, n * W : (n + 1) * W, :].astype(f32)
                    out_ref[j, n * W : (n + 1) * W, :] = jnp.where(hit, x[at : at + W].astype(f32), old).astype(bf16)


def attend(asked, asked_there, arrived, tie, turn):
    out = jax.ShapeDtypeStruct((CHIPS, 3 * W, HD), bf16)
    return pl.pallas_call(
        lambda *refs: attn_kernel(*refs, turn=turn),
        in_specs=[VMEM, VMEM, VMEM, ANY],
        out_specs=[VMEM] * 2,
        out_shape=[out, out],
        scratch_shapes=[
            pltpu.VMEM((LONG[1], RMAX, KR), f32),
            pltpu.VMEM((RMAX, 256), f32),
            pltpu.VMEM((RMAX, 256), f32),
            pltpu.VMEM((RMAX, HD), f32),
            pltpu.VMEM((6, ROWS, HD), bf16),
            pltpu.SMEM((2, CHIPS), i32),
            pltpu.SMEM((2, CHIPS), i32),
            pltpu.SMEM((2, CHIPS), i32),
            pltpu.SMEM((3,), i32),
        ],
        compiler_params=params(32),
        cost_estimate=pl.CostEstimate(flops=5 * 10**9, bytes_accessed=6 * 2**20, transcendentals=2 * 10**6),
    )(asked, asked_there, arrived, tie)


def combine_kernel(a_ref, b_ref, tie_ref, out_ref):
    del tie_ref
    R = CHIPS * W

    def read(ref):
        o, t, s = [ref[:, n * W : (n + 1) * W, :].astype(f32).reshape(R, HD) for n in range(3)]
        lse = s[:, 0:1] + s[:, 1:2] + s[:, 2:3]
        drift = s[:, 3:4] + s[:, 4:5] + s[:, 5:6]
        return o, t, lse, drift

    oa, ta, la, da = read(a_ref)
    ob, tb, lb, db = read(b_ref)
    top = jnp.maximum(la, lb)
    wa, wb = jnp.exp2(la - top), jnp.exp2(lb - top)
    inv = 1.0 / (wa + wb)
    wa, wb = wa * inv, wb * inv
    gap = wa * wb * (da - db)
    out_ref[:, 0:W, :] = (wa * oa + wb * ob).astype(bf16).reshape(CHIPS, W, HD)
    out_ref[:, W : 2 * W, :] = (wa * ta + wb * tb + gap * (oa - ob)).astype(bf16).reshape(CHIPS, W, HD)


def combine(a, b, tie):
    return pl.pallas_call(
        combine_kernel,
        in_specs=[VMEM, VMEM, ANY],
        out_specs=VMEM,
        out_shape=jax.ShapeDtypeStruct((CHIPS, 2 * W, HD), bf16),
        compiler_params=params(24),
    )(a, b, tie)


CT = 512
RT = PARTS * W


def project_kernel(side_ref, x_ref, w_ref, seg_ref, gate_ref, gate_tan_ref, resid_ref, resid_tan_ref, keep_ref, send_ref, lhs_ref):
    step = pl.program_id(0)

    @pl.when(step == 0)
    def _():
        for h in range(NH):
            for t in range(PARTS):
                s = h * PARTS + t
                lhs_ref[t * W : (t + 1) * W, h * HD : (h + 1) * HD] = x_ref[s, 0:W, :]
                lhs_ref[RT + t * W : RT + (t + 1) * W, h * HD : (h + 1) * HD] = x_ref[s, W : 2 * W, :]

    out = jnp.dot(lhs_ref[...], w_ref[...], preferred_element_type=f32)
    one = seg_ref[...].reshape(RT, 1) == 1.0
    gate = jnp.where(one, gate_ref[1:2, :], gate_ref[0:1, :])
    gate_tan = jnp.where(one, gate_tan_ref[1:2, :], gate_tan_ref[0:1, :])
    mine = jnp.where(step // (HALF // CT) == side_ref[0], 1.0, 0.0).astype(f32)
    a = gate * out[0:RT] + mine * resid_ref[...].reshape(RT, CT)
    b = gate_tan * out[0:RT] + gate * out[RT : 2 * RT] + mine * resid_tan_ref[...].reshape(RT, CT)
    keep_ref[0] = a
    keep_ref[1] = b
    send_ref[0] = a.astype(bf16)
    send_ref[1] = b.astype(bf16)


def project(side, x, w, seg, gate, gate_tan, resid, resid_tan, turn):
    half_steps = HALF // CT
    table = pl.BlockSpec((2, CT), lambda j, s: (0, j))
    here = pl.BlockSpec((2, RT, CT), lambda j, s: (0, 0, j))
    rows = pl.BlockSpec((PARTS, None, W, CT), lambda j, s: (0, turn, 0, jnp.clip(j - s[0] * half_steps, 0, half_steps - 1)))
    return pl.pallas_call(
        project_kernel,
        grid_spec=pltpu.PrefetchScalarGridSpec(
            num_scalar_prefetch=1,
            grid=(D // CT,),
            in_specs=[
                pl.BlockSpec((CHIPS, 2 * W, HD), lambda j, s: (0, 0, 0)),
                pl.BlockSpec((NH * HD, CT), lambda j, s: (0, j)),
                pl.BlockSpec((PARTS, None, W, 1), lambda j, s: (0, turn, 0, 0)),
                table,
                table,
                rows,
                rows,
            ],
            out_specs=[here, here],
            scratch_shapes=[pltpu.VMEM((2 * RT, NH * HD), bf16)],
        ),
        out_shape=[
            jax.ShapeDtypeStruct((2, RT, D), f32),
            jax.ShapeDtypeStruct((2, RT, D), bf16),
        ],
        compiler_params=params(24),
        cost_estimate=pl.CostEstimate(flops=2 * 2 * RT * NH * HD * D, bytes_accessed=16 * 2**20, transcendentals=0),
    )(side, x, w, seg, gate, gate_tan, resid, resid_tan)


def norm_kernel(side_ref, keep_ref, got_ref, seg_ref, scale_ref, scale_tan_ref, shift_ref, shift_tan_ref, *refs):
    resid_ref, resid_tan_ref, ffn_ref, ffn_tan_ref = refs[-4:]
    a = keep_ref[0] + got_ref[0].astype(f32)
    b = keep_ref[1] + got_ref[1].astype(f32)
    mine = pl.ds(pl.multiple_of(side_ref[0] * HALF, HALF), HALF)
    resid_ref[...] = keep_ref[0, :, mine] + got_ref[0, :, mine].astype(f32)
    resid_tan_ref[...] = keep_ref[1, :, mine] + got_ref[1, :, mine].astype(f32)

    def average(x):
        return jnp.sum(x, axis=1, keepdims=True) / D

    mean = average(a)
    rstd = lax.rsqrt(average(a * a) - mean * mean + norm_eps)
    mean_tan = average(b)
    cov = average(a * b) - mean * mean_tan
    slope = rstd * rstd * rstd * cov
    one = seg_ref[...] == 1.0

    def pick(ref):
        return jnp.where(one, ref[1:2, :], ref[0:1, :])

    centered = a - mean
    normed = centered * rstd
    normed_tan = (b - mean_tan) * rstd - centered * slope
    scale = 1.0 + pick(scale_ref)
    ffn_ref[...] = (normed * scale + pick(shift_ref)).astype(bf16)
    ffn_tan_ref[...] = (normed_tan * scale + normed * pick(scale_tan_ref) + pick(shift_tan_ref)).astype(bf16)


def norm(side, keep, got, seg, tables, before, turn):
    pair = pl.BlockSpec((2, W, D), lambda j, s: (0, j, 0))
    table = pl.BlockSpec((2, D), lambda j, s: (0, 0))
    half = pl.BlockSpec((None, None, W, HALF), lambda j, s: (j, turn, 0, 0))
    full = pl.BlockSpec((None, None, W, D), lambda j, s: (j, turn, 0, 0))
    return pl.pallas_call(
        norm_kernel,
        grid_spec=pltpu.PrefetchScalarGridSpec(
            num_scalar_prefetch=1,
            grid=(PARTS,),
            in_specs=[pair, pair, pl.BlockSpec((None, None, W, 1), lambda j, s: (j, turn, 0, 0))] + [table] * 4 + [ANY] * len(before),
            out_specs=[half, half, full, full],
        ),
        out_shape=[
            jax.ShapeDtypeStruct((PARTS, ROUNDS, W, HALF), f32),
            jax.ShapeDtypeStruct((PARTS, ROUNDS, W, HALF), f32),
            jax.ShapeDtypeStruct((PARTS, ROUNDS, W, D), bf16),
            jax.ShapeDtypeStruct((PARTS, ROUNDS, W, D), bf16),
        ],
        input_output_aliases={8 + i: i for i in range(len(before))},
        compiler_params=params(24),
    )(side, keep, got, seg, *tables, *before)


def body(
    queries, keys, values, queries_tan, keys_tan, values_tan, segments, positions, out_weight,
    residual, residual_tan, gate, gate_tan, mod_scale, mod_scale_tan, mod_shift, mod_shift_tan,
):
    frequency = rope_base ** (-jnp.arange(HD // 2, dtype=f32) / (HD // 2))
    angles = positions.astype(f32)[:, None] * jnp.concatenate([frequency, frequency])[None, :]
    sign = jnp.where(jnp.arange(HD) < HD // 2, -1.0, 1.0).astype(f32)
    cosine, sine = jnp.cos(angles), jnp.sin(angles) * sign[None, :]
    clips = segments.astype(f32)
    seg = clips[:, None]
    row = jnp.pad(clips, (HD - ROWS, 0))[None, :]
    swap = [(0, 1), (1, 0)]

    with jax.named_scope("pack"):
        message = pl.pallas_call(
            pack_kernel,
            in_specs=[VMEM] * 10,
            out_specs=VMEM,
            out_shape=jax.ShapeDtypeStruct((CHIPS, MSG, 256), bf16),
            compiler_params=params(24),
        )(queries, keys, values, queries_tan, keys_tan, values_tan, cosine, sine, seg, row)
    with jax.named_scope("spread"):
        arrived = lax.all_to_all(message, ("z", "y", "x"), 0, 0, tiled=True)
        asked = lax.slice_in_dim(arrived, 192, MSG, axis=1)
        asked_there = lax.ppermute(asked, "c", swap)

    side = lax.axis_index("head").astype(i32).reshape(1)
    seg = seg.reshape(PARTS, ROUNDS, W, 1)
    resid = residual.reshape(PARTS, ROUNDS, W, HALF)
    resid_tan = residual_tan.reshape(PARTS, ROUNDS, W, HALF)
    tables = (mod_scale, mod_scale_tan, mod_shift, mod_shift_tan)

    def answer_of(turn, tie_attend, tie_combine):
        with jax.named_scope("attend"):
            part, part_there = attend(asked, asked_there, arrived, tie_attend, turn)
            part_back = lax.ppermute(part_there, "c", swap)
            return combine(part, part_back, side if tie_combine is None else tie_combine)

    def project_of(turn, answer):
        with jax.named_scope("collect"):
            attended = lax.all_to_all(answer, ("z", "y", "x"), 0, 0, tiled=True)
        with jax.named_scope("project"):
            return project(side, attended, out_weight, seg, gate, gate_tan, resid, resid_tan, turn)

    first = answer_of(0, side, None)
    keep0, send0 = project_of(0, first)
    second = answer_of(1, first, send0)
    got0 = lax.ppermute(send0, "head", swap)
    keep1, send1 = project_of(1, second)
    got1 = lax.ppermute(send1, "head", swap)
    with jax.named_scope("norm"):
        outs = norm(side, keep0, got0, seg, tables, (), 0)
        outs = norm(side, keep1, got1, seg, tables, outs, 1)
    return tuple(x.reshape(ROWS, -1) for x in outs)


def solution(mesh):
    fine = Mesh(mesh.devices.reshape(4, 4, 2, 2, 2), ("z", "y", "x", "c", "head"))
    seq = ("z", "y", "x", "c")
    split = P(seq, "head")
    in_specs = (split,) * 6 + (P(seq), P(seq), P("head", None), split, split) + (P(),) * 6
    out_specs = (split, split, P(seq, None), P(seq, None))
    return jax.shard_map(body, mesh=fine, in_specs=in_specs, out_specs=out_specs, check_vma=False)
```

```python
import math

import jax
import jax.numpy as jnp
from jax import lax
from jax.experimental import pallas as pl
from jax.experimental.pallas import tpu as pltpu
from jax.sharding import Mesh, PartitionSpec as P

D = 5120
HD = 128
NH = 10
ROWS = 96
THIRD = 32
CHIPS = 32
PARTS = 3
SPAN = 5
MSG = 240
HALF = D // 2

W = THIRD
SB = 8
KR = SB * ROWS
LONG, SHORT = (21, 3), (13, 2)
RMAX = LONG[0] * 2 * THIRD

neg_fill = -1e30
norm_eps = 1e-06
rope_base = 10000.0
ln2 = math.log(2.0)
exp_scale = math.log2(math.e) / math.sqrt(HD)

f32 = jnp.float32
bf16 = jnp.bfloat16
i32 = jnp.int32
VMEM = pl.BlockSpec(memory_space=pltpu.VMEM)
ANY = pl.BlockSpec(memory_space=pl.ANY)
NT = (((1,), (1,)), ((), ()))


def worker(h, t):
    return h // SPAN * (CHIPS // 2) + h % SPAN * PARTS + t


def params(mib=56):
    return pltpu.CompilerParams(vmem_limit_bytes=mib * 2**20)


def pack_kernel(q_ref, k_ref, v_ref, qt_ref, kt_ref, vt_ref, cos_ref, sin_ref, seg_ref, row_ref, out_ref):
    cos = cos_ref[...]
    sin = sin_ref[...]
    lane = lax.broadcasted_iota(i32, (ROWS, HD), 1)
    clips = jnp.where(lane == 0, seg_ref[...], row_ref[...]).astype(bf16)

    def rot(ref, cols, factor):
        x = ref[:, cols].astype(f32)
        y = x * cos + jnp.roll(x, HD // 2, axis=1) * sin
        return (y if factor is None else y * factor).astype(bf16)

    for h in range(SPAN):
        cols = slice(h * HD, (h + 1) * HD)
        k, kt = rot(k_ref, cols, None), rot(kt_ref, cols, None)
        q, qt = rot(q_ref, cols, exp_scale), rot(qt_ref, cols, exp_scale)
        v, vt = v_ref[:, cols], vt_ref[:, cols]
        for t in range(PARTS):
            s = worker(h, t)
            at = t * THIRD
            out_ref[s, 0:96, 0:128] = k
            out_ref[s, 0:96, 128:256] = kt
            out_ref[s, 96:192, 0:128] = v
            out_ref[s, 96:192, 128:256] = vt
            out_ref[s, 192:224, 0:128] = qt[at : at + 32]
            out_ref[s, 192:224, 128:256] = q[at : at + 32]
            out_ref[s, 224:240, 0:128] = clips[at : at + 16]
            out_ref[s, 224:240, 128:256] = clips[at + 16 : at + 32]
    out_ref[SPAN * PARTS] = jnp.zeros((MSG, 256), bf16)


def bits(tiles):
    rows = jnp.concatenate([t.astype(f32)[0:1, :] for t in tiles], axis=0)
    lane = lax.broadcasted_iota(i32, (CHIPS, HD), 1)
    at = lax.broadcasted_iota(i32, (CHIPS, 1), 0)
    power = jnp.left_shift(jnp.ones((CHIPS, 1), i32), at & 15).astype(f32)
    has0 = 1.0 - jnp.min(jnp.where(lane < 32, 1.0, rows), axis=1, keepdims=True)
    has1 = jnp.max(jnp.where(lane < 32, 0.0, rows), axis=1, keepdims=True)

    def scalar(has):
        low = jnp.sum(jnp.where(at < 16, has * power, 0.0)).astype(i32)
        high = jnp.sum(jnp.where(at < 16, 0.0, has * power)).astype(i32)
        return low | (high << 16)

    return scalar(has0), scalar(has1)


def attn_kernel(qa_ref, qb_ref, kv_ref, oa_ref, ob_ref, s_ref, acc_ref, acct_ref, l_ref, pen_ref, keys_ref, kind_ref, chips_ref, cut_ref):
    own = bits([kv_ref[j, 224:240, 0:128] for j in range(CHIPS)])
    sib = bits([qb_ref[j, 32:48, 0:128] for j in range(CHIPS)])
    cut_ref[0] = i32(0)
    cut_ref[1] = i32(0)

    def sort(j, carry):
        cuts, counts = carry[0], list(carry[1:])
        has = [(own[c] >> j) & 1 for c in range(2)]
        both = has[0] & has[1]
        cut_ref[jnp.where(both == 1, jnp.minimum(cuts, 1), 2)] = j
        for c in range(2):
            at = jnp.where(has[c] == 1, counts[c], 31 - (j - counts[c]))
            keys_ref[c, at] = j
            kind_ref[c, at] = jnp.where(both == 1, 2 + 2 * c + jnp.minimum(cuts, 1), 1 - has[c])
            counts[c] = counts[c] + has[c]
            any_has = ((own[c] | sib[c]) >> j) & 1
            n = counts[2 + c]
            chips_ref[c, jnp.where(any_has == 1, n, 31 - (j - n))] = j
            counts[2 + c] = n + any_has
        return (cuts + both, *counts)

    zero = i32(0)
    counted = lax.fori_loop(0, CHIPS, sort, (zero,) * 5)
    long_clip = jnp.where(counted[4] > 16, 1, 0)

    lane = lax.broadcasted_iota(i32, (ROWS, HD), 1)
    eye = lane == lax.broadcasted_iota(i32, (ROWS, HD), 0) + 32
    pen_ref[0] = jnp.zeros((ROWS, HD), bf16)
    pen_ref[1] = jnp.where(lane == 0, neg_fill, 0.0).astype(bf16)
    for p in range(2):
        row = kv_ref[cut_ref[p], 224:240, 0:128].astype(f32)[0:1, :]
        col = jnp.sum(jnp.where(eye, row, 0.0), axis=1, keepdims=True)
        pen_ref[2 + p] = jnp.where(lane == 0, col * neg_fill, 0.0).astype(bf16)
        pen_ref[4 + p] = jnp.where(lane == 0, (1.0 - col) * neg_fill, 0.0).astype(bf16)

    for (chips, blocks), clip in ((LONG, long_clip), (SHORT, 1 - long_clip)):
        R = chips * 2 * THIRD
        listed = [chips_ref[clip, i] for i in range(chips)]
        qq = jnp.concatenate([ref[j, 0:THIRD, :] for j in listed for ref in (qa_ref, qb_ref)], axis=0)
        one = jnp.where(lax.broadcasted_iota(i32, (R, HD), 1) == 0, 1.0, 0.0).astype(bf16)
        q = jnp.concatenate([qq[:, 128:256], one], axis=1)
        m = jnp.full((R, HD), neg_fill, f32)
        for b in range(blocks):
            pairs = [(keys_ref[clip, b * SB + u], kind_ref[clip, b * SB + u]) for u in range(SB)]
            k = jnp.concatenate([jnp.concatenate([kv_ref[j, 0:96, 0:128], pen_ref[n]], axis=1) for j, n in pairs], axis=0)
            s = lax.dot_general(q, k, NT, preferred_element_type=f32)
            s_ref[b, 0:R] = s
            for j in range(KR // HD):
                m = jnp.maximum(m, s[:, j * HD : (j + 1) * HD])
        top = jnp.max(m, axis=1, keepdims=True)
        for b in range(blocks):
            js = [keys_ref[clip, b * SB + u] for u in range(SB)]
            k = jnp.concatenate([kv_ref[j, 0:96, :] for j in js], axis=0)
            v = jnp.concatenate([kv_ref[j, 96:192, :] for j in js], axis=0)
            v1 = jnp.concatenate([v[:, 0:128], jnp.ones((KR, HD), bf16)], axis=1)
            st = lax.dot_general(qq, k, NT, preferred_element_type=f32)
            p = jnp.exp2(s_ref[b, 0:R] - top)
            pt = (p * st).astype(bf16)
            l = p[:, 0:HD]
            for j in range(1, KR // HD):
                l = l + p[:, j * HD : (j + 1) * HD]
            acc = jnp.dot(p.astype(bf16), v, preferred_element_type=f32)
            acct = jnp.dot(pt, v1, preferred_element_type=f32)
            if b == 0:
                l_ref[0:R], acc_ref[0:R], acct_ref[0:R] = l, acc, acct
            else:
                l_ref[0:R] += l
                acc_ref[0:R] += acc
                acct_ref[0:R] += acct
        total = jnp.sum(l_ref[0:R], axis=1, keepdims=True)
        inv = 1.0 / total
        inv_tan = inv * ln2
        drift = acct_ref[0:R, 128:256] * inv_tan
        o = acc_ref[0:R, 0:128] * inv
        t = acct_ref[0:R, 0:128] * inv_tan + acc_ref[0:R, 128:256] * inv - drift * o
        lse = jnp.broadcast_to(top + jnp.log2(total), (R, HD))
        where = lax.broadcasted_iota(i32, (R, HD), 1)
        pieces = jnp.zeros((R, HD), f32)
        for first, x in ((0, lse), (3, drift)):
            for i in range(3):
                piece = x.astype(bf16).astype(f32)
                pieces = jnp.where(where == first + i, piece, pieces)
                x = x - piece
        whole = [x.astype(bf16) for x in (o, t, pieces)]
        wanted = clip.astype(f32)
        for i, j in enumerate(listed):
            for core, (q_ref, out_ref) in enumerate(((qa_ref, oa_ref), (qb_ref, ob_ref))):
                at = (2 * i + core) * W
                tags = q_ref[j, 32:48, :].astype(f32)
                tag = jnp.concatenate([tags[:, 0:1], tags[:, HD : HD + 1]], axis=0)
                hit = jnp.broadcast_to(tag, (W, HD)) == wanted
                for n, x in enumerate(whole):
                    old = out_ref[j, n * W : (n + 1) * W, :].astype(f32)
                    out_ref[j, n * W : (n + 1) * W, :] = jnp.where(hit, x[at : at + W].astype(f32), old).astype(bf16)


def attend(asked, asked_there, arrived):
    out = jax.ShapeDtypeStruct((CHIPS, 3 * W, HD), bf16)
    return pl.pallas_call(
        attn_kernel,
        in_specs=[VMEM] * 3,
        out_specs=[VMEM] * 2,
        out_shape=[out] * 2,
        scratch_shapes=[
            pltpu.VMEM((LONG[1], RMAX, KR), f32),
            pltpu.VMEM((RMAX, 256), f32),
            pltpu.VMEM((RMAX, 256), f32),
            pltpu.VMEM((RMAX, HD), f32),
            pltpu.VMEM((6, ROWS, HD), bf16),
            pltpu.SMEM((2, CHIPS), i32),
            pltpu.SMEM((2, CHIPS), i32),
            pltpu.SMEM((2, CHIPS), i32),
            pltpu.SMEM((3,), i32),
        ],
        compiler_params=params(40),
        cost_estimate=pl.CostEstimate(flops=5 * 10**9, bytes_accessed=6 * 2**20, transcendentals=2 * 10**6),
    )(asked, asked_there, arrived)


def combine_kernel(a_ref, b_ref, out_ref):
    R = CHIPS * W

    def read(ref):
        o, t, s = [ref[:, n * W : (n + 1) * W, :].astype(f32).reshape(R, HD) for n in range(3)]
        lse = s[:, 0:1] + s[:, 1:2] + s[:, 2:3]
        drift = s[:, 3:4] + s[:, 4:5] + s[:, 5:6]
        return o, t, lse, drift

    oa, ta, la, da = read(a_ref)
    ob, tb, lb, db = read(b_ref)
    top = jnp.maximum(la, lb)
    wa, wb = jnp.exp2(la - top), jnp.exp2(lb - top)
    inv = 1.0 / (wa + wb)
    wa, wb = wa * inv, wb * inv
    gap = wa * wb * (da - db)
    out_ref[:, 0:W, :] = (wa * oa + wb * ob).astype(bf16).reshape(CHIPS, W, HD)
    out_ref[:, W : 2 * W, :] = (wa * ta + wb * tb + gap * (oa - ob)).astype(bf16).reshape(CHIPS, W, HD)


def combine(a, b):
    return pl.pallas_call(
        combine_kernel,
        in_specs=[VMEM, VMEM],
        out_specs=VMEM,
        out_shape=jax.ShapeDtypeStruct((CHIPS, 2 * W, HD), bf16),
        compiler_params=params(16),
    )(a, b)


CT = 512
STEPS = HALF // CT


def project_kernel(side_ref, x_ref, w_ref, seg_ref, gate_ref, gate_tan_ref, *refs, own):
    if own:
        resid_ref, resid_tan_ref, keep_ref, send_ref, lhs_ref, held_ref, sem = refs
    else:
        keep_ref, send_ref, lhs_ref, held_ref, sem = refs
    start = side_ref[0] * HALF
    copies = []
    for j in range(STEPS):
        cols = pl.ds(pl.multiple_of(start + j * CT, CT), CT)
        copies.append(pltpu.make_async_copy(w_ref.at[:, cols], held_ref.at[j], sem.at[j]))
        copies[j].start()
    for h in range(NH):
        for t in range(PARTS):
            s = worker(h, t)
            lhs_ref[t * W : (t + 1) * W, h * HD : (h + 1) * HD] = x_ref[s, 0:W, :]
            lhs_ref[ROWS + t * W : ROWS + (t + 1) * W, h * HD : (h + 1) * HD] = x_ref[s, W : 2 * W, :]
    one = seg_ref[...] == 1.0
    for j in range(STEPS):
        copies[j].wait()
        out = jnp.dot(lhs_ref[...], held_ref[j], preferred_element_type=f32)
        cols = pl.ds(pl.multiple_of(start + j * CT, CT), CT)
        here = slice(j * CT, (j + 1) * CT)
        gate = jnp.where(one, gate_ref[1:2, cols], gate_ref[0:1, cols])
        gate_tan = jnp.where(one, gate_tan_ref[1:2, cols], gate_tan_ref[0:1, cols])
        a = gate * out[0:ROWS]
        b = gate_tan * out[0:ROWS] + gate * out[ROWS : 2 * ROWS]
        if own:
            a = a + resid_ref[:, here]
            b = b + resid_tan_ref[:, here]
        keep_ref[0, :, here] = a
        keep_ref[1, :, here] = b
        send_ref[0, :, here] = a.astype(bf16)
        send_ref[1, :, here] = b.astype(bf16)


def project(side, x, w, seg, gate, gate_tan, resid):
    own = len(resid) > 0
    return pl.pallas_call(
        lambda *refs: project_kernel(*refs, own=own),
        in_specs=[pl.BlockSpec(memory_space=pltpu.SMEM), VMEM, ANY] + [VMEM] * (3 + len(resid)),
        out_specs=[VMEM] * 2,
        out_shape=[
            jax.ShapeDtypeStruct((2, ROWS, HALF), f32),
            jax.ShapeDtypeStruct((2, ROWS, HALF), bf16),
        ],
        scratch_shapes=[
            pltpu.VMEM((2 * ROWS, NH * HD), bf16),
            pltpu.VMEM((STEPS, NH * HD, CT), bf16),
            pltpu.SemaphoreType.DMA((STEPS,)),
        ],
        compiler_params=params(52),
        cost_estimate=pl.CostEstimate(flops=2 * 2 * ROWS * NH * HD * HALF, bytes_accessed=10 * 2**20, transcendentals=0),
    )(side, x, w, seg, gate, gate_tan, *resid)


def sums(a, b):
    parts = [jnp.sum(x, axis=1, keepdims=True) for x in (a, a * a, b, a * b)]
    lane = lax.broadcasted_iota(i32, (a.shape[0], HD), 1)
    out = jnp.zeros((a.shape[0], HD), f32)
    for i, x in enumerate(parts):
        out = jnp.where(lane == i, x, out)
    return out


def settle_kernel(keep_ref, got_ref, resid_ref, resid_tan_ref, sums_ref):
    a = keep_ref[0] + got_ref[0].astype(f32)
    b = keep_ref[1] + got_ref[1].astype(f32)
    resid_ref[...] = a
    resid_tan_ref[...] = b
    sums_ref[...] = sums(a, b)


FT = 32


def settle(keep, got):
    pair = pl.BlockSpec((2, FT, HALF), lambda j: (0, j, 0))
    half = pl.BlockSpec((FT, HALF), lambda j: (j, 0))
    return pl.pallas_call(
        settle_kernel,
        grid=(ROWS // FT,),
        in_specs=[pair, pair],
        out_specs=[half, half, pl.BlockSpec((FT, HD), lambda j: (j, 0))],
        out_shape=[
            jax.ShapeDtypeStruct((ROWS, HALF), f32),
            jax.ShapeDtypeStruct((ROWS, HALF), f32),
            jax.ShapeDtypeStruct((ROWS, HD), f32),
        ],
        compiler_params=params(24),
    )(keep, got)


def norm_kernel(side_ref, a_ref, b_ref, sums_ref, keep_ref, got_ref, seg_ref, scale_ref, scale_tan_ref, shift_ref, shift_tan_ref, ffn_ref, ffn_tan_ref):
    other = keep_ref[0] + got_ref[0].astype(f32)
    other_tan = keep_ref[1] + got_ref[1].astype(f32)
    total = (sums_ref[...] + sums(other, other_tan)) / D
    mean, mean_tan = total[:, 0:1], total[:, 2:3]
    rstd = lax.rsqrt(total[:, 1:2] - mean * mean + norm_eps)
    cov = total[:, 3:4] - mean * mean_tan
    slope = rstd * rstd * rstd * cov
    one = seg_ref[...] == 1.0
    for side, a, b in ((1 - side_ref[0], other, other_tan), (side_ref[0], a_ref[...], b_ref[...])):
        cols = pl.ds(pl.multiple_of(side * HALF, HALF), HALF)

        def pick(ref):
            return jnp.where(one, ref[1:2, cols], ref[0:1, cols])

        centered = a - mean
        normed = centered * rstd
        normed_tan = (b - mean_tan) * rstd - centered * slope
        scale = 1.0 + pick(scale_ref)
        ffn_ref[:, cols] = (normed * scale + pick(shift_ref)).astype(bf16)
        ffn_tan_ref[:, cols] = (normed_tan * scale + normed * pick(scale_tan_ref) + pick(shift_tan_ref)).astype(bf16)


def norm(side, a, b, moments, keep, got, seg, tables):
    pair = pl.BlockSpec((2, FT, HALF), lambda j: (0, j, 0))
    half = pl.BlockSpec((FT, HALF), lambda j: (j, 0))
    full = pl.BlockSpec((FT, D), lambda j: (j, 0))
    return pl.pallas_call(
        norm_kernel,
        grid=(ROWS // FT,),
        in_specs=[pl.BlockSpec(memory_space=pltpu.SMEM), half, half, pl.BlockSpec((FT, HD), lambda j: (j, 0)), pair, pair, pl.BlockSpec((FT, 1), lambda j: (j, 0))]
        + [pl.BlockSpec((2, D), lambda j: (0, 0))] * 4,
        out_specs=[full, full],
        out_shape=[
            jax.ShapeDtypeStruct((ROWS, D), bf16),
            jax.ShapeDtypeStruct((ROWS, D), bf16),
        ],
        compiler_params=params(24),
    )(side, a, b, moments, keep, got, seg, *tables)


def body(
    queries, keys, values, queries_tan, keys_tan, values_tan, segments, positions, out_weight,
    residual, residual_tan, gate, gate_tan, mod_scale, mod_scale_tan, mod_shift, mod_shift_tan,
):
    frequency = rope_base ** (-jnp.arange(HD // 2, dtype=f32) / (HD // 2))
    angles = positions.astype(f32)[:, None] * jnp.concatenate([frequency, frequency])[None, :]
    sign = jnp.where(jnp.arange(HD) < HD // 2, -1.0, 1.0).astype(f32)
    cosine, sine = jnp.cos(angles), jnp.sin(angles) * sign[None, :]
    clips = segments.astype(f32)
    seg = clips[:, None]
    row = jnp.pad(clips, (HD - ROWS, 0))[None, :]
    swap = [(0, 1), (1, 0)]

    with jax.named_scope("pack"):
        message = pl.pallas_call(
            pack_kernel,
            grid=(NH // SPAN,),
            in_specs=[pl.BlockSpec((ROWS, SPAN * HD), lambda j: (0, j))] * 6
            + [pl.BlockSpec((ROWS, HD), lambda j: (0, 0))] * 2
            + [pl.BlockSpec((ROWS, 1), lambda j: (0, 0)), pl.BlockSpec((1, HD), lambda j: (0, 0))],
            out_specs=pl.BlockSpec((CHIPS // 2, MSG, 256), lambda j: (j, 0, 0)),
            out_shape=jax.ShapeDtypeStruct((CHIPS, MSG, 256), bf16),
            compiler_params=params(),
        )(queries, keys, values, queries_tan, keys_tan, values_tan, cosine, sine, seg, row)
    with jax.named_scope("spread"):
        arrived = lax.all_to_all(message, ("z", "y", "x"), 0, 0, tiled=True)
        asked = lax.slice_in_dim(arrived, 192, MSG, axis=1)
        asked_there = lax.ppermute(asked, "c", swap)

    side = lax.axis_index("head").astype(i32).reshape(1)
    with jax.named_scope("attend"):
        part, there = attend(asked, asked_there, arrived)
        back = lax.ppermute(there, "c", swap)
        answer = combine(part, back)
    with jax.named_scope("collect"):
        attended = lax.all_to_all(answer, ("z", "y", "x"), 0, 0, tiled=True)
    with jax.named_scope("project"):
        keep_other, send_other = project(1 - side, attended, out_weight, seg, gate, gate_tan, ())
        got_mine = lax.ppermute(send_other, "head", swap)
        keep_mine, send_mine = project(side, attended, out_weight, seg, gate, gate_tan, (residual, residual_tan))
        got_other = lax.ppermute(send_mine, "head", swap)
    with jax.named_scope("norm"):
        resid, resid_tan, moments = settle(keep_mine, got_mine)
        tables = (mod_scale, mod_scale_tan, mod_shift, mod_shift_tan)
        ffn, ffn_tan = norm(side, resid, resid_tan, moments, keep_other, got_other, seg, tables)
    return resid, resid_tan, ffn, ffn_tan


def solution(mesh):
    fine = Mesh(mesh.devices.reshape(4, 4, 2, 2, 2), ("z", "y", "x", "c", "head"))
    seq = ("z", "y", "x", "c")
    split = P(seq, "head")
    in_specs = (split,) * 6 + (P(seq), P(seq), P("head", None), split, split) + (P(),) * 6
    out_specs = (split, split, P(seq, None), P(seq, None))
    return jax.shard_map(body, mesh=fine, in_specs=in_specs, out_specs=out_specs, check_vma=False)
```

```python
import math

import jax
import jax.numpy as jnp
import numpy as np
from jax import lax
from jax.experimental import pallas as pl
from jax.experimental.pallas import tpu as pltpu
from jax.sharding import Mesh, PartitionSpec as P

D = 5120
HD = 128
NH = 10
ROWS = 96
THIRD = 32
CHIPS = 32
PARTS = 3
SPAN = 5
K, KT, V, VT, QT, Q, TAG, MSG = 0, 96, 192, 288, 384, 416, 448, 464
ASK = QT
HALF = D // 2

W = THIRD
SB = 8
KR = SB * ROWS
LONG, SHORT = (21, 3), (13, 2)
RMAX = LONG[0] * 2 * THIRD

neg_fill = -1e30
norm_eps = 1e-06
rope_base = 10000.0
ln2 = math.log(2.0)
exp_scale = math.log2(math.e) / math.sqrt(HD)

f32 = jnp.float32
bf16 = jnp.bfloat16
i32 = jnp.int32
VMEM = pl.BlockSpec(memory_space=pltpu.VMEM)
ANY = pl.BlockSpec(memory_space=pl.ANY)
NT = (((1,), (1,)), ((), ()))


def worker(h, t):
    return h // SPAN * (CHIPS // 2) + h % SPAN * PARTS + t


def params(mib=56):
    return pltpu.CompilerParams(vmem_limit_bytes=mib * 2**20)


def pack_kernel(q_hbm, k_hbm, v_hbm, qt_hbm, kt_hbm, vt_hbm, freq_ref, pos_ref, seg_ref, out_ref, tag_ref, held_ref, sem_in):
    reads = [pltpu.make_async_copy(x, held_ref.at[i], sem_in.at[i]) for i, x in enumerate((q_hbm, k_hbm, v_hbm, qt_hbm, kt_hbm, vt_hbm))]
    for copy in reads:
        copy.start()
    lane = lax.broadcasted_iota(i32, (ROWS, HD), 1)
    eye = lane == lax.broadcasted_iota(i32, (ROWS, HD), 0)
    pad = jnp.zeros((1, HD - ROWS), f32)
    clip_row = seg_ref[...].astype(f32)

    def column(row):
        return jnp.sum(jnp.where(eye, jnp.concatenate([row, pad], axis=1), 0.0), axis=1, keepdims=True)

    tag = column(clip_row)
    tag_ref[...] = jnp.broadcast_to(tag, (ROWS, HD))
    row = jnp.concatenate([pad, clip_row], axis=1)
    clips = []
    for t in range(PARTS):
        first, last = (tag[t * THIRD + i : t * THIRD + i + 16] for i in (0, 16))
        clips.append(jnp.where(lane[0:16] == 0, first, jnp.where(lane[0:16] == 1, last, row)).astype(bf16))
    angles = column(pos_ref[...].astype(f32)) * freq_ref[...]
    cos = jnp.cos(angles)
    sin = jnp.where(lane < HD // 2, -1.0, 1.0) * jnp.sin(angles)

    def rot(i, cols, factor):
        x = held_ref[i, :, cols].astype(f32)
        y = x * cos + jnp.roll(x, HD // 2, axis=1) * sin
        return (y if factor is None else y * factor).astype(bf16)

    for copy in reads:
        copy.wait()
    writes = []
    for h in range(NH):
        cols = slice(h * HD, (h + 1) * HD)
        q, k = rot(0, cols, exp_scale), rot(1, cols, None)
        qt, kt = rot(3, cols, exp_scale), rot(4, cols, None)
        v, vt = held_ref[2, :, cols], held_ref[5, :, cols]
        for t in range(PARTS):
            s = worker(h, t)
            at = t * THIRD
            out_ref[s, K:KT] = k
            out_ref[s, KT:V] = kt
            out_ref[s, V:VT] = v
            out_ref[s, VT:QT] = vt
            out_ref[s, QT:Q] = qt[at : at + THIRD]
            out_ref[s, Q:TAG] = q[at : at + THIRD]
            out_ref[s, TAG:MSG] = clips[t]
        if h % SPAN == SPAN - 1:
            out_ref[worker(h, 0) + PARTS] = jnp.zeros((MSG, HD), bf16)


def in_hbm(x):
    return pltpu.with_memory_space_constraint(x, pltpu.HBM)


def pack(arrays, freq, positions, segments):
    return pl.pallas_call(
        pack_kernel,
        in_specs=[ANY] * 6 + [VMEM] * 3,
        out_specs=[VMEM, VMEM],
        out_shape=[pltpu.VMEM((CHIPS, MSG, HD), bf16), pltpu.VMEM((ROWS, HD), f32)],
        scratch_shapes=[
            pltpu.VMEM((6, ROWS, NH * HD), bf16),
            pltpu.SemaphoreType.DMA((6,)),
        ],
        compiler_params=params(40),
    )(*[in_hbm(x) for x in (*arrays, freq, positions, segments)])


def bits(tiles):
    rows = jnp.concatenate([t.astype(f32)[0:1, :] for t in tiles], axis=0)
    lane = lax.broadcasted_iota(i32, (CHIPS, HD), 1)
    at = lax.broadcasted_iota(i32, (CHIPS, 1), 0)
    power = jnp.left_shift(jnp.ones((CHIPS, 1), i32), at & 15).astype(f32)
    has0 = 1.0 - jnp.min(jnp.where(lane < 32, 1.0, rows), axis=1, keepdims=True)
    has1 = jnp.max(jnp.where(lane < 32, 0.0, rows), axis=1, keepdims=True)

    def scalar(has):
        low = jnp.sum(jnp.where(at < 16, has * power, 0.0)).astype(i32)
        high = jnp.sum(jnp.where(at < 16, 0.0, has * power)).astype(i32)
        return low | (high << 16)

    return scalar(has0), scalar(has1)


def attn_kernel(qa_ref, qb_ref, kv_ref, oa_ref, ob_ref, s_ref, acc_ref, acct_ref, l_ref, pen_ref, keys_ref, kind_ref, chips_ref, cut_ref):
    own = bits([kv_ref[j, TAG:MSG, :] for j in range(CHIPS)])
    sib = bits([qb_ref[j, TAG - ASK : MSG - ASK, :] for j in range(CHIPS)])
    cut_ref[0] = i32(0)
    cut_ref[1] = i32(0)

    def sort(j, carry):
        cuts, counts = carry[0], list(carry[1:])
        has = [(own[c] >> j) & 1 for c in range(2)]
        both = has[0] & has[1]
        cut_ref[jnp.where(both == 1, jnp.minimum(cuts, 1), 2)] = j
        for c in range(2):
            at = jnp.where(has[c] == 1, counts[c], 31 - (j - counts[c]))
            keys_ref[c, at] = j
            kind_ref[c, at] = jnp.where(both == 1, 2 + 2 * c + jnp.minimum(cuts, 1), 1 - has[c])
            counts[c] = counts[c] + has[c]
            any_has = ((own[c] | sib[c]) >> j) & 1
            n = counts[2 + c]
            chips_ref[c, jnp.where(any_has == 1, n, 31 - (j - n))] = j
            counts[2 + c] = n + any_has
        return (cuts + both, *counts)

    zero = i32(0)
    counted = lax.fori_loop(0, CHIPS, sort, (zero,) * 5)
    long_clip = jnp.where(counted[4] > 16, 1, 0)

    lane = lax.broadcasted_iota(i32, (ROWS, HD), 1)
    eye = lane == lax.broadcasted_iota(i32, (ROWS, HD), 0) + 32
    pen_ref[0] = jnp.zeros((ROWS, HD), bf16)
    pen_ref[1] = jnp.where(lane == 0, neg_fill, 0.0).astype(bf16)
    for p in range(2):
        row = kv_ref[cut_ref[p], TAG:MSG, :].astype(f32)[0:1, :]
        col = jnp.sum(jnp.where(eye, row, 0.0), axis=1, keepdims=True)
        pen_ref[2 + p] = jnp.where(lane == 0, col * neg_fill, 0.0).astype(bf16)
        pen_ref[4 + p] = jnp.where(lane == 0, (1.0 - col) * neg_fill, 0.0).astype(bf16)

    for (chips, blocks), clip in ((LONG, long_clip), (SHORT, 1 - long_clip)):
        R = chips * 2 * THIRD
        listed = [chips_ref[clip, i] for i in range(chips)]
        qt, q = [jnp.concatenate([ref[j, at - ASK : at - ASK + THIRD, :] for j in listed for ref in (qa_ref, qb_ref)], axis=0) for at in (QT, Q)]
        qq = jnp.concatenate([qt, q], axis=1)
        one = jnp.where(lax.broadcasted_iota(i32, (R, HD), 1) == 0, 1.0, 0.0).astype(bf16)
        q = jnp.concatenate([q, one], axis=1)
        m = jnp.full((R, HD), neg_fill, f32)
        for b in range(blocks):
            pairs = [(keys_ref[clip, b * SB + u], kind_ref[clip, b * SB + u]) for u in range(SB)]
            k = jnp.concatenate([jnp.concatenate([kv_ref[j, K:KT, :], pen_ref[n]], axis=1) for j, n in pairs], axis=0)
            s = lax.dot_general(q, k, NT, preferred_element_type=f32)
            s_ref[b, 0:R] = s
            for j in range(KR // HD):
                m = jnp.maximum(m, s[:, j * HD : (j + 1) * HD])
        top = jnp.max(m, axis=1, keepdims=True)
        for b in range(blocks):
            js = [keys_ref[clip, b * SB + u] for u in range(SB)]
            k, kt, v, vt = [jnp.concatenate([kv_ref[j, at : at + ROWS, :] for j in js], axis=0) for at in (K, KT, V, VT)]
            k = jnp.concatenate([k, kt], axis=1)
            v1 = jnp.concatenate([v, jnp.ones((KR, HD), bf16)], axis=1)
            v = jnp.concatenate([v, vt], axis=1)
            st = lax.dot_general(qq, k, NT, preferred_element_type=f32)
            p = jnp.exp2(s_ref[b, 0:R] - top)
            pt = (p * st).astype(bf16)
            l = p[:, 0:HD]
            for j in range(1, KR // HD):
                l = l + p[:, j * HD : (j + 1) * HD]
            acc = jnp.dot(p.astype(bf16), v, preferred_element_type=f32)
            acct = jnp.dot(pt, v1, preferred_element_type=f32)
            if b == 0:
                l_ref[0:R], acc_ref[0:R], acct_ref[0:R] = l, acc, acct
            else:
                l_ref[0:R] += l
                acc_ref[0:R] += acc
                acct_ref[0:R] += acct
        total = jnp.sum(l_ref[0:R], axis=1, keepdims=True)
        inv = 1.0 / total
        inv_tan = inv * ln2
        drift = acct_ref[0:R, 128:256] * inv_tan
        o = acc_ref[0:R, 0:128] * inv
        t = acct_ref[0:R, 0:128] * inv_tan + acc_ref[0:R, 128:256] * inv - drift * o
        lse = jnp.broadcast_to(top + jnp.log2(total), (R, HD))
        where = lax.broadcasted_iota(i32, (R, HD), 1)
        pieces = jnp.zeros((R, HD), f32)
        for first, x in ((0, lse), (3, drift)):
            for i in range(3):
                piece = x.astype(bf16).astype(f32)
                pieces = jnp.where(where == first + i, piece, pieces)
                x = x - piece
        whole = [x.astype(bf16) for x in (o, t, pieces)]
        wanted = clip.astype(f32)
        for i, j in enumerate(listed):
            for core, (q_ref, out_ref) in enumerate(((qa_ref, oa_ref), (qb_ref, ob_ref))):
                at = (2 * i + core) * W
                tags = q_ref[j, TAG - ASK : MSG - ASK, :].astype(f32)
                tag = jnp.concatenate([tags[:, 0:1], tags[:, 1:2]], axis=0)
                hit = jnp.broadcast_to(tag, (W, HD)) == wanted
                for n, x in enumerate(whole):
                    old = out_ref[j, n * W : (n + 1) * W, :].astype(f32)
                    out_ref[j, n * W : (n + 1) * W, :] = jnp.where(hit, x[at : at + W].astype(f32), old).astype(bf16)


def attend(asked, asked_there, arrived):
    out = pltpu.VMEM((CHIPS, 3 * W, HD), bf16)
    return pl.pallas_call(
        attn_kernel,
        in_specs=[VMEM] * 3,
        out_specs=[VMEM] * 2,
        out_shape=[out] * 2,
        scratch_shapes=[
            pltpu.VMEM((LONG[1], RMAX, KR), f32),
            pltpu.VMEM((RMAX, 256), f32),
            pltpu.VMEM((RMAX, 256), f32),
            pltpu.VMEM((RMAX, HD), f32),
            pltpu.VMEM((6, ROWS, HD), bf16),
            pltpu.SMEM((2, CHIPS), i32),
            pltpu.SMEM((2, CHIPS), i32),
            pltpu.SMEM((2, CHIPS), i32),
            pltpu.SMEM((3,), i32),
        ],
        compiler_params=params(40),
        cost_estimate=pl.CostEstimate(flops=9 * 10**9, bytes_accessed=6 * 2**20, transcendentals=4 * 10**6),
    )(*[pltpu.with_memory_space_constraint(x, pltpu.VMEM) for x in (asked, asked_there, arrived)])


def combine_kernel(a_ref, b_ref, out_ref):
    R = CHIPS * W

    def read(ref):
        o, t, s = [ref[:, n * W : (n + 1) * W, :].astype(f32).reshape(R, HD) for n in range(3)]
        lse = s[:, 0:1] + s[:, 1:2] + s[:, 2:3]
        drift = s[:, 3:4] + s[:, 4:5] + s[:, 5:6]
        return o, t, lse, drift

    oa, ta, la, da = read(a_ref)
    ob, tb, lb, db = read(b_ref)
    top = jnp.maximum(la, lb)
    wa, wb = jnp.exp2(la - top), jnp.exp2(lb - top)
    inv = 1.0 / (wa + wb)
    wa, wb = wa * inv, wb * inv
    gap = wa * wb * (da - db)
    out_ref[:, 0:W, :] = (wa * oa + wb * ob).astype(bf16).reshape(CHIPS, W, HD)
    out_ref[:, W : 2 * W, :] = (wa * ta + wb * tb + gap * (oa - ob)).astype(bf16).reshape(CHIPS, W, HD)


def combine(a, b):
    return pl.pallas_call(
        combine_kernel,
        in_specs=[VMEM, VMEM],
        out_specs=VMEM,
        out_shape=pltpu.VMEM((CHIPS, 2 * W, HD), bf16),
        compiler_params=params(16),
    )(a, b)


CT = 512
STEPS = HALF // CT


def project_kernel(side_ref, x_ref, w_hbm, seg_ref, gate_ref, gate_tan_ref, *refs, own):
    if own:
        resid_ref, resid_tan_ref, send_ref, lhs_ref, held_ref, sem = refs
    else:
        send_ref, lhs_ref, held_ref, sem = refs
    start = side_ref[0] * HALF
    reads = []
    for j in range(STEPS):
        cols = pl.ds(pl.multiple_of(start + j * CT, CT), CT)
        reads.append(pltpu.make_async_copy(w_hbm.at[:, cols], held_ref.at[j], sem.at[j]))
        reads[j].start()
    for h in range(NH):
        for t in range(PARTS):
            s = worker(h, t)
            lhs_ref[t * W : (t + 1) * W, h * HD : (h + 1) * HD] = x_ref[s, 0:W, :]
            lhs_ref[ROWS + t * W : ROWS + (t + 1) * W, h * HD : (h + 1) * HD] = x_ref[s, W : 2 * W, :]
    one = seg_ref[:, 0:1] == 1.0
    for j in range(STEPS):
        reads[j].wait()
        out = jnp.dot(lhs_ref[...], held_ref[j], preferred_element_type=f32)
        cols = pl.ds(pl.multiple_of(start + j * CT, CT), CT)
        here = slice(j * CT, (j + 1) * CT)
        gate = jnp.where(one, gate_ref[1:2, cols], gate_ref[0:1, cols])
        gate_tan = jnp.where(one, gate_tan_ref[1:2, cols], gate_tan_ref[0:1, cols])
        a = gate * out[0:ROWS]
        b = gate_tan * out[0:ROWS] + gate * out[ROWS : 2 * ROWS]
        if own:
            a = a + resid_ref[:, here]
            b = b + resid_tan_ref[:, here]
        send_ref[0, :, here] = a.astype(bf16)
        send_ref[1, :, here] = b.astype(bf16)


def project(side, x, w, seg, gate, gate_tan, resid):
    own = len(resid) > 0
    return pl.pallas_call(
        lambda *refs: project_kernel(*refs, own=own),
        in_specs=[pl.BlockSpec(memory_space=pltpu.SMEM), VMEM, ANY] + [VMEM] * (3 + len(resid)),
        out_specs=VMEM,
        out_shape=pltpu.VMEM((2, ROWS, HALF), bf16),
        scratch_shapes=[
            pltpu.VMEM((2 * ROWS, NH * HD), bf16),
            pltpu.VMEM((STEPS, NH * HD, CT), bf16),
            pltpu.SemaphoreType.DMA((STEPS,)),
        ],
        compiler_params=params(48),
        cost_estimate=pl.CostEstimate(flops=2 * 2 * ROWS * NH * HD * HALF, bytes_accessed=10 * 2**20, transcendentals=0),
    )(side, x, in_hbm(w), seg, gate, gate_tan, *resid)


FT = 32


def norm_kernel(
    side_ref, mine_ref, got_mine_ref, other_ref, got_other_ref, seg_ref, scale_ref, scale_tan_ref, shift_ref, shift_tan_ref,
    resid_ref, resid_tan_ref, ffn_ref, ffn_tan_ref,
):
    a = [mine_ref[0].astype(f32) + got_mine_ref[0].astype(f32), other_ref[0].astype(f32) + got_other_ref[0].astype(f32)]
    b = [mine_ref[1].astype(f32) + got_mine_ref[1].astype(f32), other_ref[1].astype(f32) + got_other_ref[1].astype(f32)]
    resid_ref[...] = a[0]
    resid_tan_ref[...] = b[0]

    def average(x, y):
        return jnp.sum(x + y, axis=1, keepdims=True) / D

    mean, mean_tan = average(*a), average(*b)
    rstd = lax.rsqrt(average(a[0] * a[0], a[1] * a[1]) - mean * mean + norm_eps)
    cov = average(a[0] * b[0], a[1] * b[1]) - mean * mean_tan
    slope = rstd * rstd * rstd * cov
    one = seg_ref[:, 0:1] == 1.0
    for i, side in enumerate((side_ref[0], 1 - side_ref[0])):
        cols = pl.ds(pl.multiple_of(side * HALF, HALF), HALF)

        def pick(ref):
            return jnp.where(one, ref[1:2, cols], ref[0:1, cols])

        centered = a[i] - mean
        normed = centered * rstd
        normed_tan = (b[i] - mean_tan) * rstd - centered * slope
        scale = 1.0 + pick(scale_ref)
        ffn_ref[:, cols] = (normed * scale + pick(shift_ref)).astype(bf16)
        ffn_tan_ref[:, cols] = (normed_tan * scale + normed * pick(scale_tan_ref) + pick(shift_tan_ref)).astype(bf16)


def norm(side, mine, got_mine, other, got_other, seg, tables):
    pair = pl.BlockSpec((2, FT, HALF), lambda j: (0, j, 0))
    half = pl.BlockSpec((FT, HALF), lambda j: (j, 0))
    full = pl.BlockSpec((FT, D), lambda j: (j, 0))
    return pl.pallas_call(
        norm_kernel,
        grid=(ROWS // FT,),
        in_specs=[pl.BlockSpec(memory_space=pltpu.SMEM)] + [pair] * 4 + [pl.BlockSpec((FT, HD), lambda j: (j, 0))]
        + [pl.BlockSpec((2, D), lambda j: (0, 0))] * 4,
        out_specs=[half, half, full, full],
        out_shape=[jax.ShapeDtypeStruct((ROWS, HALF), f32)] * 2 + [jax.ShapeDtypeStruct((ROWS, D), bf16)] * 2,
        compiler_params=params(40),
    )(side, mine, got_mine, other, got_other, seg, *tables)


def body(
    queries, keys, values, queries_tan, keys_tan, values_tan, segments, positions, out_weight,
    residual, residual_tan, gate, gate_tan, mod_scale, mod_scale_tan, mod_shift, mod_shift_tan,
):
    frequency = np.float32(rope_base) ** (-np.arange(HD // 2, dtype=np.float32) / np.float32(HD // 2))
    freq = np.concatenate([frequency, frequency])[None, :].astype(np.float32)
    swap = [(0, 1), (1, 0)]

    with jax.named_scope("pack"):
        arrays = (queries, keys, values, queries_tan, keys_tan, values_tan)
        message, seg = pack(arrays, freq, positions[None, :], segments[None, :])
    with jax.named_scope("spread"):
        arrived = lax.all_to_all(message, ("z", "y", "x"), 0, 0, tiled=True)
        asked = lax.slice_in_dim(arrived, ASK, MSG, axis=1)
        asked_there = lax.ppermute(asked, "c", swap)

    side = lax.axis_index("head").astype(i32).reshape(1)
    with jax.named_scope("attend"):
        part, there = attend(asked, asked_there, arrived)
        back = lax.ppermute(there, "c", swap)
        answer = combine(part, back)
    with jax.named_scope("collect"):
        attended = lax.all_to_all(answer, ("z", "y", "x"), 0, 0, tiled=True)
    with jax.named_scope("project"):
        other = project(1 - side, attended, out_weight, seg, gate, gate_tan, ())
        got_mine = lax.ppermute(other, "head", swap)
        mine = project(side, attended, out_weight, seg, gate, gate_tan, (residual, residual_tan))
        got_other = lax.ppermute(mine, "head", swap)
    with jax.named_scope("norm"):
        return tuple(norm(side, mine, got_mine, other, got_other, seg, (mod_scale, mod_scale_tan, mod_shift, mod_shift_tan)))


def solution(mesh):
    fine = Mesh(mesh.devices.reshape(4, 4, 2, 2, 2), ("z", "y", "x", "c", "head"))
    seq = ("z", "y", "x", "c")
    split = P(seq, "head")
    in_specs = (split,) * 6 + (P(seq), P(seq), P("head", None), split, split) + (P(),) * 6
    out_specs = (split, split, P(seq, None), P(seq, None))
    return jax.shard_map(body, mesh=fine, in_specs=in_specs, out_specs=out_specs, check_vma=False)
```

```python
import math

import jax
import jax.numpy as jnp
import numpy as np
from jax import lax
from jax.experimental import pallas as pl
from jax.experimental.pallas import tpu as pltpu
from jax.sharding import Mesh, PartitionSpec as P

D = 5120
HD = 128
NH = 10
ROWS = 96
THIRD = 32
CHIPS = 32
PARTS = 3
SPAN = 5
K, KT, V, VT, QT, Q, TAG, MSG = 0, 96, 192, 288, 384, 416, 448, 464
ASK = QT
HALF = D // 2

W = THIRD
KR = 768
LONG, SHORT = (21, (8, 8, 5)), (13, (8, 5))
RMAX = LONG[0] * 2 * THIRD

neg_fill = -1e30
norm_eps = 1e-06
rope_base = 10000.0
ln2 = math.log(2.0)
exp_scale = math.log2(math.e) / math.sqrt(HD)

f32 = jnp.float32
bf16 = jnp.bfloat16
i32 = jnp.int32
VMEM = pl.BlockSpec(memory_space=pltpu.VMEM)
ANY = pl.BlockSpec(memory_space=pl.ANY)
NT = (((1,), (1,)), ((), ()))


def worker(h, t):
    return h // SPAN * (CHIPS // 2) + h % SPAN * PARTS + t


def params(mib=56):
    return pltpu.CompilerParams(vmem_limit_bytes=mib * 2**20)


def pack_kernel(side_ref, q_hbm, k_hbm, v_hbm, qt_hbm, kt_hbm, vt_hbm, freq_ref, pos_ref, seg_ref, out_ref, tag_ref, held_ref, sem_in):
    del side_ref
    reads = [pltpu.make_async_copy(x, held_ref.at[i], sem_in.at[i]) for i, x in enumerate((q_hbm, k_hbm, v_hbm, qt_hbm, kt_hbm, vt_hbm))]
    for copy in reads:
        copy.start()
    lane = lax.broadcasted_iota(i32, (ROWS, HD), 1)
    eye = lane == lax.broadcasted_iota(i32, (ROWS, HD), 0)
    pad = jnp.zeros((1, HD - ROWS), f32)
    clip_row = seg_ref[...].astype(f32)

    def column(row):
        return jnp.sum(jnp.where(eye, jnp.concatenate([row, pad], axis=1), 0.0), axis=1, keepdims=True)

    tag = column(clip_row)
    tag_ref[...] = jnp.broadcast_to(tag, (ROWS, HD))
    row = jnp.concatenate([pad, clip_row], axis=1)
    clips = []
    for t in range(PARTS):
        first, last = (tag[t * THIRD + i : t * THIRD + i + 16] for i in (0, 16))
        clips.append(jnp.where(lane[0:16] == 0, first, jnp.where(lane[0:16] == 1, last, row)).astype(bf16))
    angles = column(pos_ref[...].astype(f32)) * freq_ref[...]
    cos = jnp.cos(angles)
    sin = jnp.where(lane < HD // 2, -1.0, 1.0) * jnp.sin(angles)

    def rot(i, cols, factor):
        x = held_ref[i, :, cols].astype(f32)
        y = x * cos + jnp.roll(x, HD // 2, axis=1) * sin
        return (y if factor is None else y * factor).astype(bf16)

    for copy in reads:
        copy.wait()
    writes = []
    for h in range(NH):
        cols = slice(h * HD, (h + 1) * HD)
        q, k = rot(0, cols, exp_scale), rot(1, cols, None)
        qt, kt = rot(3, cols, exp_scale), rot(4, cols, None)
        v, vt = held_ref[2, :, cols], held_ref[5, :, cols]
        for t in range(PARTS):
            s = worker(h, t)
            at = t * THIRD
            out_ref[s, K:KT] = k
            out_ref[s, KT:V] = kt
            out_ref[s, V:VT] = v
            out_ref[s, VT:QT] = vt
            out_ref[s, QT:Q] = qt[at : at + THIRD]
            out_ref[s, Q:TAG] = q[at : at + THIRD]
            out_ref[s, TAG:MSG] = clips[t]
        if h % SPAN == SPAN - 1:
            out_ref[worker(h, 0) + PARTS] = jnp.zeros((MSG, HD), bf16)


def in_hbm(x):
    return pltpu.with_memory_space_constraint(x, pltpu.HBM)


def in_vmem(x):
    return pltpu.with_memory_space_constraint(x, pltpu.VMEM)


def pack(side, arrays, freq, positions, segments):
    return pl.pallas_call(
        pack_kernel,
        in_specs=[pl.BlockSpec(memory_space=pltpu.SMEM)] + [ANY] * 6 + [VMEM] * 3,
        out_specs=[VMEM, VMEM],
        out_shape=[pltpu.VMEM((CHIPS, MSG, HD), bf16), pltpu.VMEM((ROWS, HD), f32)],
        scratch_shapes=[
            pltpu.VMEM((6, ROWS, NH * HD), bf16),
            pltpu.SemaphoreType.DMA((6,)),
        ],
        compiler_params=params(40),
    )(side, *[in_hbm(x) for x in (*arrays, freq, positions, segments)])


def bits(tiles):
    rows = jnp.concatenate([t.astype(f32)[0:1, :] for t in tiles], axis=0)
    lane = lax.broadcasted_iota(i32, (CHIPS, HD), 1)
    at = lax.broadcasted_iota(i32, (CHIPS, 1), 0)
    power = jnp.left_shift(jnp.ones((CHIPS, 1), i32), at & 15).astype(f32)
    has0 = 1.0 - jnp.min(jnp.where(lane < 32, 1.0, rows), axis=1, keepdims=True)
    has1 = jnp.max(jnp.where(lane < 32, 0.0, rows), axis=1, keepdims=True)

    def scalar(has):
        low = jnp.sum(jnp.where(at < 16, has * power, 0.0)).astype(i32)
        high = jnp.sum(jnp.where(at < 16, 0.0, has * power)).astype(i32)
        return low | (high << 16)

    return scalar(has0), scalar(has1)


def attn_kernel(qa_ref, qb_ref, kv_ref, *refs):
    n = (len(refs) - 12) // 2
    wanted_later, (oa_ref, ob_ref), fetched = refs[:n], refs[n : n + 2], refs[n + 2 : 2 * n + 2]
    s_ref, acc_ref, acct_ref, l_ref, pen_ref, keys_ref, kind_ref, chips_ref, cut_ref, sem = refs[2 * n + 2 :]
    copies = []
    for src, dst in zip(wanted_later, fetched):
        cuts = FETCHES if src.shape[0] % (16 * FETCHES) == 0 else 1
        step = src.shape[0] // cuts
        for i in range(cuts):
            rows = slice(i * step, (i + 1) * step)
            copies.append(pltpu.make_async_copy(src.at[rows], dst.at[rows], sem.at[len(copies)]))
            copies[-1].start()
    own = bits([kv_ref[j, TAG:MSG, :] for j in range(CHIPS)])
    sib = bits([qb_ref[j, TAG - ASK : MSG - ASK, :] for j in range(CHIPS)])
    cut_ref[0] = i32(0)
    cut_ref[1] = i32(0)

    def sort(j, carry):
        cuts, counts = carry[0], list(carry[1:])
        has = [(own[c] >> j) & 1 for c in range(2)]
        both = has[0] & has[1]
        cut_ref[jnp.where(both == 1, jnp.minimum(cuts, 1), 2)] = j
        for c in range(2):
            at = jnp.where(has[c] == 1, counts[c], 31 - (j - counts[c]))
            keys_ref[c, at] = j
            kind_ref[c, at] = jnp.where(both == 1, 2 + 2 * c + jnp.minimum(cuts, 1), 1 - has[c])
            counts[c] = counts[c] + has[c]
            any_has = ((own[c] | sib[c]) >> j) & 1
            n = counts[2 + c]
            chips_ref[c, jnp.where(any_has == 1, n, 31 - (j - n))] = j
            counts[2 + c] = n + any_has
        return (cuts + both, *counts)

    zero = i32(0)
    counted = lax.fori_loop(0, CHIPS, sort, (zero,) * 5)
    long_clip = jnp.where(counted[4] > 16, 1, 0)

    lane = lax.broadcasted_iota(i32, (ROWS, HD), 1)
    eye = lane == lax.broadcasted_iota(i32, (ROWS, HD), 0) + 32
    pen_ref[0] = jnp.zeros((ROWS, HD), bf16)
    pen_ref[1] = jnp.where(lane == 0, neg_fill, 0.0).astype(bf16)
    for p in range(2):
        row = kv_ref[cut_ref[p], TAG:MSG, :].astype(f32)[0:1, :]
        col = jnp.sum(jnp.where(eye, row, 0.0), axis=1, keepdims=True)
        pen_ref[2 + p] = jnp.where(lane == 0, col * neg_fill, 0.0).astype(bf16)
        pen_ref[4 + p] = jnp.where(lane == 0, (1.0 - col) * neg_fill, 0.0).astype(bf16)

    for (chips, blocks), clip in ((LONG, long_clip), (SHORT, 1 - long_clip)):
        R = chips * 2 * THIRD
        listed = [chips_ref[clip, i] for i in range(chips)]
        qt, q = [jnp.concatenate([ref[j, at - ASK : at - ASK + THIRD, :] for j in listed for ref in (qa_ref, qb_ref)], axis=0) for at in (QT, Q)]
        qq = jnp.concatenate([qt, q], axis=1)
        one = jnp.where(lax.broadcasted_iota(i32, (R, HD), 1) == 0, 1.0, 0.0).astype(bf16)
        q = jnp.concatenate([q, one], axis=1)
        m = jnp.full((R, HD), neg_fill, f32)
        places = [(b, range(sum(blocks[:b]), sum(blocks[: b + 1])), -(-n * ROWS // 256) * 256) for b, n in enumerate(blocks)]
        for b, span, width in places:
            gap = width - len(span) * ROWS
            parts = [jnp.concatenate([kv_ref[keys_ref[clip, i], K:KT, :], pen_ref[kind_ref[clip, i]]], axis=1) for i in span]
            parts += [jnp.concatenate([jnp.zeros((gap, HD), bf16), pen_ref[1, 0:gap, :]], axis=1)] * (gap > 0)
            s = lax.dot_general(q, jnp.concatenate(parts, axis=0), NT, preferred_element_type=f32)
            s_ref[b, 0:R, 0:width] = s
            for j in range(width // HD):
                m = jnp.maximum(m, s[:, j * HD : (j + 1) * HD])
        top = jnp.max(m, axis=1, keepdims=True)
        for b, span, width in places:
            gap = width - len(span) * ROWS
            fill = [jnp.zeros((gap, HD), bf16)] * (gap > 0)
            js = [keys_ref[clip, i] for i in span]
            k, kt, v, vt = [jnp.concatenate([kv_ref[j, at : at + ROWS, :] for j in js] + fill, axis=0) for at in (K, KT, V, VT)]
            k = jnp.concatenate([k, kt], axis=1)
            v1 = jnp.concatenate([v, jnp.ones((width, HD), bf16)], axis=1)
            v = jnp.concatenate([v, vt], axis=1)
            st = lax.dot_general(qq, k, NT, preferred_element_type=f32)
            p = jnp.exp2(s_ref[b, 0:R, 0:width] - top)
            pt = (p * st).astype(bf16)
            l = p[:, 0:HD]
            for j in range(1, width // HD):
                l = l + p[:, j * HD : (j + 1) * HD]
            acc = jnp.dot(p.astype(bf16), v, preferred_element_type=f32)
            acct = jnp.dot(pt, v1, preferred_element_type=f32)
            if b == 0:
                l_ref[0:R], acc_ref[0:R], acct_ref[0:R] = l, acc, acct
            else:
                l_ref[0:R] += l
                acc_ref[0:R] += acc
                acct_ref[0:R] += acct
        total = jnp.sum(l_ref[0:R], axis=1, keepdims=True)
        inv = 1.0 / total
        inv_tan = inv * ln2
        drift = acct_ref[0:R, 128:256] * inv_tan
        o = acc_ref[0:R, 0:128] * inv
        t = acct_ref[0:R, 0:128] * inv_tan + acc_ref[0:R, 128:256] * inv - drift * o
        lse = jnp.broadcast_to(top + jnp.log2(total), (R, HD))
        where = lax.broadcasted_iota(i32, (R, HD), 1)
        pieces = jnp.zeros((R, HD), f32)
        for first, x in ((0, lse), (3, drift)):
            for i in range(3):
                piece = x.astype(bf16).astype(f32)
                pieces = jnp.where(where == first + i, piece, pieces)
                x = x - piece
        whole = [x.astype(bf16) for x in (o, t, pieces)]
        wanted = clip.astype(f32)
        for i, j in enumerate(listed):
            for core, (q_ref, out_ref) in enumerate(((qa_ref, oa_ref), (qb_ref, ob_ref))):
                at = (2 * i + core) * W
                tags = q_ref[j, TAG - ASK : MSG - ASK, :].astype(f32)
                tag = jnp.concatenate([tags[:, 0:1], tags[:, 1:2]], axis=0)
                hit = jnp.broadcast_to(tag, (W, HD)) == wanted
                for n, x in enumerate(whole):
                    old = out_ref[j, n * W : (n + 1) * W, :].astype(f32)
                    out_ref[j, n * W : (n + 1) * W, :] = jnp.where(hit, x[at : at + W].astype(f32), old).astype(bf16)
    for copy in copies:
        copy.wait()


FETCHES = 2


def attend(asked, asked_there, arrived, later):
    out = pltpu.VMEM((CHIPS, 3 * W, HD), bf16)
    outs = pl.pallas_call(
        attn_kernel,
        in_specs=[VMEM] * 3 + [ANY] * len(later),
        out_specs=[VMEM] * (2 + len(later)),
        out_shape=[out] * 2 + [pltpu.VMEM(x.shape, x.dtype) for x in later],
        scratch_shapes=[
            pltpu.VMEM((len(LONG[1]), RMAX, KR), f32),
            pltpu.VMEM((RMAX, 256), f32),
            pltpu.VMEM((RMAX, 256), f32),
            pltpu.VMEM((RMAX, HD), f32),
            pltpu.VMEM((6, ROWS, HD), bf16),
            pltpu.SMEM((2, CHIPS), i32),
            pltpu.SMEM((2, CHIPS), i32),
            pltpu.SMEM((2, CHIPS), i32),
            pltpu.SMEM((3,), i32),
            pltpu.SemaphoreType.DMA((FETCHES * len(later),)),
        ],
        compiler_params=params(36),
        cost_estimate=pl.CostEstimate(flops=9 * 10**9, bytes_accessed=6 * 2**20, transcendentals=4 * 10**6),
    )(*[in_vmem(x) for x in (asked, asked_there, arrived)], *[in_hbm(x) for x in later])
    return outs[0], outs[1], outs[2:]


def combine_kernel(a_ref, b_ref, out_ref):
    R = CHIPS * W

    row = lax.broadcasted_iota(i32, (HD, 2 * HD), 0)
    left = lax.broadcasted_iota(i32, (HD, 2 * HD), 1) < HD
    begin = jnp.where(left, 0, 3)
    select = jnp.where((row >= begin) & (row < begin + 3), 1.0, 0.0).astype(bf16)

    def read(ref):
        o, t = [ref[:, n * W : (n + 1) * W, :].astype(f32).reshape(R, HD) for n in range(2)]
        s = jnp.dot(ref[:, 2 * W : 3 * W, :].reshape(R, HD), select, preferred_element_type=f32)
        return o, t, s[:, 0:HD], s[:, HD : 2 * HD]

    oa, ta, la, da = read(a_ref)
    ob, tb, lb, db = read(b_ref)
    top = jnp.maximum(la, lb)
    wa, wb = jnp.exp2(la - top), jnp.exp2(lb - top)
    inv = 1.0 / (wa + wb)
    wa, wb = wa * inv, wb * inv
    gap = wa * wb * (da - db)
    out_ref[:, 0:W, :] = (wa * oa + wb * ob).astype(bf16).reshape(CHIPS, W, HD)
    out_ref[:, W : 2 * W, :] = (wa * ta + wb * tb + gap * (oa - ob)).astype(bf16).reshape(CHIPS, W, HD)


def combine(a, b):
    return pl.pallas_call(
        combine_kernel,
        in_specs=[VMEM, VMEM],
        out_specs=VMEM,
        out_shape=pltpu.VMEM((CHIPS, 2 * W, HD), bf16),
        compiler_params=params(16),
    )(a, b)


CT = 256
SENDS = 2
PIECE = HALF // SENDS
STEPS = PIECE // CT


def project_kernel(side_ref, x_ref, w_ref, seg_ref, gate_ref, gate_tan_ref, *refs, own, part):
    if own:
        resid_ref, resid_tan_ref, send_ref, lhs_ref = refs
    else:
        send_ref, lhs_ref = refs
    side = side_ref[0] if own else 1 - side_ref[0]
    start = side * HALF + part * PIECE
    for h in range(NH):
        for t in range(PARTS):
            s = worker(h, t)
            lhs_ref[t * W : (t + 1) * W, h * HD : (h + 1) * HD] = x_ref[s, 0:W, :]
            lhs_ref[ROWS + t * W : ROWS + (t + 1) * W, h * HD : (h + 1) * HD] = x_ref[s, W : 2 * W, :]
    one = seg_ref[:, 0:1] == 1.0
    for j in range(STEPS):
        cols = pl.ds(pl.multiple_of(start + j * CT, CT), CT)
        out = jnp.dot(lhs_ref[...], w_ref[:, cols], preferred_element_type=f32)
        here = slice(j * CT, (j + 1) * CT)
        gate = jnp.where(one, gate_ref[1:2, cols], gate_ref[0:1, cols])
        gate_tan = jnp.where(one, gate_tan_ref[1:2, cols], gate_tan_ref[0:1, cols])
        a = gate * out[0:ROWS]
        b = gate_tan * out[0:ROWS] + gate * out[ROWS : 2 * ROWS]
        if own:
            a = a + resid_ref[:, part * PIECE + j * CT : part * PIECE + (j + 1) * CT]
            b = b + resid_tan_ref[:, part * PIECE + j * CT : part * PIECE + (j + 1) * CT]
        send_ref[0, :, here] = a.astype(bf16)
        send_ref[1, :, here] = b.astype(bf16)


def project(side, x, w, seg, gate, gate_tan, resid, part):
    own = len(resid) > 0
    return pl.pallas_call(
        lambda *refs: project_kernel(*refs, own=own, part=part),
        in_specs=[pl.BlockSpec(memory_space=pltpu.SMEM)] + [VMEM] * (5 + len(resid)),
        out_specs=VMEM,
        out_shape=pltpu.VMEM((2, ROWS, PIECE), bf16),
        scratch_shapes=[
            pltpu.VMEM((2 * ROWS, NH * HD), bf16),
        ],
        compiler_params=params(16),
        cost_estimate=pl.CostEstimate(flops=2 * 2 * ROWS * NH * HD * HALF, bytes_accessed=10 * 2**20, transcendentals=0),
    )(side, *[in_vmem(x) for x in (x, w, seg, gate, gate_tan, *resid)])


FT = 32


def norm_kernel(side_ref, *refs):
    rows = [refs[i * SENDS : (i + 1) * SENDS] for i in range(4)]
    seg_ref, scale_ref, scale_tan_ref, shift_ref, shift_tan_ref = refs[4 * SENDS : 4 * SENDS + 5]
    outs, held, sem = refs[4 * SENDS + 5 : 4 * SENDS + 9], refs[4 * SENDS + 9 : 4 * SENDS + 13], refs[-1]
    resid_ref, resid_tan_ref, ffn_ref, ffn_tan_ref = held
    copies = []
    for step in range(ROWS // FT):
        at = slice(step * FT, (step + 1) * FT)

        def whole(kept, got, i):
            return jnp.concatenate([x[i, at].astype(f32) + y[i, at].astype(f32) for x, y in zip(kept, got)], axis=1)

        a = [whole(rows[0], rows[1], 0), whole(rows[2], rows[3], 0)]
        b = [whole(rows[0], rows[1], 1), whole(rows[2], rows[3], 1)]
        resid_ref[at] = a[0]
        resid_tan_ref[at] = b[0]

        def average(x, y):
            return jnp.sum(x + y, axis=1, keepdims=True) / D

        mean, mean_tan = average(*a), average(*b)
        rstd = lax.rsqrt(average(a[0] * a[0], a[1] * a[1]) - mean * mean + norm_eps)
        cov = average(a[0] * b[0], a[1] * b[1]) - mean * mean_tan
        slope = rstd * rstd * rstd * cov
        one = seg_ref[at, 0:1] == 1.0
        for i, side in enumerate((side_ref[0], 1 - side_ref[0])):
            cols = pl.ds(pl.multiple_of(side * HALF, HALF), HALF)

            def pick(ref):
                return jnp.where(one, ref[1:2, cols], ref[0:1, cols])

            centered = a[i] - mean
            normed = centered * rstd
            normed_tan = (b[i] - mean_tan) * rstd - centered * slope
            scale = 1.0 + pick(scale_ref)
            ffn_ref[at, cols] = (normed * scale + pick(shift_ref)).astype(bf16)
            ffn_tan_ref[at, cols] = (normed_tan * scale + normed * pick(scale_tan_ref) + pick(shift_tan_ref)).astype(bf16)
        for i in range(4):
            copies.append(pltpu.make_async_copy(held[i].at[at], outs[i].at[at], sem.at[step, i]))
            copies[-1].start()
    for copy in copies:
        copy.wait()


def norm(side, mine, got_mine, other, got_other, seg, tables):
    outs = [jax.ShapeDtypeStruct((ROWS, HALF), f32)] * 2 + [jax.ShapeDtypeStruct((ROWS, D), bf16)] * 2
    return pl.pallas_call(
        norm_kernel,
        in_specs=[pl.BlockSpec(memory_space=pltpu.SMEM)] + [VMEM] * (4 * SENDS + 5),
        out_specs=[ANY] * 4,
        out_shape=outs,
        scratch_shapes=[pltpu.VMEM(x.shape, x.dtype) for x in outs] + [pltpu.SemaphoreType.DMA((ROWS // FT, 4))],
        compiler_params=params(32),
    )(side, *[in_vmem(x) for x in (*mine, *got_mine, *other, *got_other, seg, *tables)])


def body(
    queries, keys, values, queries_tan, keys_tan, values_tan, segments, positions, out_weight,
    residual, residual_tan, gate, gate_tan, mod_scale, mod_scale_tan, mod_shift, mod_shift_tan,
):
    frequency = np.float32(rope_base) ** (-np.arange(HD // 2, dtype=np.float32) / np.float32(HD // 2))
    freq = np.concatenate([frequency, frequency])[None, :].astype(np.float32)
    swap = [(0, 1), (1, 0)]

    side = lax.axis_index("head").astype(i32).reshape(1)
    with jax.named_scope("pack"):
        arrays = (queries, keys, values, queries_tan, keys_tan, values_tan)
        message, seg = pack(side, arrays, freq, positions[None, :], segments[None, :])
    with jax.named_scope("spread"):
        arrived = lax.all_to_all(message, ("z", "y", "x"), 0, 0, tiled=True)
        asked = lax.slice_in_dim(arrived, ASK, MSG, axis=1)
        asked_there = lax.ppermute(asked, "c", swap)

    with jax.named_scope("attend"):
        later = (out_weight, gate, gate_tan, residual, residual_tan, mod_scale, mod_scale_tan, mod_shift, mod_shift_tan)
        part, there, later = attend(asked, asked_there, arrived, later)
        held_weight, held_gate, held_gate_tan, held_resid, held_resid_tan, *tables = later
        back = lax.ppermute(there, "c", swap)
        answer = combine(part, back)
    with jax.named_scope("collect"):
        attended = lax.all_to_all(answer, ("z", "y", "x"), 0, 0, tiled=True)
    with jax.named_scope("project"):
        args = (attended, held_weight, seg, held_gate, held_gate_tan)
        other, got_mine, mine, got_other = [], [], [], []
        for part in range(SENDS):
            other.append(project(side, *args, (), part))
            got_mine.append(lax.ppermute(other[part], "head", swap))
        for part in range(SENDS):
            mine.append(project(side, *args, (held_resid, held_resid_tan), part))
            got_other.append(lax.ppermute(mine[part], "head", swap))
    with jax.named_scope("norm"):
        return tuple(norm(side, mine, got_mine, other, got_other, seg, tables))


def solution(mesh):
    fine = Mesh(mesh.devices.reshape(4, 4, 2, 2, 2), ("z", "y", "x", "c", "head"))
    seq = ("z", "y", "x", "c")
    split = P(seq, "head")
    in_specs = (split,) * 6 + (P(seq), P(seq), P("head", None), split, split) + (P(),) * 6
    out_specs = (split, split, P(seq, None), P(seq, None))
    return jax.shard_map(body, mesh=fine, in_specs=in_specs, out_specs=out_specs, check_vma=False)
```

```python
import math

import jax
import jax.numpy as jnp
import numpy as np
from jax import lax
from jax.experimental import pallas as pl
from jax.experimental.pallas import tpu as pltpu
from jax.sharding import Mesh, PartitionSpec as P

D = 5120
HD = 128
NH = 10
ROWS = 96
THIRD = 32
CHIPS = 32
PARTS = 3
SPAN = 5
K, KT, V, VT, QT, Q, TAG, MSG = 0, 96, 192, 288, 384, 416, 448, 464
HALF = D // 2

W = THIRD
KR = 768
LONG, SHORT = (21, (8, 8, 5)), (13, (8, 5))
RLONG, RSHORT = LONG[0] * THIRD, SHORT[0] * THIRD
RALL = RLONG + RSHORT

neg_fill = -1e30
norm_eps = 1e-06
rope_base = 10000.0
ln2 = math.log(2.0)
exp_scale = math.log2(math.e) / math.sqrt(HD)

f32 = jnp.float32
bf16 = jnp.bfloat16
i32 = jnp.int32
VMEM = pl.BlockSpec(memory_space=pltpu.VMEM)
ANY = pl.BlockSpec(memory_space=pl.ANY)
NT = (((1,), (1,)), ((), ()))


def worker(h, t):
    return h // SPAN * (CHIPS // 2) + h % SPAN * PARTS + t


def params(mib=56):
    return pltpu.CompilerParams(vmem_limit_bytes=mib * 2**20)


def pack_kernel(side_ref, q_hbm, k_hbm, v_hbm, qt_hbm, kt_hbm, vt_hbm, freq_ref, pos_ref, seg_ref, out_ref, tag_ref, held_ref, sem_in):
    del side_ref
    reads = [pltpu.make_async_copy(x, held_ref.at[i], sem_in.at[i]) for i, x in enumerate((q_hbm, k_hbm, v_hbm, qt_hbm, kt_hbm, vt_hbm))]
    for copy in reads:
        copy.start()
    lane = lax.broadcasted_iota(i32, (ROWS, HD), 1)
    eye = lane == lax.broadcasted_iota(i32, (ROWS, HD), 0)
    pad = jnp.zeros((1, HD - ROWS), f32)
    clip_row = seg_ref[...].astype(f32)

    def column(row):
        return jnp.sum(jnp.where(eye, jnp.concatenate([row, pad], axis=1), 0.0), axis=1, keepdims=True)

    tag = column(clip_row)
    tag_ref[...] = jnp.broadcast_to(tag, (ROWS, HD))
    row = jnp.concatenate([pad, clip_row], axis=1)
    clips = []
    for t in range(PARTS):
        first, last = (tag[t * THIRD + i : t * THIRD + i + 16] for i in (0, 16))
        clips.append(jnp.where(lane[0:16] == 0, first, jnp.where(lane[0:16] == 1, last, row)).astype(bf16))
    angles = column(pos_ref[...].astype(f32)) * freq_ref[...]
    cos = jnp.cos(angles)
    sin = jnp.where(lane < HD // 2, -1.0, 1.0) * jnp.sin(angles)

    def rot(i, cols, factor):
        x = held_ref[i, :, cols].astype(f32)
        y = x * cos + jnp.roll(x, HD // 2, axis=1) * sin
        return (y if factor is None else y * factor).astype(bf16)

    for copy in reads:
        copy.wait()
    writes = []
    for h in range(NH):
        cols = slice(h * HD, (h + 1) * HD)
        q, k = rot(0, cols, exp_scale), rot(1, cols, None)
        qt, kt = rot(3, cols, exp_scale), rot(4, cols, None)
        v, vt = held_ref[2, :, cols], held_ref[5, :, cols]
        for t in range(PARTS):
            s = worker(h, t)
            at = t * THIRD
            out_ref[s, K:KT] = k
            out_ref[s, KT:V] = kt
            out_ref[s, V:VT] = v
            out_ref[s, VT:QT] = vt
            out_ref[s, QT:Q] = qt[at : at + THIRD]
            out_ref[s, Q:TAG] = q[at : at + THIRD]
            out_ref[s, TAG:MSG] = clips[t]
        if h % SPAN == SPAN - 1:
            out_ref[worker(h, 0) + PARTS] = jnp.zeros((MSG, HD), bf16)


def in_hbm(x):
    return pltpu.with_memory_space_constraint(x, pltpu.HBM)


def in_vmem(x):
    return pltpu.with_memory_space_constraint(x, pltpu.VMEM)


def pack(side, arrays, freq, positions, segments):
    return pl.pallas_call(
        pack_kernel,
        in_specs=[pl.BlockSpec(memory_space=pltpu.SMEM)] + [ANY] * 6 + [VMEM] * 3,
        out_specs=[VMEM, VMEM],
        out_shape=[pltpu.VMEM((CHIPS, MSG, HD), bf16), pltpu.VMEM((ROWS, HD), f32)],
        scratch_shapes=[
            pltpu.VMEM((6, ROWS, NH * HD), bf16),
            pltpu.SemaphoreType.DMA((6,)),
        ],
        compiler_params=params(40),
    )(side, *[in_hbm(x) for x in (*arrays, freq, positions, segments)])


def bits(tiles):
    rows = jnp.concatenate([t.astype(f32)[0:1, :] for t in tiles], axis=0)
    lane = lax.broadcasted_iota(i32, (CHIPS, HD), 1)
    at = lax.broadcasted_iota(i32, (CHIPS, 1), 0)
    power = jnp.left_shift(jnp.ones((CHIPS, 1), i32), at & 15).astype(f32)
    has0 = 1.0 - jnp.min(jnp.where(lane < 32, 1.0, rows), axis=1, keepdims=True)
    has1 = jnp.max(jnp.where(lane < 32, 0.0, rows), axis=1, keepdims=True)

    def scalar(has):
        low = jnp.sum(jnp.where(at < 16, has * power, 0.0)).astype(i32)
        high = jnp.sum(jnp.where(at < 16, 0.0, has * power)).astype(i32)
        return low | (high << 16)

    return scalar(has0), scalar(has1)


def attn_kernel(q_ref, kv_ref, *refs, second):
    s_ref, pen_ref, keys_ref, kind_ref, chips_ref, cut_ref = refs[-6:]
    copies = []
    if second:
        old_ref, old_stat_ref, out_ref, acc_ref, stat_ref = refs[:-6]
    else:
        n = (len(refs) - 9) // 2
        acc_ref, stat_ref = refs[n : n + 2]
        sem = refs[-7]
        for src, dst in zip(refs[:n], refs[n + 2 : 2 * n + 2]):
            cuts = FETCHES if src.shape[0] % (16 * FETCHES) == 0 else 1
            step = src.shape[0] // cuts
            for i in range(cuts):
                rows = slice(i * step, (i + 1) * step)
                copies.append(pltpu.make_async_copy(src.at[rows], dst.at[rows], sem.at[len(copies)]))
                copies[-1].start()
    asks = bits([q_ref[j, TAG:MSG, :] for j in range(CHIPS)])
    holds = bits([kv_ref[j, TAG:MSG, :] for j in range(CHIPS)]) if second else asks
    cut_ref[0] = i32(0)
    cut_ref[1] = i32(0)

    def sort(j, carry):
        cuts, counts = carry[0], list(carry[1:])
        has = [(holds[c] >> j) & 1 for c in range(2)]
        both = has[0] & has[1]
        cut_ref[jnp.where(both == 1, jnp.minimum(cuts, 1), 2)] = j
        for c in range(2):
            at = jnp.where(has[c] == 1, counts[c], 31 - (j - counts[c]))
            keys_ref[c, at] = j
            kind_ref[c, at] = jnp.where(both == 1, 2 + 2 * c + jnp.minimum(cuts, 1), 1 - has[c])
            counts[c] = counts[c] + has[c]
            ask = (asks[c] >> j) & 1
            n = counts[2 + c]
            chips_ref[c, jnp.where(ask == 1, n, 31 - (j - n))] = j
            counts[2 + c] = n + ask
        return (cuts + both, *counts)

    zero = i32(0)
    counted = lax.fori_loop(0, CHIPS, sort, (zero,) * 5)
    long_clip = jnp.where(counted[4] > 16, 1, 0)

    lane = lax.broadcasted_iota(i32, (ROWS, HD), 1)
    eye = lane == lax.broadcasted_iota(i32, (ROWS, HD), 0) + 32
    pen_ref[0] = jnp.zeros((ROWS, HD), bf16)
    pen_ref[1] = jnp.where(lane == 0, neg_fill, 0.0).astype(bf16)
    for p in range(2):
        row = kv_ref[cut_ref[p], TAG:MSG, :].astype(f32)[0:1, :]
        col = jnp.sum(jnp.where(eye, row, 0.0), axis=1, keepdims=True)
        pen_ref[2 + p] = jnp.where(lane == 0, col * neg_fill, 0.0).astype(bf16)
        pen_ref[4 + p] = jnp.where(lane == 0, (1.0 - col) * neg_fill, 0.0).astype(bf16)

    for (chips, blocks), clip, base in ((LONG, long_clip, 0), (SHORT, 1 - long_clip, RLONG)):
        R = chips * THIRD
        here = slice(base, base + R)
        listed = [chips_ref[clip, i] for i in range(chips)]
        qt, q = [jnp.concatenate([q_ref[j, at : at + THIRD, :] for j in listed], axis=0) for at in (QT, Q)]
        qq = jnp.concatenate([qt, q], axis=1)
        one = jnp.where(lax.broadcasted_iota(i32, (R, HD), 1) == 0, 1.0, 0.0).astype(bf16)
        q = jnp.concatenate([q, one], axis=1)
        m = old_stat_ref[here, 0:HD] if second else jnp.full((R, HD), neg_fill, f32)
        places = [(b, range(sum(blocks[:b]), sum(blocks[: b + 1])), -(-n * ROWS // 256) * 256) for b, n in enumerate(blocks)]
        for b, span, width in places:
            gap = width - len(span) * ROWS
            parts = [jnp.concatenate([kv_ref[keys_ref[clip, i], K:KT, :], pen_ref[kind_ref[clip, i]]], axis=1) for i in span]
            parts += [jnp.concatenate([jnp.zeros((gap, HD), bf16), pen_ref[1, 0:gap, :]], axis=1)] * (gap > 0)
            s = lax.dot_general(q, jnp.concatenate(parts, axis=0), NT, preferred_element_type=f32)
            s_ref[b, 0:R, 0:width] = s
            for j in range(width // HD):
                m = jnp.maximum(m, s[:, j * HD : (j + 1) * HD])
        top = jnp.max(m, axis=1, keepdims=True)
        m_old = old_stat_ref[here, 0:1] if second else None
        for b, span, width in places:
            gap = width - len(span) * ROWS
            fill = [jnp.zeros((gap, HD), bf16)] * (gap > 0)
            js = [keys_ref[clip, i] for i in span]
            k, kt, v, vt = [jnp.concatenate([kv_ref[j, at : at + ROWS, :] for j in js] + fill, axis=0) for at in (K, KT, V, VT)]
            k = jnp.concatenate([k, kt], axis=1)
            v1 = jnp.concatenate([v, jnp.ones((width, HD), bf16)], axis=1)
            v = jnp.concatenate([v, vt], axis=1)
            st = lax.dot_general(qq, k, NT, preferred_element_type=f32)
            p = jnp.exp2(s_ref[b, 0:R, 0:width] - top)
            pt = (p * st).astype(bf16)
            l = p[:, 0:HD]
            for j in range(1, width // HD):
                l = l + p[:, j * HD : (j + 1) * HD]
            acc = jnp.dot(p.astype(bf16), v, preferred_element_type=f32)
            acct = jnp.dot(pt, v1, preferred_element_type=f32)
            if b > 0 or second:
                fade = jnp.exp2(m_old - top) if b == 0 else None
                l += stat_ref[here, HD:] if b > 0 else old_stat_ref[here, HD:] * fade
                acc += acc_ref[here, 0:256] if b > 0 else old_ref[here, 0:256] * fade
                acct += acc_ref[here, 256:512] if b > 0 else old_ref[here, 256:512] * fade
            stat_ref[here, HD:] = l
            acc_ref[here, 0:256] = acc
            acc_ref[here, 256:512] = acct
        if not second:
            stat_ref[here, 0:HD] = jnp.broadcast_to(top, (R, HD))
            continue
        total = jnp.sum(stat_ref[here, HD:], axis=1, keepdims=True)
        inv = 1.0 / total
        inv_tan = inv * ln2
        drift = acc_ref[here, 384:512] * inv_tan
        o = acc_ref[here, 0:128] * inv
        t = acc_ref[here, 256:384] * inv_tan + acc_ref[here, 128:256] * inv - drift * o
        wanted = clip.astype(f32)
        for i, j in enumerate(listed):
            at = i * W
            tags = q_ref[j, TAG:MSG, :].astype(f32)
            tag = jnp.concatenate([tags[:, 0:1], tags[:, 1:2]], axis=0)
            hit = jnp.broadcast_to(tag, (W, HD)) == wanted
            for n, x in enumerate((o, t)):
                old = out_ref[j, n * W : (n + 1) * W, :].astype(f32)
                out_ref[j, n * W : (n + 1) * W, :] = jnp.where(hit, x[at : at + W], old).astype(bf16)
    for copy in copies:
        copy.wait()


FETCHES = 2


def scratch():
    lists = [pltpu.SMEM((2, CHIPS), i32)] * 3 + [pltpu.SMEM((3,), i32)]
    return [pltpu.VMEM((len(LONG[1]), RLONG, KR), f32), pltpu.VMEM((6, ROWS, HD), bf16)] + lists


def attend(arrived, later):
    outs = pl.pallas_call(
        lambda *refs: attn_kernel(*refs, second=False),
        in_specs=[VMEM] * 2 + [ANY] * len(later),
        out_specs=[VMEM] * (2 + len(later)),
        out_shape=[pltpu.VMEM((RALL, 512), f32), pltpu.VMEM((RALL, 2 * HD), f32)] + [pltpu.VMEM(x.shape, x.dtype) for x in later],
        scratch_shapes=[pltpu.SemaphoreType.DMA((FETCHES * len(later),))] + scratch(),
        compiler_params=params(28),
        cost_estimate=pl.CostEstimate(flops=5 * 10**9, bytes_accessed=20 * 2**20, transcendentals=2 * 10**6),
    )(in_vmem(arrived), in_vmem(arrived), *[in_hbm(x) for x in later])
    return outs[:2], outs[2:]


def attend_more(arrived, swapped, state):
    return pl.pallas_call(
        lambda *refs: attn_kernel(*refs, second=True),
        in_specs=[VMEM] * 4,
        out_specs=VMEM,
        out_shape=pltpu.VMEM((CHIPS, 2 * W, HD), bf16),
        scratch_shapes=[pltpu.VMEM((RALL, 512), f32), pltpu.VMEM((RALL, 2 * HD), f32)] + scratch(),
        compiler_params=params(28),
        cost_estimate=pl.CostEstimate(flops=5 * 10**9, bytes_accessed=8 * 2**20, transcendentals=2 * 10**6),
    )(*[in_vmem(x) for x in (arrived, swapped, *state)])


CT = 256
SENDS = 2
PIECE = HALF // SENDS
STEPS = PIECE // CT


def project_kernel(side_ref, x_ref, w_ref, seg_ref, gate_ref, gate_tan_ref, *refs, own, part):
    if own:
        resid_ref, resid_tan_ref, send_ref, lhs_ref = refs
    else:
        send_ref, lhs_ref = refs
    side = side_ref[0] if own else 1 - side_ref[0]
    start = side * HALF + part * PIECE
    for h in range(NH):
        for t in range(PARTS):
            s = worker(h, t)
            lhs_ref[t * W : (t + 1) * W, h * HD : (h + 1) * HD] = x_ref[s, 0:W, :]
            lhs_ref[ROWS + t * W : ROWS + (t + 1) * W, h * HD : (h + 1) * HD] = x_ref[s, W : 2 * W, :]
    one = seg_ref[:, 0:1] == 1.0
    for j in range(STEPS):
        cols = pl.ds(pl.multiple_of(start + j * CT, CT), CT)
        out = jnp.dot(lhs_ref[...], w_ref[:, cols], preferred_element_type=f32)
        here = slice(j * CT, (j + 1) * CT)
        gate = jnp.where(one, gate_ref[1:2, cols], gate_ref[0:1, cols])
        gate_tan = jnp.where(one, gate_tan_ref[1:2, cols], gate_tan_ref[0:1, cols])
        a = gate * out[0:ROWS]
        b = gate_tan * out[0:ROWS] + gate * out[ROWS : 2 * ROWS]
        if own:
            a = a + resid_ref[:, part * PIECE + j * CT : part * PIECE + (j + 1) * CT]
            b = b + resid_tan_ref[:, part * PIECE + j * CT : part * PIECE + (j + 1) * CT]
        send_ref[0, :, here] = a.astype(bf16)
        send_ref[1, :, here] = b.astype(bf16)


def project(side, x, w, seg, gate, gate_tan, resid, part):
    own = len(resid) > 0
    return pl.pallas_call(
        lambda *refs: project_kernel(*refs, own=own, part=part),
        in_specs=[pl.BlockSpec(memory_space=pltpu.SMEM)] + [VMEM] * (5 + len(resid)),
        out_specs=VMEM,
        out_shape=pltpu.VMEM((2, ROWS, PIECE), bf16),
        scratch_shapes=[
            pltpu.VMEM((2 * ROWS, NH * HD), bf16),
        ],
        compiler_params=params(16),
        cost_estimate=pl.CostEstimate(flops=2 * 2 * ROWS * NH * HD * HALF, bytes_accessed=10 * 2**20, transcendentals=0),
    )(side, *[in_vmem(x) for x in (x, w, seg, gate, gate_tan, *resid)])


FT = 32


def norm_kernel(side_ref, *refs):
    rows = [refs[i * SENDS : (i + 1) * SENDS] for i in range(4)]
    seg_ref, scale_ref, scale_tan_ref, shift_ref, shift_tan_ref = refs[4 * SENDS : 4 * SENDS + 5]
    outs, held, sem = refs[4 * SENDS + 5 : 4 * SENDS + 9], refs[4 * SENDS + 9 : 4 * SENDS + 13], refs[-1]
    resid_ref, resid_tan_ref, ffn_ref, ffn_tan_ref = held
    copies = []
    for step in range(ROWS // FT):
        at = slice(step * FT, (step + 1) * FT)

        def whole(kept, got, i):
            return jnp.concatenate([x[i, at].astype(f32) + y[i, at].astype(f32) for x, y in zip(kept, got)], axis=1)

        a = [whole(rows[0], rows[1], 0), whole(rows[2], rows[3], 0)]
        b = [whole(rows[0], rows[1], 1), whole(rows[2], rows[3], 1)]
        resid_ref[at] = a[0]
        resid_tan_ref[at] = b[0]

        def average(x, y):
            return jnp.sum(x + y, axis=1, keepdims=True) / D

        mean, mean_tan = average(*a), average(*b)
        rstd = lax.rsqrt(average(a[0] * a[0], a[1] * a[1]) - mean * mean + norm_eps)
        cov = average(a[0] * b[0], a[1] * b[1]) - mean * mean_tan
        slope = rstd * rstd * rstd * cov
        one = seg_ref[at, 0:1] == 1.0
        for i, side in enumerate((side_ref[0], 1 - side_ref[0])):
            cols = pl.ds(pl.multiple_of(side * HALF, HALF), HALF)

            def pick(ref):
                return jnp.where(one, ref[1:2, cols], ref[0:1, cols])

            centered = a[i] - mean
            normed = centered * rstd
            normed_tan = (b[i] - mean_tan) * rstd - centered * slope
            scale = 1.0 + pick(scale_ref)
            ffn_ref[at, cols] = (normed * scale + pick(shift_ref)).astype(bf16)
            ffn_tan_ref[at, cols] = (normed_tan * scale + normed * pick(scale_tan_ref) + pick(shift_tan_ref)).astype(bf16)
        for i in range(4):
            copies.append(pltpu.make_async_copy(held[i].at[at], outs[i].at[at], sem.at[step, i]))
            copies[-1].start()
    for copy in copies:
        copy.wait()


def norm(side, mine, got_mine, other, got_other, seg, tables):
    outs = [jax.ShapeDtypeStruct((ROWS, HALF), f32)] * 2 + [jax.ShapeDtypeStruct((ROWS, D), bf16)] * 2
    return pl.pallas_call(
        norm_kernel,
        in_specs=[pl.BlockSpec(memory_space=pltpu.SMEM)] + [VMEM] * (4 * SENDS + 5),
        out_specs=[ANY] * 4,
        out_shape=outs,
        scratch_shapes=[pltpu.VMEM(x.shape, x.dtype) for x in outs] + [pltpu.SemaphoreType.DMA((ROWS // FT, 4))],
        compiler_params=params(32),
    )(side, *[in_vmem(x) for x in (*mine, *got_mine, *other, *got_other, seg, *tables)])


def body(
    queries, keys, values, queries_tan, keys_tan, values_tan, segments, positions, out_weight,
    residual, residual_tan, gate, gate_tan, mod_scale, mod_scale_tan, mod_shift, mod_shift_tan,
):
    frequency = np.float32(rope_base) ** (-np.arange(HD // 2, dtype=np.float32) / np.float32(HD // 2))
    freq = np.concatenate([frequency, frequency])[None, :].astype(np.float32)
    swap = [(0, 1), (1, 0)]

    side = lax.axis_index("head").astype(i32).reshape(1)
    with jax.named_scope("pack"):
        arrays = (queries, keys, values, queries_tan, keys_tan, values_tan)
        message, seg = pack(side, arrays, freq, positions[None, :], segments[None, :])
    with jax.named_scope("spread"):
        arrived = lax.all_to_all(message, ("z", "y", "x"), 0, 0, tiled=True)
        swapped = lax.ppermute(arrived, "c", swap)
    with jax.named_scope("attend"):
        later = (out_weight, gate, gate_tan, residual, residual_tan, mod_scale, mod_scale_tan, mod_shift, mod_shift_tan)
        state, later = attend(arrived, later)
        held_weight, held_gate, held_gate_tan, held_resid, held_resid_tan, *tables = later
        answer = attend_more(arrived, swapped, state)
    with jax.named_scope("collect"):
        attended = lax.all_to_all(answer, ("z", "y", "x"), 0, 0, tiled=True)
    with jax.named_scope("project"):
        args = (attended, held_weight, seg, held_gate, held_gate_tan)
        other, got_mine, mine, got_other = [], [], [], []
        for part in range(SENDS):
            other.append(project(side, *args, (), part))
            got_mine.append(lax.ppermute(other[part], "head", swap))
        for part in range(SENDS):
            mine.append(project(side, *args, (held_resid, held_resid_tan), part))
            got_other.append(lax.ppermute(mine[part], "head", swap))
    with jax.named_scope("norm"):
        return tuple(norm(side, mine, got_mine, other, got_other, seg, tables))


def solution(mesh):
    fine = Mesh(mesh.devices.reshape(4, 4, 2, 2, 2), ("z", "y", "x", "c", "head"))
    seq = ("z", "y", "x", "c")
    split = P(seq, "head")
    in_specs = (split,) * 6 + (P(seq), P(seq), P("head", None), split, split) + (P(),) * 6
    out_specs = (split, split, P(seq, None), P(seq, None))
    return jax.shard_map(body, mesh=fine, in_specs=in_specs, out_specs=out_specs, check_vma=False)
```

```python
import math

import jax
import jax.numpy as jnp
import numpy as np
from jax import lax
from jax.experimental import pallas as pl
from jax.experimental.pallas import tpu as pltpu
from jax.sharding import Mesh, PartitionSpec as P

D = 5120
HD = 128
NH = 10
ROWS = 96
THIRD = 32
CHIPS = 32
PARTS = 3
SPAN = 5
K, KT, V, VT, QT, Q, TAG, MSG = 0, 96, 192, 288, 384, 416, 448, 464
HALF = D // 2

W = THIRD
KR = 768
LONG, SHORT = (21, (8, 8, 5)), (13, (8, 5))
RLONG, RSHORT = LONG[0] * THIRD, SHORT[0] * THIRD
RALL = RLONG + RSHORT

neg_fill = -1e30
norm_eps = 1e-06
rope_base = 10000.0
ln2 = math.log(2.0)
exp_scale = math.log2(math.e) / math.sqrt(HD)

f32 = jnp.float32
bf16 = jnp.bfloat16
i32 = jnp.int32
VMEM = pl.BlockSpec(memory_space=pltpu.VMEM)
ANY = pl.BlockSpec(memory_space=pl.ANY)
NT = (((1,), (1,)), ((), ()))


def worker(h, t):
    return h // SPAN * (CHIPS // 2) + h % SPAN * PARTS + t


def params(mib=56):
    return pltpu.CompilerParams(vmem_limit_bytes=mib * 2**20)


def pack_kernel(side_ref, q_hbm, k_hbm, v_hbm, qt_hbm, kt_hbm, vt_hbm, freq_ref, pos_ref, seg_ref, out_ref, tag_ref, held_ref, sem_in):
    del side_ref
    reads = [pltpu.make_async_copy(x, held_ref.at[i], sem_in.at[i]) for i, x in enumerate((q_hbm, k_hbm, v_hbm, qt_hbm, kt_hbm, vt_hbm))]
    for copy in reads:
        copy.start()
    lane = lax.broadcasted_iota(i32, (ROWS, HD), 1)
    eye = lane == lax.broadcasted_iota(i32, (ROWS, HD), 0)
    pad = jnp.zeros((1, HD - ROWS), f32)
    clip_row = seg_ref[...].astype(f32)

    def column(row):
        return jnp.sum(jnp.where(eye, jnp.concatenate([row, pad], axis=1), 0.0), axis=1, keepdims=True)

    tag = column(clip_row)
    tag_ref[...] = jnp.broadcast_to(tag, (ROWS, HD))
    row = jnp.concatenate([pad, clip_row], axis=1)
    clips = []
    for t in range(PARTS):
        first, last = (tag[t * THIRD + i : t * THIRD + i + 16] for i in (0, 16))
        clips.append(jnp.where(lane[0:16] == 0, first, jnp.where(lane[0:16] == 1, last, row)).astype(bf16))
    angles = column(pos_ref[...].astype(f32)) * freq_ref[...]
    cos = jnp.cos(angles)
    sin = jnp.where(lane < HD // 2, -1.0, 1.0) * jnp.sin(angles)

    def rot(i, cols, factor):
        x = held_ref[i, :, cols].astype(f32)
        y = x * cos + jnp.roll(x, HD // 2, axis=1) * sin
        return (y if factor is None else y * factor).astype(bf16)

    for copy in reads:
        copy.wait()
    writes = []
    for h in range(NH):
        cols = slice(h * HD, (h + 1) * HD)
        q, k = rot(0, cols, exp_scale), rot(1, cols, None)
        qt, kt = rot(3, cols, exp_scale), rot(4, cols, None)
        v, vt = held_ref[2, :, cols], held_ref[5, :, cols]
        for t in range(PARTS):
            s = worker(h, t)
            at = t * THIRD
            out_ref[s, K:KT] = k
            out_ref[s, KT:V] = kt
            out_ref[s, V:VT] = v
            out_ref[s, VT:QT] = vt
            out_ref[s, QT:Q] = qt[at : at + THIRD]
            out_ref[s, Q:TAG] = q[at : at + THIRD]
            out_ref[s, TAG:MSG] = clips[t]
        if h % SPAN == SPAN - 1:
            out_ref[worker(h, 0) + PARTS] = jnp.zeros((MSG, HD), bf16)


def in_hbm(x):
    return pltpu.with_memory_space_constraint(x, pltpu.HBM)


def in_vmem(x):
    return pltpu.with_memory_space_constraint(x, pltpu.VMEM)


def pack(side, arrays, freq, positions, segments):
    return pl.pallas_call(
        pack_kernel,
        in_specs=[pl.BlockSpec(memory_space=pltpu.SMEM)] + [ANY] * 6 + [VMEM] * 3,
        out_specs=[VMEM, VMEM],
        out_shape=[pltpu.VMEM((CHIPS, MSG, HD), bf16), pltpu.VMEM((ROWS, HD), f32)],
        scratch_shapes=[
            pltpu.VMEM((6, ROWS, NH * HD), bf16),
            pltpu.SemaphoreType.DMA((6,)),
        ],
        compiler_params=params(40),
    )(side, *[in_hbm(x) for x in (*arrays, freq, positions, segments)])


def bits(tiles):
    rows = jnp.concatenate([t.astype(f32)[0:1, :] for t in tiles], axis=0)
    lane = lax.broadcasted_iota(i32, (CHIPS, HD), 1)
    at = lax.broadcasted_iota(i32, (CHIPS, 1), 0)
    power = jnp.left_shift(jnp.ones((CHIPS, 1), i32), at & 15).astype(f32)
    has0 = 1.0 - jnp.min(jnp.where(lane < 32, 1.0, rows), axis=1, keepdims=True)
    has1 = jnp.max(jnp.where(lane < 32, 0.0, rows), axis=1, keepdims=True)

    def scalar(has):
        low = jnp.sum(jnp.where(at < 16, has * power, 0.0)).astype(i32)
        high = jnp.sum(jnp.where(at < 16, 0.0, has * power)).astype(i32)
        return low | (high << 16)

    return scalar(has0), scalar(has1)


def attn_kernel(q_ref, kv_ref, *refs, second):
    s_ref, pen_ref, keys_ref, kind_ref, chips_ref, cut_ref = refs[-6:]
    copies = []
    if second:
        old_ref, old_stat_ref, out_ref, acc_ref, stat_ref = refs[:-6]
    else:
        n = (len(refs) - 9) // 2
        acc_ref, stat_ref = refs[n : n + 2]
        sem = refs[-7]
        for src, dst in zip(refs[:n], refs[n + 2 : 2 * n + 2]):
            cuts = FETCHES if src.shape[0] % (16 * FETCHES) == 0 else 1
            step = src.shape[0] // cuts
            for i in range(cuts):
                rows = slice(i * step, (i + 1) * step)
                copies.append(pltpu.make_async_copy(src.at[rows], dst.at[rows], sem.at[len(copies)]))
                copies[-1].start()
    asks = bits([q_ref[j, TAG:MSG, :] for j in range(CHIPS)])
    holds = bits([kv_ref[j, TAG:MSG, :] for j in range(CHIPS)]) if second else asks
    cut_ref[0] = i32(0)
    cut_ref[1] = i32(0)

    def sort(j, carry):
        cuts, counts = carry[0], list(carry[1:])
        has = [(holds[c] >> j) & 1 for c in range(2)]
        both = has[0] & has[1]
        cut_ref[jnp.where(both == 1, jnp.minimum(cuts, 1), 2)] = j
        for c in range(2):
            at = jnp.where(has[c] == 1, counts[c], 31 - (j - counts[c]))
            keys_ref[c, at] = j
            kind_ref[c, at] = jnp.where(both == 1, 2 + 2 * c + jnp.minimum(cuts, 1), 1 - has[c])
            counts[c] = counts[c] + has[c]
            ask = (asks[c] >> j) & 1
            n = counts[2 + c]
            chips_ref[c, jnp.where(ask == 1, n, 31 - (j - n))] = j
            counts[2 + c] = n + ask
        return (cuts + both, *counts)

    zero = i32(0)
    counted = lax.fori_loop(0, CHIPS, sort, (zero,) * 5)
    long_clip = jnp.where(counted[4] > 16, 1, 0)

    lane = lax.broadcasted_iota(i32, (ROWS, HD), 1)
    eye = lane == lax.broadcasted_iota(i32, (ROWS, HD), 0) + 32
    pen_ref[0] = jnp.zeros((ROWS, HD), bf16)
    pen_ref[1] = jnp.where(lane == 0, neg_fill, 0.0).astype(bf16)
    for p in range(2):
        row = kv_ref[cut_ref[p], TAG:MSG, :].astype(f32)[0:1, :]
        col = jnp.sum(jnp.where(eye, row, 0.0), axis=1, keepdims=True)
        pen_ref[2 + p] = jnp.where(lane == 0, col * neg_fill, 0.0).astype(bf16)
        pen_ref[4 + p] = jnp.where(lane == 0, (1.0 - col) * neg_fill, 0.0).astype(bf16)

    for (chips, blocks), clip, base in ((LONG, long_clip, 0), (SHORT, 1 - long_clip, RLONG)):
        R = chips * THIRD
        here = slice(base, base + R)
        listed = [chips_ref[clip, i] for i in range(chips)]
        qt, q = [jnp.concatenate([q_ref[j, at : at + THIRD, :] for j in listed], axis=0) for at in (QT, Q)]
        qq = jnp.concatenate([qt, q], axis=1)
        one = jnp.where(lax.broadcasted_iota(i32, (R, HD), 1) == 0, 1.0, 0.0).astype(bf16)
        q = jnp.concatenate([q, one], axis=1)
        m = old_stat_ref[here, 0:HD] if second else jnp.full((R, HD), neg_fill, f32)
        places = [(b, range(sum(blocks[:b]), sum(blocks[: b + 1])), -(-n * ROWS // 256) * 256) for b, n in enumerate(blocks)]
        for b, span, width in places:
            gap = width - len(span) * ROWS
            parts = [jnp.concatenate([kv_ref[keys_ref[clip, i], K:KT, :], pen_ref[kind_ref[clip, i]]], axis=1) for i in span]
            parts += [jnp.concatenate([jnp.zeros((gap, HD), bf16), pen_ref[1, 0:gap, :]], axis=1)] * (gap > 0)
            s = lax.dot_general(q, jnp.concatenate(parts, axis=0), NT, preferred_element_type=f32)
            s_ref[b, 0:R, 0:width] = s
            for j in range(width // HD):
                m = jnp.maximum(m, s[:, j * HD : (j + 1) * HD])
        top = jnp.max(m, axis=1, keepdims=True)
        m_old = old_stat_ref[here, 0:1] if second else None
        for b, span, width in places:
            gap = width - len(span) * ROWS
            fill = [jnp.zeros((gap, HD), bf16)] * (gap > 0)
            js = [keys_ref[clip, i] for i in span]
            k, kt, v, vt = [jnp.concatenate([kv_ref[j, at : at + ROWS, :] for j in js] + fill, axis=0) for at in (K, KT, V, VT)]
            k = jnp.concatenate([k, kt], axis=1)
            v1 = jnp.concatenate([v, jnp.ones((width, HD), bf16)], axis=1)
            v = jnp.concatenate([v, vt], axis=1)
            st = lax.dot_general(qq, k, NT, preferred_element_type=f32)
            p = jnp.exp2(s_ref[b, 0:R, 0:width] - top)
            pt = (p * st).astype(bf16)
            l = p[:, 0:HD]
            for j in range(1, width // HD):
                l = l + p[:, j * HD : (j + 1) * HD]
            acc = jnp.dot(p.astype(bf16), v, preferred_element_type=f32)
            acct = jnp.dot(pt, v1, preferred_element_type=f32)
            if b > 0 or second:
                fade = jnp.exp2(m_old - top) if b == 0 else None
                l += stat_ref[here, HD:] if b > 0 else old_stat_ref[here, HD:] * fade
                acc += acc_ref[here, 0:256] if b > 0 else old_ref[here, 0:256] * fade
                acct += acc_ref[here, 256:512] if b > 0 else old_ref[here, 256:512] * fade
            stat_ref[here, HD:] = l
            acc_ref[here, 0:256] = acc
            acc_ref[here, 256:512] = acct
        if not second:
            stat_ref[here, 0:HD] = jnp.broadcast_to(top, (R, HD))
            continue
        total = jnp.sum(stat_ref[here, HD:], axis=1, keepdims=True)
        inv = 1.0 / total
        inv_tan = inv * ln2
        drift = acc_ref[here, 384:512] * inv_tan
        o = acc_ref[here, 0:128] * inv
        t = acc_ref[here, 256:384] * inv_tan + acc_ref[here, 128:256] * inv - drift * o
        wanted = clip.astype(f32)
        for i, j in enumerate(listed):
            at = i * W
            tags = q_ref[j, TAG:MSG, :].astype(f32)
            tag = jnp.concatenate([tags[:, 0:1], tags[:, 1:2]], axis=0)
            hit = jnp.broadcast_to(tag, (W, HD)) == wanted
            for n, x in enumerate((o, t)):
                lanes = slice(n * HD, (n + 1) * HD)
                old = out_ref[j, :, lanes].astype(f32)
                out_ref[j, :, lanes] = jnp.where(hit, x[at : at + W], old).astype(bf16)
    for copy in copies:
        copy.wait()


FETCHES = 2


def scratch():
    lists = [pltpu.SMEM((2, CHIPS), i32)] * 3 + [pltpu.SMEM((3,), i32)]
    return [pltpu.VMEM((len(LONG[1]), RLONG, KR), f32), pltpu.VMEM((6, ROWS, HD), bf16)] + lists


def attend(arrived, later):
    outs = pl.pallas_call(
        lambda *refs: attn_kernel(*refs, second=False),
        in_specs=[VMEM] * 2 + [ANY] * len(later),
        out_specs=[VMEM] * (2 + len(later)),
        out_shape=[pltpu.VMEM((RALL, 512), f32), pltpu.VMEM((RALL, 2 * HD), f32)] + [pltpu.VMEM(x.shape, x.dtype) for x in later],
        scratch_shapes=[pltpu.SemaphoreType.DMA((FETCHES * len(later),))] + scratch(),
        compiler_params=params(28),
        cost_estimate=pl.CostEstimate(flops=5 * 10**9, bytes_accessed=20 * 2**20, transcendentals=2 * 10**6),
    )(in_vmem(arrived), in_vmem(arrived), *[in_hbm(x) for x in later])
    return outs[:2], outs[2:]


def attend_more(arrived, swapped, state):
    return pl.pallas_call(
        lambda *refs: attn_kernel(*refs, second=True),
        in_specs=[VMEM] * 4,
        out_specs=VMEM,
        out_shape=pltpu.VMEM((CHIPS, W, 2 * HD), bf16),
        scratch_shapes=[pltpu.VMEM((RALL, 512), f32), pltpu.VMEM((RALL, 2 * HD), f32)] + scratch(),
        compiler_params=params(28),
        cost_estimate=pl.CostEstimate(flops=5 * 10**9, bytes_accessed=8 * 2**20, transcendentals=2 * 10**6),
    )(*[in_vmem(x) for x in (arrived, swapped, *state)])


CT = 256
SENDS = 2
PIECE = HALF // SENDS
STEPS = PIECE // CT


def project_kernel(side_ref, x_ref, w_ref, seg_ref, gate_ref, gate_tan_ref, *refs, own, part):
    if own:
        resid_ref, resid_tan_ref, send_ref, lhs_ref = refs
    else:
        send_ref, lhs_ref = refs
    side = side_ref[0] if own else 1 - side_ref[0]
    start = side * HALF + part * PIECE
    for h in range(NH):
        for t in range(PARTS):
            s = worker(h, t)
            lhs_ref[t * W : (t + 1) * W, h * HD : (h + 1) * HD] = x_ref[s, :, 0:HD]
            lhs_ref[ROWS + t * W : ROWS + (t + 1) * W, h * HD : (h + 1) * HD] = x_ref[s, :, HD : 2 * HD]
    one = seg_ref[:, 0:1] == 1.0
    for j in range(STEPS):
        cols = pl.ds(pl.multiple_of(start + j * CT, CT), CT)
        out = jnp.dot(lhs_ref[...], w_ref[:, cols], preferred_element_type=f32)
        here = slice(j * CT, (j + 1) * CT)
        gate = jnp.where(one, gate_ref[1:2, cols], gate_ref[0:1, cols])
        gate_tan = jnp.where(one, gate_tan_ref[1:2, cols], gate_tan_ref[0:1, cols])
        a = gate * out[0:ROWS]
        b = gate_tan * out[0:ROWS] + gate * out[ROWS : 2 * ROWS]
        if own:
            a = a + resid_ref[:, part * PIECE + j * CT : part * PIECE + (j + 1) * CT]
            b = b + resid_tan_ref[:, part * PIECE + j * CT : part * PIECE + (j + 1) * CT]
        send_ref[0, :, here] = a.astype(bf16)
        send_ref[1, :, here] = b.astype(bf16)


def project(side, x, w, seg, gate, gate_tan, resid, part):
    own = len(resid) > 0
    return pl.pallas_call(
        lambda *refs: project_kernel(*refs, own=own, part=part),
        in_specs=[pl.BlockSpec(memory_space=pltpu.SMEM)] + [VMEM] * (5 + len(resid)),
        out_specs=VMEM,
        out_shape=pltpu.VMEM((2, ROWS, PIECE), bf16),
        scratch_shapes=[
            pltpu.VMEM((2 * ROWS, NH * HD), bf16),
        ],
        compiler_params=params(16),
        cost_estimate=pl.CostEstimate(flops=2 * 2 * ROWS * NH * HD * HALF, bytes_accessed=10 * 2**20, transcendentals=0),
    )(side, *[in_vmem(x) for x in (x, w, seg, gate, gate_tan, *resid)])


FT, FN = 16, 16


def moments(a, b):
    lane = lax.broadcasted_iota(i32, (a.shape[0], HD), 1)
    out = jnp.zeros((a.shape[0], HD), f32)
    for i, x in enumerate((a, a * a, b, a * b)):
        out = jnp.where(lane == i, jnp.sum(x, axis=1, keepdims=True), out)
    return out


def settle_kernel(*refs):
    kept, got, refs = refs[:SENDS], refs[SENDS : 2 * SENDS], refs[2 * SENDS :]
    seg_ref, tables, (pass_ref, a_ref, b_ref, sums_ref, rows_ref, resid_hbm, resid_tan_hbm, sem) = refs[0], refs[1:5], refs[5:]
    del pass_ref
    copies = []
    for step in range(ROWS // FT):
        at = slice(step * FT, (step + 1) * FT)
        a, b = (jnp.concatenate([x[i, at].astype(f32) + y[i, at].astype(f32) for x, y in zip(kept, got)], axis=1) for i in range(2))
        a_ref[at] = a
        b_ref[at] = b
        sums_ref[at] = moments(a, b)
        for i, (src, dst) in enumerate(((a_ref, resid_hbm), (b_ref, resid_tan_hbm))):
            copies.append(pltpu.make_async_copy(src.at[at], dst.at[at], sem.at[step, i]))
            copies[-1].start()
    one = seg_ref[:, 0:1] == 1.0
    for i, table in enumerate(tables):
        row = jnp.where(one, table[1:2, :], table[0:1, :])
        rows_ref[i] = row + 1.0 if i == 0 else row
    for copy in copies:
        copy.wait()


def settle(kept, got, seg, tables):
    half, out = pltpu.VMEM((ROWS, HALF), f32), jax.ShapeDtypeStruct((ROWS, HALF), f32)
    return pl.pallas_call(
        settle_kernel,
        in_specs=[VMEM] * (2 * SENDS + 5),
        out_specs=[VMEM] * 5 + [ANY] * 2,
        out_shape=[pltpu.VMEM((2, ROWS, PIECE), bf16), half, half, pltpu.VMEM((ROWS, HD), f32), pltpu.VMEM((4, ROWS, D), f32), out, out],
        input_output_aliases={SENDS - 1: 0},
        scratch_shapes=[pltpu.SemaphoreType.DMA((ROWS // FT, 2))],
        compiler_params=params(16),
    )(*[in_vmem(x) for x in (*kept, *got, seg, *tables)])


def norm_kernel(side_ref, *refs):
    rows = [refs[i * SENDS : (i + 1) * SENDS] for i in range(2)]
    a_ref, b_ref, sums_ref, rows_ref = refs[2 * SENDS : 2 * SENDS + 4]
    outs, held, sem = refs[2 * SENDS + 4 : 2 * SENDS + 6], refs[2 * SENDS + 6 : 2 * SENDS + 8], refs[-1]
    ffn_ref, ffn_tan_ref = held
    copies = []
    for step in range(ROWS // FN):
        at = slice(step * FN, (step + 1) * FN)
        a, b = (jnp.concatenate([x[i, at].astype(f32) + y[i, at].astype(f32) for x, y in zip(*rows)], axis=1) for i in range(2))
        total = (moments(a, b) + sums_ref[at]) / D
        mean, mean_tan = total[:, 0:1], total[:, 2:3]
        rstd = lax.rsqrt(total[:, 1:2] - mean * mean + norm_eps)
        cov = total[:, 3:4] - mean * mean_tan
        slope = rstd * rstd * rstd * cov
        for side, x, y in ((1 - side_ref[0], a, b), (side_ref[0], a_ref[at], b_ref[at])):
            cols = pl.ds(pl.multiple_of(side * HALF, HALF), HALF)
            centered = x - mean
            normed = centered * rstd
            normed_tan = (y - mean_tan) * rstd - centered * slope
            scale, scale_tan, shift, shift_tan = (rows_ref[i, at, cols] for i in range(4))
            ffn_ref[at, cols] = (normed * scale + shift).astype(bf16)
            ffn_tan_ref[at, cols] = (normed_tan * scale + normed * scale_tan + shift_tan).astype(bf16)
        for i in range(2):
            copies.append(pltpu.make_async_copy(held[i].at[at], outs[i].at[at], sem.at[step, i]))
            copies[-1].start()
    for copy in copies:
        copy.wait()


def norm(side, other, got_other, settled):
    outs = [jax.ShapeDtypeStruct((ROWS, D), bf16)] * 2
    return pl.pallas_call(
        norm_kernel,
        in_specs=[pl.BlockSpec(memory_space=pltpu.SMEM)] + [VMEM] * (2 * SENDS + 4),
        out_specs=[ANY] * 2,
        out_shape=outs,
        scratch_shapes=[pltpu.VMEM(x.shape, x.dtype) for x in outs] + [pltpu.SemaphoreType.DMA((ROWS // FN, 2))],
        compiler_params=params(32),
    )(side, *[in_vmem(x) for x in (*other, *got_other, *settled)])


def body(
    queries, keys, values, queries_tan, keys_tan, values_tan, segments, positions, out_weight,
    residual, residual_tan, gate, gate_tan, mod_scale, mod_scale_tan, mod_shift, mod_shift_tan,
):
    frequency = np.float32(rope_base) ** (-np.arange(HD // 2, dtype=np.float32) / np.float32(HD // 2))
    freq = np.concatenate([frequency, frequency])[None, :].astype(np.float32)
    swap = [(0, 1), (1, 0)]

    side = lax.axis_index("head").astype(i32).reshape(1)
    with jax.named_scope("pack"):
        arrays = (queries, keys, values, queries_tan, keys_tan, values_tan)
        message, seg = pack(side, arrays, freq, positions[None, :], segments[None, :])
    with jax.named_scope("spread"):
        arrived = lax.all_to_all(message, ("z", "y", "x"), 0, 0, tiled=True)
        swapped = lax.ppermute(arrived, "c", swap)
    with jax.named_scope("attend"):
        later = (out_weight, gate, gate_tan, residual, residual_tan, mod_scale, mod_scale_tan, mod_shift, mod_shift_tan)
        state, later = attend(arrived, later)
        held_weight, held_gate, held_gate_tan, held_resid, held_resid_tan, *tables = later
        answer = attend_more(arrived, swapped, state)
    with jax.named_scope("collect"):
        attended = lax.all_to_all(answer, ("z", "y", "x"), 0, 0, tiled=True)
    with jax.named_scope("project"):
        args = (attended, held_weight, seg, held_gate, held_gate_tan)
        other = [project(side, *args, (), part) for part in range(SENDS)]
        got_mine = [lax.ppermute(x, "head", swap) for x in other]
        mine = [project(side, *args, (held_resid, held_resid_tan), part) for part in range(SENDS)]
        got_other = [lax.ppermute(x, "head", swap) for x in mine[:-1]]
        last, *settled, resid, resid_tan = settle(mine, got_mine, seg, tables)
        got_other.append(lax.ppermute(last, "head", swap))
    with jax.named_scope("norm"):
        ffn, ffn_tan = norm(side, other, got_other, settled)
    return resid, resid_tan, ffn, ffn_tan


def solution(mesh):
    fine = Mesh(mesh.devices.reshape(4, 4, 2, 2, 2), ("z", "y", "x", "c", "head"))
    seq = ("z", "y", "x", "c")
    split = P(seq, "head")
    in_specs = (split,) * 6 + (P(seq), P(seq), P("head", None), split, split) + (P(),) * 6
    out_specs = (split, split, P(seq, None), P(seq, None))
    return jax.shard_map(body, mesh=fine, in_specs=in_specs, out_specs=out_specs, check_vma=False)
```

```python
import math

import jax
import jax.numpy as jnp
import numpy as np
from jax import lax
from jax.experimental import pallas as pl
from jax.experimental.pallas import tpu as pltpu
from jax.sharding import Mesh, PartitionSpec as P

D = 5120
HD = 128
NH = 10
ROWS = 96
THIRD = 32
CHIPS = 32
PARTS = 3
SPAN = 5
K, KT, V, VT, QT, Q, TAG, MSG = 0, 96, 192, 288, 384, 416, 448, 464
HALF = D // 2

W = THIRD
KR = 768
LONG, SHORT = (21, (8, 8, 5)), (13, (8, 5))
RLONG, RSHORT = LONG[0] * THIRD, SHORT[0] * THIRD
RALL = RLONG + RSHORT

neg_fill = -1e30
norm_eps = 1e-06
rope_base = 10000.0
ln2 = math.log(2.0)
exp_scale = math.log2(math.e) / math.sqrt(HD)

f32 = jnp.float32
bf16 = jnp.bfloat16
i32 = jnp.int32
VMEM = pl.BlockSpec(memory_space=pltpu.VMEM)
ANY = pl.BlockSpec(memory_space=pl.ANY)
NT = (((1,), (1,)), ((), ()))


def worker(h, t):
    return h // SPAN * (CHIPS // 2) + h % SPAN * PARTS + t


def params(mib=56):
    return pltpu.CompilerParams(vmem_limit_bytes=mib * 2**20)


def pack_kernel(side_ref, q_hbm, k_hbm, v_hbm, qt_hbm, kt_hbm, vt_hbm, freq_ref, pos_ref, seg_ref, out_ref, tag_ref, held_ref, sem_in):
    del side_ref
    reads = [pltpu.make_async_copy(x, held_ref.at[i], sem_in.at[i]) for i, x in enumerate((q_hbm, k_hbm, v_hbm, qt_hbm, kt_hbm, vt_hbm))]
    for copy in reads:
        copy.start()
    lane = lax.broadcasted_iota(i32, (ROWS, HD), 1)
    eye = lane == lax.broadcasted_iota(i32, (ROWS, HD), 0)
    pad = jnp.zeros((1, HD - ROWS), f32)
    clip_row = seg_ref[...].astype(f32)

    def column(row):
        return jnp.sum(jnp.where(eye, jnp.concatenate([row, pad], axis=1), 0.0), axis=1, keepdims=True)

    tag = column(clip_row)
    tag_ref[...] = jnp.broadcast_to(tag, (ROWS, HD))
    row = jnp.concatenate([pad, clip_row], axis=1)
    clips = []
    for t in range(PARTS):
        first, last = (tag[t * THIRD + i : t * THIRD + i + 16] for i in (0, 16))
        clips.append(jnp.where(lane[0:16] == 0, first, jnp.where(lane[0:16] == 1, last, row)).astype(bf16))
    angles = column(pos_ref[...].astype(f32)) * freq_ref[...]
    cos = jnp.cos(angles)
    sin = jnp.where(lane < HD // 2, -1.0, 1.0) * jnp.sin(angles)

    def rot(i, cols, factor):
        x = held_ref[i, :, cols].astype(f32)
        y = x * cos + jnp.roll(x, HD // 2, axis=1) * sin
        return (y if factor is None else y * factor).astype(bf16)

    for copy in reads:
        copy.wait()
    writes = []
    for h in range(NH):
        cols = slice(h * HD, (h + 1) * HD)
        q, k = rot(0, cols, exp_scale), rot(1, cols, None)
        qt, kt = rot(3, cols, exp_scale), rot(4, cols, None)
        v, vt = held_ref[2, :, cols], held_ref[5, :, cols]
        for t in range(PARTS):
            s = worker(h, t)
            at = t * THIRD
            out_ref[s, K:KT] = k
            out_ref[s, KT:V] = kt
            out_ref[s, V:VT] = v
            out_ref[s, VT:QT] = vt
            out_ref[s, QT:Q] = qt[at : at + THIRD]
            out_ref[s, Q:TAG] = q[at : at + THIRD]
            out_ref[s, TAG:MSG] = clips[t]
        if h % SPAN == SPAN - 1:
            out_ref[worker(h, 0) + PARTS] = jnp.zeros((MSG, HD), bf16)


def in_hbm(x):
    return pltpu.with_memory_space_constraint(x, pltpu.HBM)


def in_vmem(x):
    return pltpu.with_memory_space_constraint(x, pltpu.VMEM)


def pack(side, arrays, freq, positions, segments):
    return pl.pallas_call(
        pack_kernel,
        in_specs=[pl.BlockSpec(memory_space=pltpu.SMEM)] + [ANY] * 6 + [VMEM] * 3,
        out_specs=[VMEM, VMEM],
        out_shape=[pltpu.VMEM((CHIPS, MSG, HD), bf16), pltpu.VMEM((ROWS, HD), f32)],
        scratch_shapes=[
            pltpu.VMEM((6, ROWS, NH * HD), bf16),
            pltpu.SemaphoreType.DMA((6,)),
        ],
        compiler_params=params(40),
    )(side, *[in_hbm(x) for x in (*arrays, freq, positions, segments)])


def bits(tiles):
    rows = jnp.concatenate([t.astype(f32)[0:1, :] for t in tiles], axis=0)
    lane = lax.broadcasted_iota(i32, (CHIPS, HD), 1)
    at = lax.broadcasted_iota(i32, (CHIPS, 1), 0)
    power = jnp.left_shift(jnp.ones((CHIPS, 1), i32), at & 15).astype(f32)
    has0 = 1.0 - jnp.min(jnp.where(lane < 32, 1.0, rows), axis=1, keepdims=True)
    has1 = jnp.max(jnp.where(lane < 32, 0.0, rows), axis=1, keepdims=True)

    def scalar(has):
        low = jnp.sum(jnp.where(at < 16, has * power, 0.0)).astype(i32)
        high = jnp.sum(jnp.where(at < 16, 0.0, has * power)).astype(i32)
        return low | (high << 16)

    return scalar(has0), scalar(has1)


def attn_kernel(q_ref, kv_ref, *refs, second):
    long_ref, short_ref, pen_ref, keys_ref, kind_ref, chips_ref, cut_ref = refs[-7:]
    copies = []
    if second:
        old_ref, old_stat_ref, out_ref, acc_ref, stat_ref = refs[:-7]
    else:
        n = (len(refs) - 10) // 2
        acc_ref, stat_ref = refs[n : n + 2]
        sem = refs[-8]
        for src, dst in zip(refs[:n], refs[n + 2 : 2 * n + 2]):
            cuts = FETCHES if src.shape[0] % (16 * FETCHES) == 0 else 1
            step = src.shape[0] // cuts
            for i in range(cuts):
                rows = slice(i * step, (i + 1) * step)
                copies.append(pltpu.make_async_copy(src.at[rows], dst.at[rows], sem.at[len(copies)]))
                copies[-1].start()
    asks = bits([q_ref[j, TAG:MSG, :] for j in range(CHIPS)])
    holds = bits([kv_ref[j, TAG:MSG, :] for j in range(CHIPS)]) if second else asks
    cut_ref[0] = i32(0)
    cut_ref[1] = i32(0)

    def sort(j, carry):
        cuts, counts = carry[0], list(carry[1:])
        has = [(holds[c] >> j) & 1 for c in range(2)]
        both = has[0] & has[1]
        cut_ref[jnp.where(both == 1, jnp.minimum(cuts, 1), 2)] = j
        for c in range(2):
            at = jnp.where(has[c] == 1, counts[c], 31 - (j - counts[c]))
            keys_ref[c, at] = j
            kind_ref[c, at] = jnp.where(both == 1, 2 + 2 * c + jnp.minimum(cuts, 1), 1 - has[c])
            counts[c] = counts[c] + has[c]
            ask = (asks[c] >> j) & 1
            n = counts[2 + c]
            chips_ref[c, jnp.where(ask == 1, n, 31 - (j - n))] = j
            counts[2 + c] = n + ask
        return (cuts + both, *counts)

    zero = i32(0)
    counted = lax.fori_loop(0, CHIPS, sort, (zero,) * 5)
    long_clip = jnp.where(counted[4] > 16, 1, 0)

    lane = lax.broadcasted_iota(i32, (ROWS, HD), 1)
    eye = lane == lax.broadcasted_iota(i32, (ROWS, HD), 0) + 32
    pen_ref[0] = jnp.zeros((ROWS, HD), bf16)
    pen_ref[1] = jnp.where(lane == 0, neg_fill, 0.0).astype(bf16)
    for p in range(2):
        row = kv_ref[cut_ref[p], TAG:MSG, :].astype(f32)[0:1, :]
        col = jnp.sum(jnp.where(eye, row, 0.0), axis=1, keepdims=True)
        pen_ref[2 + p] = jnp.where(lane == 0, col * neg_fill, 0.0).astype(bf16)
        pen_ref[4 + p] = jnp.where(lane == 0, (1.0 - col) * neg_fill, 0.0).astype(bf16)

    held = []
    for (chips, blocks), clip, base, s_ref in ((LONG, long_clip, 0, long_ref), (SHORT, 1 - long_clip, RLONG, short_ref)):
        R = chips * THIRD
        here = slice(base, base + R)
        listed = [chips_ref[clip, i] for i in range(chips)]
        qt, q = [jnp.concatenate([q_ref[j, at : at + THIRD, :] for j in listed], axis=0) for at in (QT, Q)]
        qq = jnp.concatenate([qt, q], axis=1)
        one = jnp.where(lax.broadcasted_iota(i32, (R, HD), 1) == 0, 1.0, 0.0).astype(bf16)
        q = jnp.concatenate([q, one], axis=1)
        m = old_stat_ref[here, 0:HD] if second else jnp.full((R, HD), neg_fill, f32)
        places = [(b, range(sum(blocks[:b]), sum(blocks[: b + 1])), -(-n * ROWS // 256) * 256) for b, n in enumerate(blocks)]
        for b, span, width in places:
            gap = width - len(span) * ROWS
            parts = [jnp.concatenate([kv_ref[keys_ref[clip, i], K:KT, :], pen_ref[kind_ref[clip, i]]], axis=1) for i in span]
            parts += [jnp.concatenate([jnp.zeros((gap, HD), bf16), pen_ref[1, 0:gap, :]], axis=1)] * (gap > 0)
            s = lax.dot_general(q, jnp.concatenate(parts, axis=0), NT, preferred_element_type=f32)
            s_ref[b, 0:R, 0:width] = s
            for j in range(width // HD):
                m = jnp.maximum(m, s[:, j * HD : (j + 1) * HD])
        top = jnp.max(m, axis=1, keepdims=True)
        m_old = old_stat_ref[here, 0:1] if second else None
        held.append((clip, here, s_ref, listed, qq, places, top, m_old, R))
    for clip, here, s_ref, listed, qq, places, top, m_old, R in held:
        for b, span, width in places:
            gap = width - len(span) * ROWS
            fill = [jnp.zeros((gap, HD), bf16)] * (gap > 0)
            js = [keys_ref[clip, i] for i in span]
            k, kt, v, vt = [jnp.concatenate([kv_ref[j, at : at + ROWS, :] for j in js] + fill, axis=0) for at in (K, KT, V, VT)]
            k = jnp.concatenate([k, kt], axis=1)
            v1 = jnp.concatenate([v, jnp.ones((width, HD), bf16)], axis=1)
            v = jnp.concatenate([v, vt], axis=1)
            st = lax.dot_general(qq, k, NT, preferred_element_type=f32)
            p = jnp.exp2(s_ref[b, 0:R, 0:width] - top)
            pt = (p * st).astype(bf16)
            l = p[:, 0:HD]
            for j in range(1, width // HD):
                l = l + p[:, j * HD : (j + 1) * HD]
            acc = jnp.dot(p.astype(bf16), v, preferred_element_type=f32)
            acct = jnp.dot(pt, v1, preferred_element_type=f32)
            if b > 0 or second:
                fade = jnp.exp2(m_old - top) if b == 0 else None
                l += stat_ref[here, HD:] if b > 0 else old_stat_ref[here, HD:] * fade
                acc += acc_ref[here, 0:256] if b > 0 else old_ref[here, 0:256] * fade
                acct += acc_ref[here, 256:512] if b > 0 else old_ref[here, 256:512] * fade
            stat_ref[here, HD:] = l
            acc_ref[here, 0:256] = acc
            acc_ref[here, 256:512] = acct
        if not second:
            stat_ref[here, 0:HD] = jnp.broadcast_to(top, (R, HD))
            continue
        total = jnp.sum(stat_ref[here, HD:], axis=1, keepdims=True)
        inv = 1.0 / total
        inv_tan = inv * ln2
        drift = acc_ref[here, 384:512] * inv_tan
        o = acc_ref[here, 0:128] * inv
        t = acc_ref[here, 256:384] * inv_tan + acc_ref[here, 128:256] * inv - drift * o
        wanted = clip.astype(f32)
        for i, j in enumerate(listed):
            at = i * W
            tags = q_ref[j, TAG:MSG, :].astype(f32)
            tag = jnp.concatenate([tags[:, 0:1], tags[:, 1:2]], axis=0)
            hit = jnp.broadcast_to(tag, (W, HD)) == wanted
            for n, x in enumerate((o, t)):
                lanes = slice(n * HD, (n + 1) * HD)
                old = out_ref[j, :, lanes].astype(f32)
                out_ref[j, :, lanes] = jnp.where(hit, x[at : at + W], old).astype(bf16)
    for copy in copies:
        copy.wait()


FETCHES = 2


def scratch():
    lists = [pltpu.SMEM((2, CHIPS), i32)] * 3 + [pltpu.SMEM((3,), i32)]
    scores = [pltpu.VMEM((len(LONG[1]), RLONG, KR), f32), pltpu.VMEM((len(SHORT[1]), RSHORT, KR), f32)]
    return scores + [pltpu.VMEM((6, ROWS, HD), bf16)] + lists


def attend(arrived, later):
    outs = pl.pallas_call(
        lambda *refs: attn_kernel(*refs, second=False),
        in_specs=[VMEM] * 2 + [ANY] * len(later),
        out_specs=[VMEM] * (2 + len(later)),
        out_shape=[pltpu.VMEM((RALL, 512), f32), pltpu.VMEM((RALL, 2 * HD), f32)] + [pltpu.VMEM(x.shape, x.dtype) for x in later],
        scratch_shapes=[pltpu.SemaphoreType.DMA((FETCHES * len(later),))] + scratch(),
        compiler_params=params(28),
        cost_estimate=pl.CostEstimate(flops=5 * 10**9, bytes_accessed=20 * 2**20, transcendentals=2 * 10**6),
    )(in_vmem(arrived), in_vmem(arrived), *[in_hbm(x) for x in later])
    return outs[:2], outs[2:]


def attend_more(arrived, swapped, state):
    return pl.pallas_call(
        lambda *refs: attn_kernel(*refs, second=True),
        in_specs=[VMEM] * 4,
        out_specs=VMEM,
        out_shape=pltpu.VMEM((CHIPS, W, 2 * HD), bf16),
        scratch_shapes=[pltpu.VMEM((RALL, 512), f32), pltpu.VMEM((RALL, 2 * HD), f32)] + scratch(),
        compiler_params=params(28),
        cost_estimate=pl.CostEstimate(flops=5 * 10**9, bytes_accessed=8 * 2**20, transcendentals=2 * 10**6),
    )(*[in_vmem(x) for x in (arrived, swapped, *state)])


CT = 512
SENDS = 5
PIECE = HALF // SENDS
STEPS = PIECE // CT


def project_kernel(side_ref, x_ref, w_ref, seg_ref, gate_ref, gate_tan_ref, *refs, own, part):
    if own:
        resid_ref, resid_tan_ref, send_ref, lhs_ref = refs
    else:
        send_ref, lhs_ref = refs
    side = side_ref[0] if own else 1 - side_ref[0]
    start = side * HALF + part * PIECE
    for h in range(NH):
        for t in range(PARTS):
            s = worker(h, t)
            lhs_ref[t * W : (t + 1) * W, h * HD : (h + 1) * HD] = x_ref[s, :, 0:HD]
            lhs_ref[ROWS + t * W : ROWS + (t + 1) * W, h * HD : (h + 1) * HD] = x_ref[s, :, HD : 2 * HD]
    one = seg_ref[:, 0:1] == 1.0
    for j in range(STEPS):
        cols = pl.ds(pl.multiple_of(start + j * CT, CT), CT)
        out = jnp.dot(lhs_ref[...], w_ref[:, cols], preferred_element_type=f32)
        here = slice(j * CT, (j + 1) * CT)
        gate = jnp.where(one, gate_ref[1:2, cols], gate_ref[0:1, cols])
        gate_tan = jnp.where(one, gate_tan_ref[1:2, cols], gate_tan_ref[0:1, cols])
        a = gate * out[0:ROWS]
        b = gate_tan * out[0:ROWS] + gate * out[ROWS : 2 * ROWS]
        if own:
            a = a + resid_ref[:, part * PIECE + j * CT : part * PIECE + (j + 1) * CT]
            b = b + resid_tan_ref[:, part * PIECE + j * CT : part * PIECE + (j + 1) * CT]
        send_ref[0, :, here] = a.astype(bf16)
        send_ref[1, :, here] = b.astype(bf16)


def project(side, x, w, seg, gate, gate_tan, resid, part):
    own = len(resid) > 0
    return pl.pallas_call(
        lambda *refs: project_kernel(*refs, own=own, part=part),
        in_specs=[pl.BlockSpec(memory_space=pltpu.SMEM)] + [VMEM] * (5 + len(resid)),
        out_specs=VMEM,
        out_shape=pltpu.VMEM((2, ROWS, PIECE), bf16),
        scratch_shapes=[
            pltpu.VMEM((2 * ROWS, NH * HD), bf16),
        ],
        compiler_params=params(16),
        cost_estimate=pl.CostEstimate(flops=2 * 2 * ROWS * NH * HD * HALF, bytes_accessed=10 * 2**20, transcendentals=0),
    )(side, *[in_vmem(x) for x in (x, w, seg, gate, gate_tan, *resid)])


FT, FN = 16, 16


def moments(a, b):
    lane = lax.broadcasted_iota(i32, (a.shape[0], HD), 1)
    out = jnp.zeros((a.shape[0], HD), f32)
    for i, x in enumerate((a, a * a, b, a * b)):
        out = jnp.where(lane == i, jnp.sum(x, axis=1, keepdims=True), out)
    return out


def settle_kernel(*refs):
    kept, got, refs = refs[:SENDS], refs[SENDS : 2 * SENDS], refs[2 * SENDS :]
    seg_ref, tables, (pass_ref, a_ref, b_ref, sums_ref, rows_ref, resid_hbm, resid_tan_hbm, sem) = refs[0], refs[1:5], refs[5:]
    del pass_ref
    copies = []
    for step in range(ROWS // FT):
        at = slice(step * FT, (step + 1) * FT)
        a, b = (jnp.concatenate([x[i, at].astype(f32) + y[i, at].astype(f32) for x, y in zip(kept, got)], axis=1) for i in range(2))
        a_ref[at] = a
        b_ref[at] = b
        sums_ref[at] = moments(a, b)
        for i, (src, dst) in enumerate(((a_ref, resid_hbm), (b_ref, resid_tan_hbm))):
            copies.append(pltpu.make_async_copy(src.at[at], dst.at[at], sem.at[step, i]))
            copies[-1].start()
    one = seg_ref[:, 0:1] == 1.0
    for i, table in enumerate(tables):
        row = jnp.where(one, table[1:2, :], table[0:1, :])
        rows_ref[i] = row + 1.0 if i == 0 else row
    for copy in copies:
        copy.wait()


def settle(kept, got, seg, tables):
    half, out = pltpu.VMEM((ROWS, HALF), f32), jax.ShapeDtypeStruct((ROWS, HALF), f32)
    return pl.pallas_call(
        settle_kernel,
        in_specs=[VMEM] * (2 * SENDS + 5),
        out_specs=[VMEM] * 5 + [ANY] * 2,
        out_shape=[pltpu.VMEM((2, ROWS, PIECE), bf16), half, half, pltpu.VMEM((ROWS, HD), f32), pltpu.VMEM((4, ROWS, D), f32), out, out],
        input_output_aliases={SENDS - 1: 0},
        scratch_shapes=[pltpu.SemaphoreType.DMA((ROWS // FT, 2))],
        compiler_params=params(16),
    )(*[in_vmem(x) for x in (*kept, *got, seg, *tables)])


def norm_kernel(side_ref, *refs):
    rows = [refs[i * SENDS : (i + 1) * SENDS] for i in range(2)]
    a_ref, b_ref, sums_ref, rows_ref = refs[2 * SENDS : 2 * SENDS + 4]
    outs, held, sem = refs[2 * SENDS + 4 : 2 * SENDS + 6], refs[2 * SENDS + 6 : 2 * SENDS + 8], refs[-1]
    ffn_ref, ffn_tan_ref = held
    copies = []
    for step in range(ROWS // FN):
        at = slice(step * FN, (step + 1) * FN)
        a, b = (jnp.concatenate([x[i, at].astype(f32) + y[i, at].astype(f32) for x, y in zip(*rows)], axis=1) for i in range(2))
        total = (moments(a, b) + sums_ref[at]) / D
        mean, mean_tan = total[:, 0:1], total[:, 2:3]
        rstd = lax.rsqrt(total[:, 1:2] - mean * mean + norm_eps)
        cov = total[:, 3:4] - mean * mean_tan
        slope = rstd * rstd * rstd * cov
        for side, x, y in ((1 - side_ref[0], a, b), (side_ref[0], a_ref[at], b_ref[at])):
            cols = pl.ds(pl.multiple_of(side * HALF, HALF), HALF)
            centered = x - mean
            normed = centered * rstd
            normed_tan = (y - mean_tan) * rstd - centered * slope
            scale, scale_tan, shift, shift_tan = (rows_ref[i, at, cols] for i in range(4))
            ffn_ref[at, cols] = (normed * scale + shift).astype(bf16)
            ffn_tan_ref[at, cols] = (normed_tan * scale + normed * scale_tan + shift_tan).astype(bf16)
        for i in range(2):
            copies.append(pltpu.make_async_copy(held[i].at[at], outs[i].at[at], sem.at[step, i]))
            copies[-1].start()
    for copy in copies:
        copy.wait()


def norm(side, other, got_other, settled):
    outs = [jax.ShapeDtypeStruct((ROWS, D), bf16)] * 2
    return pl.pallas_call(
        norm_kernel,
        in_specs=[pl.BlockSpec(memory_space=pltpu.SMEM)] + [VMEM] * (2 * SENDS + 4),
        out_specs=[ANY] * 2,
        out_shape=outs,
        scratch_shapes=[pltpu.VMEM(x.shape, x.dtype) for x in outs] + [pltpu.SemaphoreType.DMA((ROWS // FN, 2))],
        compiler_params=params(32),
    )(side, *[in_vmem(x) for x in (*other, *got_other, *settled)])


def body(
    queries, keys, values, queries_tan, keys_tan, values_tan, segments, positions, out_weight,
    residual, residual_tan, gate, gate_tan, mod_scale, mod_scale_tan, mod_shift, mod_shift_tan,
):
    frequency = np.float32(rope_base) ** (-np.arange(HD // 2, dtype=np.float32) / np.float32(HD // 2))
    freq = np.concatenate([frequency, frequency])[None, :].astype(np.float32)
    swap = [(0, 1), (1, 0)]

    side = lax.axis_index("head").astype(i32).reshape(1)
    with jax.named_scope("pack"):
        arrays = (queries, keys, values, queries_tan, keys_tan, values_tan)
        message, seg = pack(side, arrays, freq, positions[None, :], segments[None, :])
    with jax.named_scope("spread"):
        arrived = lax.all_to_all(message, ("x", "z", "y"), 0, 0, tiled=True)
        swapped = lax.ppermute(arrived, "c", swap)
    with jax.named_scope("attend"):
        later = (out_weight, gate, gate_tan, residual, residual_tan, mod_scale, mod_scale_tan, mod_shift, mod_shift_tan)
        state, later = attend(arrived, later)
        held_weight, held_gate, held_gate_tan, held_resid, held_resid_tan, *tables = later
        answer = attend_more(arrived, swapped, state)
    with jax.named_scope("collect"):
        attended = lax.all_to_all(answer, ("x", "z", "y"), 0, 0, tiled=True)
    with jax.named_scope("project"):
        args = (attended, held_weight, seg, held_gate, held_gate_tan)
        other = [project(side, *args, (), part) for part in range(SENDS)]
        got_mine = [lax.ppermute(x, "head", swap) for x in other]
        mine = [project(side, *args, (held_resid, held_resid_tan), part) for part in range(SENDS)]
        got_other = [lax.ppermute(x, "head", swap) for x in mine[:-1]]
        last, *settled, resid, resid_tan = settle(mine, got_mine, seg, tables)
        got_other.append(lax.ppermute(last, "head", swap))
    with jax.named_scope("norm"):
        ffn, ffn_tan = norm(side, other, got_other, settled)
    return resid, resid_tan, ffn, ffn_tan


def solution(mesh):
    fine = Mesh(mesh.devices.reshape(4, 4, 2, 2, 2), ("z", "y", "x", "c", "head"))
    seq = ("z", "y", "x", "c")
    split = P(seq, "head")
    in_specs = (split,) * 6 + (P(seq), P(seq), P("head", None), split, split) + (P(),) * 6
    out_specs = (split, split, P(seq, None), P(seq, None))
    return jax.shard_map(body, mesh=fine, in_specs=in_specs, out_specs=out_specs, check_vma=False)
```

```python
import math

import jax
import jax.numpy as jnp
import numpy as np
from jax import lax
from jax.experimental import pallas as pl
from jax.experimental.pallas import tpu as pltpu
from jax.sharding import Mesh, PartitionSpec as P

D = 5120
HD = 128
NH = 10
ROWS = 96
THIRD = 32
CHIPS = 32
PARTS = 3
SPAN = 5
K, KT, V, VT, QT, Q, TAG, MSG = 0, 96, 192, 288, 384, 416, 448, 464
HALF = D // 2

W = THIRD
KR = 768
LONG, SHORT = (21, (8, 8, 5)), (13, (8, 5))
RLONG, RSHORT = LONG[0] * THIRD, SHORT[0] * THIRD
RALL = RLONG + RSHORT

neg_fill = -1e30
norm_eps = 1e-06
rope_base = 10000.0
ln2 = math.log(2.0)
exp_scale = math.log2(math.e) / math.sqrt(HD)

f32 = jnp.float32
bf16 = jnp.bfloat16
i32 = jnp.int32
VMEM = pl.BlockSpec(memory_space=pltpu.VMEM)
ANY = pl.BlockSpec(memory_space=pl.ANY)
NT = (((1,), (1,)), ((), ()))


def worker(h, t):
    return h // SPAN * (CHIPS // 2) + h % SPAN * PARTS + t


def params(mib=56):
    return pltpu.CompilerParams(vmem_limit_bytes=mib * 2**20)


def pack_kernel(side_ref, q_hbm, k_hbm, v_hbm, qt_hbm, kt_hbm, vt_hbm, freq_ref, pos_ref, seg_ref, out_ref, tag_ref, held_ref, sem_in):
    del side_ref
    reads = []
    for part in range(NH // SPAN):
        cols = slice(part * SPAN * HD, (part + 1) * SPAN * HD)
        for i, x in enumerate((q_hbm, k_hbm, v_hbm, qt_hbm, kt_hbm, vt_hbm)):
            reads.append(pltpu.make_async_copy(x.at[:, cols], held_ref.at[i, :, cols], sem_in.at[part, i]))
            reads[-1].start()
    lane = lax.broadcasted_iota(i32, (ROWS, HD), 1)
    eye = lane == lax.broadcasted_iota(i32, (ROWS, HD), 0)
    pad = jnp.zeros((1, HD - ROWS), f32)
    clip_row = seg_ref[...].astype(f32)

    def column(row):
        return jnp.sum(jnp.where(eye, jnp.concatenate([row, pad], axis=1), 0.0), axis=1, keepdims=True)

    tag = column(clip_row)
    tag_ref[...] = jnp.broadcast_to(tag, (ROWS, HD))
    row = jnp.concatenate([pad, clip_row], axis=1)
    clips = []
    for t in range(PARTS):
        first, last = (tag[t * THIRD + i : t * THIRD + i + 16] for i in (0, 16))
        clips.append(jnp.where(lane[0:16] == 0, first, jnp.where(lane[0:16] == 1, last, row)).astype(bf16))
    angles = column(pos_ref[...].astype(f32)) * freq_ref[...]
    cos = jnp.cos(angles)
    sin = jnp.where(lane < HD // 2, -1.0, 1.0) * jnp.sin(angles)

    def rot(i, cols, factor):
        x = held_ref[i, :, cols].astype(f32)
        y = x * cos + jnp.roll(x, HD // 2, axis=1) * sin
        return (y if factor is None else y * factor).astype(bf16)

    writes = []
    for h in range(NH):
        if h % SPAN == 0:
            for copy in reads[h // SPAN * 6 : h // SPAN * 6 + 6]:
                copy.wait()
        cols = slice(h * HD, (h + 1) * HD)
        q, k = rot(0, cols, exp_scale), rot(1, cols, None)
        qt, kt = rot(3, cols, exp_scale), rot(4, cols, None)
        v, vt = held_ref[2, :, cols], held_ref[5, :, cols]
        for t in range(PARTS):
            s = worker(h, t)
            at = t * THIRD
            out_ref[s, K:KT] = k
            out_ref[s, KT:V] = kt
            out_ref[s, V:VT] = v
            out_ref[s, VT:QT] = vt
            out_ref[s, QT:Q] = qt[at : at + THIRD]
            out_ref[s, Q:TAG] = q[at : at + THIRD]
            out_ref[s, TAG:MSG] = clips[t]
        if h % SPAN == SPAN - 1:
            out_ref[worker(h, 0) + PARTS] = jnp.zeros((MSG, HD), bf16)


def in_hbm(x):
    return pltpu.with_memory_space_constraint(x, pltpu.HBM)


def in_vmem(x):
    return pltpu.with_memory_space_constraint(x, pltpu.VMEM)


def pack(side, arrays, freq, positions, segments):
    return pl.pallas_call(
        pack_kernel,
        in_specs=[pl.BlockSpec(memory_space=pltpu.SMEM)] + [ANY] * 6 + [VMEM] * 3,
        out_specs=[VMEM, VMEM],
        out_shape=[pltpu.VMEM((CHIPS, MSG, HD), bf16), pltpu.VMEM((ROWS, HD), f32)],
        scratch_shapes=[
            pltpu.VMEM((6, ROWS, NH * HD), bf16),
            pltpu.SemaphoreType.DMA((NH // SPAN, 6)),
        ],
        compiler_params=params(40),
    )(side, *[in_hbm(x) for x in (*arrays, freq, positions, segments)])


def bits(tiles):
    rows = jnp.concatenate([t.astype(f32)[0:1, :] for t in tiles], axis=0)
    lane = lax.broadcasted_iota(i32, (CHIPS, HD), 1)
    at = lax.broadcasted_iota(i32, (CHIPS, 1), 0)
    power = jnp.left_shift(jnp.ones((CHIPS, 1), i32), at & 15).astype(f32)
    has0 = 1.0 - jnp.min(jnp.where(lane < 32, 1.0, rows), axis=1, keepdims=True)
    has1 = jnp.max(jnp.where(lane < 32, 0.0, rows), axis=1, keepdims=True)

    def scalar(has):
        low = jnp.sum(jnp.where(at < 16, has * power, 0.0)).astype(i32)
        high = jnp.sum(jnp.where(at < 16, 0.0, has * power)).astype(i32)
        return low | (high << 16)

    return scalar(has0), scalar(has1)


def attn_kernel(q_ref, kv_ref, *refs, second):
    long_ref, short_ref, pen_ref, keys_ref, kind_ref, chips_ref, cut_ref = refs[-7:]
    copies = []
    if second:
        old_ref, old_stat_ref, out_ref, acc_ref, stat_ref = refs[:-7]
    else:
        n = (len(refs) - 10) // 2
        acc_ref, stat_ref = refs[n : n + 2]
        sem = refs[-8]
        for src, dst in zip(refs[:n], refs[n + 2 : 2 * n + 2]):
            cuts = FETCHES if src.shape[0] % (16 * FETCHES) == 0 else 1
            step = src.shape[0] // cuts
            for i in range(cuts):
                rows = slice(i * step, (i + 1) * step)
                copies.append(pltpu.make_async_copy(src.at[rows], dst.at[rows], sem.at[len(copies)]))
                copies[-1].start()
    asks = bits([q_ref[j, TAG:MSG, :] for j in range(CHIPS)])
    holds = bits([kv_ref[j, TAG:MSG, :] for j in range(CHIPS)]) if second else asks
    cut_ref[0] = i32(0)
    cut_ref[1] = i32(0)

    def sort(j, carry):
        cuts, counts = carry[0], list(carry[1:])
        has = [(holds[c] >> j) & 1 for c in range(2)]
        both = has[0] & has[1]
        cut_ref[jnp.where(both == 1, jnp.minimum(cuts, 1), 2)] = j
        for c in range(2):
            at = jnp.where(has[c] == 1, counts[c], 31 - (j - counts[c]))
            keys_ref[c, at] = j
            kind_ref[c, at] = jnp.where(both == 1, 2 + 2 * c + jnp.minimum(cuts, 1), 1 - has[c])
            counts[c] = counts[c] + has[c]
            ask = (asks[c] >> j) & 1
            n = counts[2 + c]
            chips_ref[c, jnp.where(ask == 1, n, 31 - (j - n))] = j
            counts[2 + c] = n + ask
        return (cuts + both, *counts)

    zero = i32(0)
    counted = lax.fori_loop(0, CHIPS, sort, (zero,) * 5)
    long_clip = jnp.where(counted[4] > 16, 1, 0)

    lane = lax.broadcasted_iota(i32, (ROWS, HD), 1)
    eye = lane == lax.broadcasted_iota(i32, (ROWS, HD), 0) + 32
    pen_ref[0] = jnp.zeros((ROWS, HD), bf16)
    pen_ref[1] = jnp.where(lane == 0, neg_fill, 0.0).astype(bf16)
    for p in range(2):
        row = kv_ref[cut_ref[p], TAG:MSG, :].astype(f32)[0:1, :]
        col = jnp.sum(jnp.where(eye, row, 0.0), axis=1, keepdims=True)
        pen_ref[2 + p] = jnp.where(lane == 0, col * neg_fill, 0.0).astype(bf16)
        pen_ref[4 + p] = jnp.where(lane == 0, (1.0 - col) * neg_fill, 0.0).astype(bf16)

    held = []
    for (chips, blocks), clip, base, s_ref in ((LONG, long_clip, 0, long_ref), (SHORT, 1 - long_clip, RLONG, short_ref)):
        R = chips * THIRD
        here = slice(base, base + R)
        listed = [chips_ref[clip, i] for i in range(chips)]
        qt, q = [jnp.concatenate([q_ref[j, at : at + THIRD, :] for j in listed], axis=0) for at in (QT, Q)]
        qq = jnp.concatenate([qt, q], axis=1)
        one = jnp.where(lax.broadcasted_iota(i32, (R, HD), 1) == 0, 1.0, 0.0).astype(bf16)
        q = jnp.concatenate([q, one], axis=1)
        m = old_stat_ref[here, 0:HD] if second else jnp.full((R, HD), neg_fill, f32)
        places = [(b, range(sum(blocks[:b]), sum(blocks[: b + 1])), -(-n * ROWS // 256) * 256) for b, n in enumerate(blocks)]
        for b, span, width in places:
            gap = width - len(span) * ROWS
            parts = [jnp.concatenate([kv_ref[keys_ref[clip, i], K:KT, :], pen_ref[kind_ref[clip, i]]], axis=1) for i in span]
            parts += [jnp.concatenate([jnp.zeros((gap, HD), bf16), pen_ref[1, 0:gap, :]], axis=1)] * (gap > 0)
            s = lax.dot_general(q, jnp.concatenate(parts, axis=0), NT, preferred_element_type=f32)
            s_ref[b, 0:R, 0:width] = s
            for j in range(width // HD):
                m = jnp.maximum(m, s[:, j * HD : (j + 1) * HD])
        top = jnp.max(m, axis=1, keepdims=True)
        m_old = old_stat_ref[here, 0:1] if second else None
        held.append((clip, here, s_ref, listed, qq, places, top, m_old, R))
    for clip, here, s_ref, listed, qq, places, top, m_old, R in held:
        for b, span, width in places:
            gap = width - len(span) * ROWS
            fill = [jnp.zeros((gap, HD), bf16)] * (gap > 0)
            js = [keys_ref[clip, i] for i in span]
            k, kt, v, vt = [jnp.concatenate([kv_ref[j, at : at + ROWS, :] for j in js] + fill, axis=0) for at in (K, KT, V, VT)]
            k = jnp.concatenate([k, kt], axis=1)
            v1 = jnp.concatenate([v, jnp.ones((width, HD), bf16)], axis=1)
            v = jnp.concatenate([v, vt], axis=1)
            st = lax.dot_general(qq, k, NT, preferred_element_type=f32)
            p = jnp.exp2(s_ref[b, 0:R, 0:width] - top)
            pt = (p * st).astype(bf16)
            l = p[:, 0:HD]
            for j in range(1, width // HD):
                l = l + p[:, j * HD : (j + 1) * HD]
            acc = jnp.dot(p.astype(bf16), v, preferred_element_type=f32)
            acct = jnp.dot(pt, v1, preferred_element_type=f32)
            if b > 0 or second:
                fade = jnp.exp2(m_old - top) if b == 0 else None
                l += stat_ref[here, HD:] if b > 0 else old_stat_ref[here, HD:] * fade
                acc += acc_ref[here, 0:256] if b > 0 else old_ref[here, 0:256] * fade
                acct += acc_ref[here, 256:512] if b > 0 else old_ref[here, 256:512] * fade
            stat_ref[here, HD:] = l
            acc_ref[here, 0:256] = acc
            acc_ref[here, 256:512] = acct
        if not second:
            stat_ref[here, 0:HD] = jnp.broadcast_to(top, (R, HD))
            continue
        total = jnp.sum(stat_ref[here, HD:], axis=1, keepdims=True)
        inv = 1.0 / total
        inv_tan = inv * ln2
        drift = acc_ref[here, 384:512] * inv_tan
        o = acc_ref[here, 0:128] * inv
        t = acc_ref[here, 256:384] * inv_tan + acc_ref[here, 128:256] * inv - drift * o
        wanted = clip.astype(f32)
        for i, j in enumerate(listed):
            at = i * W
            tags = q_ref[j, TAG:MSG, :].astype(f32)
            tag = jnp.concatenate([tags[:, 0:1], tags[:, 1:2]], axis=0)
            hit = jnp.broadcast_to(tag, (W, HD)) == wanted
            for n, x in enumerate((o, t)):
                lanes = slice(n * HD, (n + 1) * HD)
                old = out_ref[j, :, lanes].astype(f32)
                out_ref[j, :, lanes] = jnp.where(hit, x[at : at + W], old).astype(bf16)
    for copy in copies:
        copy.wait()


FETCHES = 2


def scratch():
    lists = [pltpu.SMEM((2, CHIPS), i32)] * 3 + [pltpu.SMEM((3,), i32)]
    scores = [pltpu.VMEM((len(LONG[1]), RLONG, KR), f32), pltpu.VMEM((len(SHORT[1]), RSHORT, KR), f32)]
    return scores + [pltpu.VMEM((6, ROWS, HD), bf16)] + lists


def attend(arrived, later):
    outs = pl.pallas_call(
        lambda *refs: attn_kernel(*refs, second=False),
        in_specs=[VMEM] * 2 + [ANY] * len(later),
        out_specs=[VMEM] * (2 + len(later)),
        out_shape=[pltpu.VMEM((RALL, 512), f32), pltpu.VMEM((RALL, 2 * HD), f32)] + [pltpu.VMEM(x.shape, x.dtype) for x in later],
        scratch_shapes=[pltpu.SemaphoreType.DMA((FETCHES * len(later),))] + scratch(),
        compiler_params=params(28),
        cost_estimate=pl.CostEstimate(flops=5 * 10**9, bytes_accessed=20 * 2**20, transcendentals=2 * 10**6),
    )(in_vmem(arrived), in_vmem(arrived), *[in_hbm(x) for x in later])
    return outs[:2], outs[2:]


def attend_more(arrived, swapped, state):
    return pl.pallas_call(
        lambda *refs: attn_kernel(*refs, second=True),
        in_specs=[VMEM] * 4,
        out_specs=VMEM,
        out_shape=pltpu.VMEM((CHIPS, W, 2 * HD), bf16),
        scratch_shapes=[pltpu.VMEM((RALL, 512), f32), pltpu.VMEM((RALL, 2 * HD), f32)] + scratch(),
        compiler_params=params(28),
        cost_estimate=pl.CostEstimate(flops=5 * 10**9, bytes_accessed=8 * 2**20, transcendentals=2 * 10**6),
    )(*[in_vmem(x) for x in (arrived, swapped, *state)])


CT = 512
SENDS = 5
PIECE = HALF // SENDS
STEPS = PIECE // CT


def project_kernel(side_ref, x_ref, w_ref, seg_ref, gate_ref, gate_tan_ref, *refs, own, part):
    if own:
        resid_ref, resid_tan_ref, send_ref, lhs_ref = refs
    else:
        send_ref, lhs_ref = refs
    side = side_ref[0] if own else 1 - side_ref[0]
    start = side * HALF + part * PIECE
    for h in range(NH):
        for t in range(PARTS):
            s = worker(h, t)
            lhs_ref[t * W : (t + 1) * W, h * HD : (h + 1) * HD] = x_ref[s, :, 0:HD]
            lhs_ref[ROWS + t * W : ROWS + (t + 1) * W, h * HD : (h + 1) * HD] = x_ref[s, :, HD : 2 * HD]
    one = seg_ref[:, 0:1] == 1.0
    for j in range(STEPS):
        cols = pl.ds(pl.multiple_of(start + j * CT, CT), CT)
        out = jnp.dot(lhs_ref[...], w_ref[:, cols], preferred_element_type=f32)
        here = slice(j * CT, (j + 1) * CT)
        gate = jnp.where(one, gate_ref[1:2, cols], gate_ref[0:1, cols])
        gate_tan = jnp.where(one, gate_tan_ref[1:2, cols], gate_tan_ref[0:1, cols])
        a = gate * out[0:ROWS]
        b = gate_tan * out[0:ROWS] + gate * out[ROWS : 2 * ROWS]
        if own:
            a = a + resid_ref[:, part * PIECE + j * CT : part * PIECE + (j + 1) * CT]
            b = b + resid_tan_ref[:, part * PIECE + j * CT : part * PIECE + (j + 1) * CT]
        send_ref[0, :, here] = a.astype(bf16)
        send_ref[1, :, here] = b.astype(bf16)


def project(side, x, w, seg, gate, gate_tan, resid, part):
    own = len(resid) > 0
    return pl.pallas_call(
        lambda *refs: project_kernel(*refs, own=own, part=part),
        in_specs=[pl.BlockSpec(memory_space=pltpu.SMEM)] + [VMEM] * (5 + len(resid)),
        out_specs=VMEM,
        out_shape=pltpu.VMEM((2, ROWS, PIECE), bf16),
        scratch_shapes=[
            pltpu.VMEM((2 * ROWS, NH * HD), bf16),
        ],
        compiler_params=params(16),
        cost_estimate=pl.CostEstimate(flops=2 * 2 * ROWS * NH * HD * HALF, bytes_accessed=10 * 2**20, transcendentals=0),
    )(side, *[in_vmem(x) for x in (x, w, seg, gate, gate_tan, *resid)])


FT, FN = 16, 16


def moments(a, b):
    lane = lax.broadcasted_iota(i32, (a.shape[0], HD), 1)
    out = jnp.zeros((a.shape[0], HD), f32)
    for i, x in enumerate((a, a * a, b, a * b)):
        out = jnp.where(lane == i, jnp.sum(x, axis=1, keepdims=True), out)
    return out


def settle_kernel(*refs):
    kept, got, refs = refs[:SENDS], refs[SENDS : 2 * SENDS], refs[2 * SENDS :]
    seg_ref, tables, (pass_ref, a_ref, b_ref, sums_ref, rows_ref, resid_hbm, resid_tan_hbm, sem) = refs[0], refs[1:5], refs[5:]
    del pass_ref
    copies = []
    for step in range(ROWS // FT):
        at = slice(step * FT, (step + 1) * FT)
        a, b = (jnp.concatenate([x[i, at].astype(f32) + y[i, at].astype(f32) for x, y in zip(kept, got)], axis=1) for i in range(2))
        a_ref[at] = a
        b_ref[at] = b
        sums_ref[at] = moments(a, b)
        for i, (src, dst) in enumerate(((a_ref, resid_hbm), (b_ref, resid_tan_hbm))):
            copies.append(pltpu.make_async_copy(src.at[at], dst.at[at], sem.at[step, i]))
            copies[-1].start()
    one = seg_ref[:, 0:1] == 1.0
    for i, table in enumerate(tables):
        row = jnp.where(one, table[1:2, :], table[0:1, :])
        rows_ref[i] = row + 1.0 if i == 0 else row
    for copy in copies:
        copy.wait()


def settle(kept, got, seg, tables):
    half, out = pltpu.VMEM((ROWS, HALF), f32), jax.ShapeDtypeStruct((ROWS, HALF), f32)
    return pl.pallas_call(
        settle_kernel,
        in_specs=[VMEM] * (2 * SENDS + 5),
        out_specs=[VMEM] * 5 + [ANY] * 2,
        out_shape=[pltpu.VMEM((2, ROWS, PIECE), bf16), half, half, pltpu.VMEM((ROWS, HD), f32), pltpu.VMEM((4, ROWS, D), f32), out, out],
        input_output_aliases={SENDS - 1: 0},
        scratch_shapes=[pltpu.SemaphoreType.DMA((ROWS // FT, 2))],
        compiler_params=params(16),
    )(*[in_vmem(x) for x in (*kept, *got, seg, *tables)])


def norm_kernel(side_ref, *refs):
    rows = [refs[i * SENDS : (i + 1) * SENDS] for i in range(2)]
    a_ref, b_ref, sums_ref, rows_ref = refs[2 * SENDS : 2 * SENDS + 4]
    outs, held, sem = refs[2 * SENDS + 4 : 2 * SENDS + 6], refs[2 * SENDS + 6 : 2 * SENDS + 8], refs[-1]
    ffn_ref, ffn_tan_ref = held
    copies = []
    for step in range(ROWS // FN):
        at = slice(step * FN, (step + 1) * FN)
        a, b = (jnp.concatenate([x[i, at].astype(f32) + y[i, at].astype(f32) for x, y in zip(*rows)], axis=1) for i in range(2))
        total = (moments(a, b) + sums_ref[at]) / D
        mean, mean_tan = total[:, 0:1], total[:, 2:3]
        rstd = lax.rsqrt(total[:, 1:2] - mean * mean + norm_eps)
        cov = total[:, 3:4] - mean * mean_tan
        slope = rstd * rstd * rstd * cov
        for side, x, y in ((1 - side_ref[0], a, b), (side_ref[0], a_ref[at], b_ref[at])):
            cols = pl.ds(pl.multiple_of(side * HALF, HALF), HALF)
            centered = x - mean
            normed = centered * rstd
            normed_tan = (y - mean_tan) * rstd - centered * slope
            scale, scale_tan, shift, shift_tan = (rows_ref[i, at, cols] for i in range(4))
            ffn_ref[at, cols] = (normed * scale + shift).astype(bf16)
            ffn_tan_ref[at, cols] = (normed_tan * scale + normed * scale_tan + shift_tan).astype(bf16)
        for i in range(2):
            copies.append(pltpu.make_async_copy(held[i].at[at], outs[i].at[at], sem.at[step, i]))
            copies[-1].start()
    for copy in copies:
        copy.wait()


def norm(side, other, got_other, settled):
    outs = [jax.ShapeDtypeStruct((ROWS, D), bf16)] * 2
    return pl.pallas_call(
        norm_kernel,
        in_specs=[pl.BlockSpec(memory_space=pltpu.SMEM)] + [VMEM] * (2 * SENDS + 4),
        out_specs=[ANY] * 2,
        out_shape=outs,
        scratch_shapes=[pltpu.VMEM(x.shape, x.dtype) for x in outs] + [pltpu.SemaphoreType.DMA((ROWS // FN, 2))],
        compiler_params=params(32),
    )(side, *[in_vmem(x) for x in (*other, *got_other, *settled)])


def body(
    queries, keys, values, queries_tan, keys_tan, values_tan, segments, positions, out_weight,
    residual, residual_tan, gate, gate_tan, mod_scale, mod_scale_tan, mod_shift, mod_shift_tan,
):
    frequency = np.float32(rope_base) ** (-np.arange(HD // 2, dtype=np.float32) / np.float32(HD // 2))
    freq = np.concatenate([frequency, frequency])[None, :].astype(np.float32)
    swap = [(0, 1), (1, 0)]

    side = lax.axis_index("head").astype(i32).reshape(1)
    with jax.named_scope("pack"):
        arrays = (queries, keys, values, queries_tan, keys_tan, values_tan)
        message, seg = pack(side, arrays, freq, positions[None, :], segments[None, :])
    with jax.named_scope("spread"):
        arrived = lax.all_to_all(message, ("x", "y", "z"), 0, 0, tiled=True)
        swapped = lax.ppermute(arrived, "c", swap)
    with jax.named_scope("attend"):
        later = (out_weight, gate, gate_tan, residual, residual_tan, mod_scale, mod_scale_tan, mod_shift, mod_shift_tan)
        state, later = attend(arrived, later)
        held_weight, held_gate, held_gate_tan, held_resid, held_resid_tan, *tables = later
        answer = attend_more(arrived, swapped, state)
    with jax.named_scope("collect"):
        attended = lax.all_to_all(answer, ("x", "y", "z"), 0, 0, tiled=True)
    with jax.named_scope("project"):
        args = (attended, held_weight, seg, held_gate, held_gate_tan)
        other = [project(side, *args, (), part) for part in range(SENDS)]
        got_mine = [lax.ppermute(x, "head", swap) for x in other]
        mine = [project(side, *args, (held_resid, held_resid_tan), part) for part in range(SENDS)]
        got_other = [lax.ppermute(x, "head", swap) for x in mine[:-1]]
        last, *settled, resid, resid_tan = settle(mine, got_mine, seg, tables)
        got_other.append(lax.ppermute(last, "head", swap))
    with jax.named_scope("norm"):
        ffn, ffn_tan = norm(side, other, got_other, settled)
    return resid, resid_tan, ffn, ffn_tan


def solution(mesh):
    fine = Mesh(mesh.devices.reshape(4, 4, 2, 2, 2), ("z", "y", "x", "c", "head"))
    seq = ("z", "y", "x", "c")
    split = P(seq, "head")
    in_specs = (split,) * 6 + (P(seq), P(seq), P("head", None), split, split) + (P(),) * 6
    out_specs = (split, split, P(seq, None), P(seq, None))
    return jax.shard_map(body, mesh=fine, in_specs=in_specs, out_specs=out_specs, check_vma=False)
```

```python
import math

import jax
import jax.numpy as jnp
import numpy as np
from jax import lax
from jax.experimental import pallas as pl
from jax.experimental.pallas import tpu as pltpu
from jax.sharding import Mesh, PartitionSpec as P

D = 5120
HD = 128
NH = 10
ROWS = 96
THIRD = 32
CHIPS = 32
PARTS = 3
SPAN = 5
K, KT, V, VT, QT, Q, TAG, MSG = 0, 96, 192, 288, 384, 416, 448, 464
HALF = D // 2

W = THIRD
KR = 768
LONG, SHORT = (21, (8, 8, 5)), (13, (8, 5))
RLONG, RSHORT = LONG[0] * THIRD, SHORT[0] * THIRD
RALL = RLONG + RSHORT

neg_fill = -1e30
norm_eps = 1e-06
rope_base = 10000.0
ln2 = math.log(2.0)
exp_scale = math.log2(math.e) / math.sqrt(HD)

f32 = jnp.float32
bf16 = jnp.bfloat16
i32 = jnp.int32
VMEM = pl.BlockSpec(memory_space=pltpu.VMEM)
ANY = pl.BlockSpec(memory_space=pl.ANY)
NT = (((1,), (1,)), ((), ()))


def worker(h, t):
    return h // SPAN * (CHIPS // 2) + h % SPAN * PARTS + t


def params(mib=56):
    return pltpu.CompilerParams(vmem_limit_bytes=mib * 2**20)


def pack_kernel(side_ref, q_hbm, k_hbm, v_hbm, qt_hbm, kt_hbm, vt_hbm, freq_ref, pos_ref, seg_ref, out_ref, tag_ref, held_ref, sem_in):
    del side_ref
    reads = []
    for part in range(NH // SPAN):
        cols = slice(part * SPAN * HD, (part + 1) * SPAN * HD)
        for i, x in enumerate((q_hbm, k_hbm, v_hbm, qt_hbm, kt_hbm, vt_hbm)):
            reads.append(pltpu.make_async_copy(x.at[:, cols], held_ref.at[i, :, cols], sem_in.at[part, i]))
            reads[-1].start()
    lane = lax.broadcasted_iota(i32, (ROWS, HD), 1)
    eye = lane == lax.broadcasted_iota(i32, (ROWS, HD), 0)
    pad = jnp.zeros((1, HD - ROWS), f32)
    clip_row = seg_ref[...].astype(f32)

    def column(row):
        return jnp.sum(jnp.where(eye, jnp.concatenate([row, pad], axis=1), 0.0), axis=1, keepdims=True)

    tag = column(clip_row)
    tag_ref[...] = jnp.broadcast_to(tag, (ROWS, HD))
    row = jnp.concatenate([pad, clip_row], axis=1)
    clips = []
    for t in range(PARTS):
        first, last = (tag[t * THIRD + i : t * THIRD + i + 16] for i in (0, 16))
        clips.append(jnp.where(lane[0:16] == 0, first, jnp.where(lane[0:16] == 1, last, row)).astype(bf16))
    angles = column(pos_ref[...].astype(f32)) * freq_ref[...]
    cos = jnp.cos(angles)
    sin = jnp.where(lane < HD // 2, -1.0, 1.0) * jnp.sin(angles)

    def rot(i, cols, factor):
        x = held_ref[i, :, cols].astype(f32)
        y = x * cos + jnp.roll(x, HD // 2, axis=1) * sin
        return (y if factor is None else y * factor).astype(bf16)

    writes = []
    for h in range(NH):
        if h % SPAN == 0:
            for copy in reads[h // SPAN * 6 : h // SPAN * 6 + 6]:
                copy.wait()
        cols = slice(h * HD, (h + 1) * HD)
        q, k = rot(0, cols, exp_scale), rot(1, cols, None)
        qt, kt = rot(3, cols, exp_scale), rot(4, cols, None)
        v, vt = held_ref[2, :, cols], held_ref[5, :, cols]
        for t in range(PARTS):
            s = worker(h, t)
            at = t * THIRD
            out_ref[s, K:KT] = k
            out_ref[s, KT:V] = kt
            out_ref[s, V:VT] = v
            out_ref[s, VT:QT] = vt
            out_ref[s, QT:Q] = qt[at : at + THIRD]
            out_ref[s, Q:TAG] = q[at : at + THIRD]
            out_ref[s, TAG:MSG] = clips[t]
        if h % SPAN == SPAN - 1:
            out_ref[worker(h, 0) + PARTS] = jnp.zeros((MSG, HD), bf16)


def in_hbm(x):
    return pltpu.with_memory_space_constraint(x, pltpu.HBM)


def in_vmem(x):
    return pltpu.with_memory_space_constraint(x, pltpu.VMEM)


def pack(side, arrays, freq, positions, segments):
    return pl.pallas_call(
        pack_kernel,
        in_specs=[pl.BlockSpec(memory_space=pltpu.SMEM)] + [ANY] * 6 + [VMEM] * 3,
        out_specs=[VMEM, VMEM],
        out_shape=[pltpu.VMEM((CHIPS, MSG, HD), bf16), pltpu.VMEM((ROWS, HD), f32)],
        scratch_shapes=[
            pltpu.VMEM((6, ROWS, NH * HD), bf16),
            pltpu.SemaphoreType.DMA((NH // SPAN, 6)),
        ],
        compiler_params=params(40),
    )(side, *[in_hbm(x) for x in (*arrays, freq, positions, segments)])


def bits(tiles):
    rows = jnp.concatenate([t.astype(f32)[0:1, :] for t in tiles], axis=0)
    lane = lax.broadcasted_iota(i32, (CHIPS, HD), 1)
    at = lax.broadcasted_iota(i32, (CHIPS, 1), 0)
    power = jnp.left_shift(jnp.ones((CHIPS, 1), i32), at & 15).astype(f32)
    has0 = 1.0 - jnp.min(jnp.where(lane < 32, 1.0, rows), axis=1, keepdims=True)
    has1 = jnp.max(jnp.where(lane < 32, 0.0, rows), axis=1, keepdims=True)

    def scalar(has):
        low = jnp.sum(jnp.where(at < 16, has * power, 0.0)).astype(i32)
        high = jnp.sum(jnp.where(at < 16, 0.0, has * power)).astype(i32)
        return low | (high << 16)

    return scalar(has0), scalar(has1)


def attn_kernel(q_ref, kv_ref, *refs, second):
    long_ref, short_ref, pen_ref, keys_ref, kind_ref, chips_ref, cut_ref = refs[-7:]
    copies = []
    if second:
        old_ref, old_stat_ref, out_ref, acc_ref, stat_ref = refs[:-7]
    else:
        n = (len(refs) - 10) // 2
        acc_ref, stat_ref = refs[n : n + 2]
        sem = refs[-8]
        for src, dst in zip(refs[:n], refs[n + 2 : 2 * n + 2]):
            cuts = FETCHES if src.shape[0] % (16 * FETCHES) == 0 else 1
            step = src.shape[0] // cuts
            for i in range(cuts):
                rows = slice(i * step, (i + 1) * step)
                copies.append(pltpu.make_async_copy(src.at[rows], dst.at[rows], sem.at[len(copies)]))
                copies[-1].start()
    asks = bits([q_ref[j, TAG:MSG, :] for j in range(CHIPS)])
    holds = bits([kv_ref[j, TAG:MSG, :] for j in range(CHIPS)]) if second else asks
    cut_ref[0] = i32(0)
    cut_ref[1] = i32(0)

    def sort(j, carry):
        cuts, counts = carry[0], list(carry[1:])
        has = [(holds[c] >> j) & 1 for c in range(2)]
        both = has[0] & has[1]
        cut_ref[jnp.where(both == 1, jnp.minimum(cuts, 1), 2)] = j
        for c in range(2):
            at = jnp.where(has[c] == 1, counts[c], 31 - (j - counts[c]))
            keys_ref[c, at] = j
            kind_ref[c, at] = jnp.where(both == 1, 2 + 2 * c + jnp.minimum(cuts, 1), 1 - has[c])
            counts[c] = counts[c] + has[c]
            ask = (asks[c] >> j) & 1
            n = counts[2 + c]
            chips_ref[c, jnp.where(ask == 1, n, 31 - (j - n))] = j
            counts[2 + c] = n + ask
        return (cuts + both, *counts)

    zero = i32(0)
    counted = lax.fori_loop(0, CHIPS, sort, (zero,) * 5)
    long_clip = jnp.where(counted[4] > 16, 1, 0)

    lane = lax.broadcasted_iota(i32, (ROWS, HD), 1)
    eye = lane == lax.broadcasted_iota(i32, (ROWS, HD), 0) + 32
    pen_ref[0] = jnp.zeros((ROWS, HD), bf16)
    pen_ref[1] = jnp.where(lane == 0, neg_fill, 0.0).astype(bf16)
    for p in range(2):
        row = kv_ref[cut_ref[p], TAG:MSG, :].astype(f32)[0:1, :]
        col = jnp.sum(jnp.where(eye, row, 0.0), axis=1, keepdims=True)
        pen_ref[2 + p] = jnp.where(lane == 0, col * neg_fill, 0.0).astype(bf16)
        pen_ref[4 + p] = jnp.where(lane == 0, (1.0 - col) * neg_fill, 0.0).astype(bf16)

    held = []
    for (chips, blocks), clip, base, s_ref in ((LONG, long_clip, 0, long_ref), (SHORT, 1 - long_clip, RLONG, short_ref)):
        R = chips * THIRD
        here = slice(base, base + R)
        listed = [chips_ref[clip, i] for i in range(chips)]
        qt, q = [jnp.concatenate([q_ref[j, at : at + THIRD, :] for j in listed], axis=0) for at in (QT, Q)]
        qq = jnp.concatenate([qt, q], axis=1)
        one = jnp.where(lax.broadcasted_iota(i32, (R, HD), 1) == 0, 1.0, 0.0).astype(bf16)
        q = jnp.concatenate([q, one], axis=1)
        m = old_stat_ref[here, 0:HD] if second else jnp.full((R, HD), neg_fill, f32)
        places = [(b, range(sum(blocks[:b]), sum(blocks[: b + 1])), -(-n * ROWS // 256) * 256) for b, n in enumerate(blocks)]
        for b, span, width in places:
            gap = width - len(span) * ROWS
            parts = [jnp.concatenate([kv_ref[keys_ref[clip, i], K:KT, :], pen_ref[kind_ref[clip, i]]], axis=1) for i in span]
            parts += [jnp.concatenate([jnp.zeros((gap, HD), bf16), pen_ref[1, 0:gap, :]], axis=1)] * (gap > 0)
            s = lax.dot_general(q, jnp.concatenate(parts, axis=0), NT, preferred_element_type=f32)
            s_ref[b, 0:R, 0:width] = s
            for j in range(width // HD):
                m = jnp.maximum(m, s[:, j * HD : (j + 1) * HD])
        top = jnp.max(m, axis=1, keepdims=True)
        m_old = old_stat_ref[here, 0:1] if second else None
        held.append((clip, here, s_ref, listed, qq, places, top, m_old, R))
    for clip, here, s_ref, listed, qq, places, top, m_old, R in held:
        for b, span, width in places:
            gap = width - len(span) * ROWS
            fill = [jnp.zeros((gap, HD), bf16)] * (gap > 0)
            js = [keys_ref[clip, i] for i in span]
            k, kt, v, vt = [jnp.concatenate([kv_ref[j, at : at + ROWS, :] for j in js] + fill, axis=0) for at in (K, KT, V, VT)]
            k = jnp.concatenate([k, kt], axis=1)
            v1 = jnp.concatenate([v, jnp.ones((width, HD), bf16)], axis=1)
            v = jnp.concatenate([v, vt], axis=1)
            st = lax.dot_general(qq, k, NT, preferred_element_type=f32)
            p = jnp.exp2(s_ref[b, 0:R, 0:width] - top)
            pt = (p * st).astype(bf16)
            l = p[:, 0:HD]
            for j in range(1, width // HD):
                l = l + p[:, j * HD : (j + 1) * HD]
            acc = jnp.dot(p.astype(bf16), v, preferred_element_type=f32)
            acct = jnp.dot(pt, v1, preferred_element_type=f32)
            if b > 0 or second:
                fade = jnp.exp2(m_old - top) if b == 0 else None
                l += stat_ref[here, HD:] if b > 0 else old_stat_ref[here, HD:] * fade
                acc += acc_ref[here, 0:256] if b > 0 else old_ref[here, 0:256] * fade
                acct += acc_ref[here, 256:512] if b > 0 else old_ref[here, 256:512] * fade
            stat_ref[here, HD:] = l
            acc_ref[here, 0:256] = acc
            acc_ref[here, 256:512] = acct
        if not second:
            stat_ref[here, 0:HD] = jnp.broadcast_to(top, (R, HD))
            continue
        total = jnp.sum(stat_ref[here, HD:], axis=1, keepdims=True)
        inv = 1.0 / total
        inv_tan = inv * ln2
        drift = acc_ref[here, 384:512] * inv_tan
        o = acc_ref[here, 0:128] * inv
        t = acc_ref[here, 256:384] * inv_tan + acc_ref[here, 128:256] * inv - drift * o
        wanted = clip.astype(f32)
        for i, j in enumerate(listed):
            at = i * W
            tags = q_ref[j, TAG:MSG, :].astype(f32)
            tag = jnp.concatenate([tags[:, 0:1], tags[:, 1:2]], axis=0)
            hit = jnp.broadcast_to(tag, (W, HD)) == wanted
            for n, x in enumerate((o, t)):
                lanes = slice(n * HD, (n + 1) * HD)
                old = out_ref[j, :, lanes].astype(f32)
                out_ref[j, :, lanes] = jnp.where(hit, x[at : at + W], old).astype(bf16)
    for copy in copies:
        copy.wait()


FETCHES = 2


def scratch():
    lists = [pltpu.SMEM((2, CHIPS), i32)] * 3 + [pltpu.SMEM((3,), i32)]
    scores = [pltpu.VMEM((len(LONG[1]), RLONG, KR), f32), pltpu.VMEM((len(SHORT[1]), RSHORT, KR), f32)]
    return scores + [pltpu.VMEM((6, ROWS, HD), bf16)] + lists


def attend(arrived, later):
    outs = pl.pallas_call(
        lambda *refs: attn_kernel(*refs, second=False),
        in_specs=[VMEM] * 2 + [ANY] * len(later),
        out_specs=[VMEM] * (2 + len(later)),
        out_shape=[pltpu.VMEM((RALL, 512), f32), pltpu.VMEM((RALL, 2 * HD), f32)] + [pltpu.VMEM(x.shape, x.dtype) for x in later],
        scratch_shapes=[pltpu.SemaphoreType.DMA((FETCHES * len(later),))] + scratch(),
        compiler_params=params(28),
        cost_estimate=pl.CostEstimate(flops=5 * 10**9, bytes_accessed=20 * 2**20, transcendentals=2 * 10**6),
    )(in_vmem(arrived), in_vmem(arrived), *[in_hbm(x) for x in later])
    return outs[:2], outs[2:]


def attend_more(arrived, swapped, state):
    return pl.pallas_call(
        lambda *refs: attn_kernel(*refs, second=True),
        in_specs=[VMEM] * 4,
        out_specs=VMEM,
        out_shape=pltpu.VMEM((CHIPS, W, 2 * HD), bf16),
        scratch_shapes=[pltpu.VMEM((RALL, 512), f32), pltpu.VMEM((RALL, 2 * HD), f32)] + scratch(),
        compiler_params=params(28),
        cost_estimate=pl.CostEstimate(flops=5 * 10**9, bytes_accessed=8 * 2**20, transcendentals=2 * 10**6),
    )(*[in_vmem(x) for x in (arrived, swapped, *state)])


CT = 256
SENDS = 10
PIECE = HALF // SENDS
STEPS = PIECE // CT


def project_kernel(side_ref, x_ref, w_ref, seg_ref, gate_ref, gate_tan_ref, *refs, own, part):
    if own:
        resid_ref, resid_tan_ref, send_ref, lhs_ref = refs
    else:
        send_ref, lhs_ref = refs
    side = side_ref[0] if own else 1 - side_ref[0]
    start = side * HALF + part * PIECE
    for h in range(NH):
        for t in range(PARTS):
            s = worker(h, t)
            lhs_ref[t * W : (t + 1) * W, h * HD : (h + 1) * HD] = x_ref[s, :, 0:HD]
            lhs_ref[ROWS + t * W : ROWS + (t + 1) * W, h * HD : (h + 1) * HD] = x_ref[s, :, HD : 2 * HD]
    one = seg_ref[:, 0:1] == 1.0
    for j in range(STEPS):
        cols = pl.ds(pl.multiple_of(start + j * CT, CT), CT)
        out = jnp.dot(lhs_ref[...], w_ref[:, cols], preferred_element_type=f32)
        here = slice(j * CT, (j + 1) * CT)
        gate = jnp.where(one, gate_ref[1:2, cols], gate_ref[0:1, cols])
        gate_tan = jnp.where(one, gate_tan_ref[1:2, cols], gate_tan_ref[0:1, cols])
        a = gate * out[0:ROWS]
        b = gate_tan * out[0:ROWS] + gate * out[ROWS : 2 * ROWS]
        if own:
            a = a + resid_ref[:, part * PIECE + j * CT : part * PIECE + (j + 1) * CT]
            b = b + resid_tan_ref[:, part * PIECE + j * CT : part * PIECE + (j + 1) * CT]
        send_ref[0, :, here] = a.astype(bf16)
        send_ref[1, :, here] = b.astype(bf16)


def project(side, x, w, seg, gate, gate_tan, resid, part):
    own = len(resid) > 0
    return pl.pallas_call(
        lambda *refs: project_kernel(*refs, own=own, part=part),
        in_specs=[pl.BlockSpec(memory_space=pltpu.SMEM)] + [VMEM] * (5 + len(resid)),
        out_specs=VMEM,
        out_shape=pltpu.VMEM((2, ROWS, PIECE), bf16),
        scratch_shapes=[
            pltpu.VMEM((2 * ROWS, NH * HD), bf16),
        ],
        compiler_params=params(16),
        cost_estimate=pl.CostEstimate(flops=2 * 2 * ROWS * NH * HD * HALF, bytes_accessed=10 * 2**20, transcendentals=0),
    )(side, *[in_vmem(x) for x in (x, w, seg, gate, gate_tan, *resid)])


FT, FN = 16, 16


def moments(a, b):
    lane = lax.broadcasted_iota(i32, (a.shape[0], HD), 1)
    out = jnp.zeros((a.shape[0], HD), f32)
    for i, x in enumerate((a, a * a, b, a * b)):
        out = jnp.where(lane == i, jnp.sum(x, axis=1, keepdims=True), out)
    return out


def settle_kernel(*refs):
    kept, got, refs = refs[:SENDS], refs[SENDS : 2 * SENDS], refs[2 * SENDS :]
    seg_ref, tables, (pass_ref, a_ref, b_ref, sums_ref, rows_ref, resid_hbm, resid_tan_hbm, sem) = refs[0], refs[1:5], refs[5:]
    del pass_ref
    copies = []
    for step in range(ROWS // FT):
        at = slice(step * FT, (step + 1) * FT)
        a, b = (jnp.concatenate([x[i, at].astype(f32) + y[i, at].astype(f32) for x, y in zip(kept, got)], axis=1) for i in range(2))
        a_ref[at] = a
        b_ref[at] = b
        sums_ref[at] = moments(a, b)
        for i, (src, dst) in enumerate(((a_ref, resid_hbm), (b_ref, resid_tan_hbm))):
            copies.append(pltpu.make_async_copy(src.at[at], dst.at[at], sem.at[step, i]))
            copies[-1].start()
    one = seg_ref[:, 0:1] == 1.0
    for i, table in enumerate(tables):
        row = jnp.where(one, table[1:2, :], table[0:1, :])
        rows_ref[i] = row + 1.0 if i == 0 else row
    for copy in copies:
        copy.wait()


def settle(kept, got, seg, tables):
    half, out = pltpu.VMEM((ROWS, HALF), f32), jax.ShapeDtypeStruct((ROWS, HALF), f32)
    return pl.pallas_call(
        settle_kernel,
        in_specs=[VMEM] * (2 * SENDS + 5),
        out_specs=[VMEM] * 5 + [ANY] * 2,
        out_shape=[pltpu.VMEM((2, ROWS, PIECE), bf16), half, half, pltpu.VMEM((ROWS, HD), f32), pltpu.VMEM((4, ROWS, D), f32), out, out],
        input_output_aliases={SENDS - 1: 0},
        scratch_shapes=[pltpu.SemaphoreType.DMA((ROWS // FT, 2))],
        compiler_params=params(16),
    )(*[in_vmem(x) for x in (*kept, *got, seg, *tables)])


def norm_kernel(side_ref, *refs):
    rows = [refs[i * SENDS : (i + 1) * SENDS] for i in range(2)]
    a_ref, b_ref, sums_ref, rows_ref = refs[2 * SENDS : 2 * SENDS + 4]
    outs, held, sem = refs[2 * SENDS + 4 : 2 * SENDS + 6], refs[2 * SENDS + 6 : 2 * SENDS + 8], refs[-1]
    ffn_ref, ffn_tan_ref = held
    copies = []
    for step in range(ROWS // FN):
        at = slice(step * FN, (step + 1) * FN)
        a, b = (jnp.concatenate([x[i, at].astype(f32) + y[i, at].astype(f32) for x, y in zip(*rows)], axis=1) for i in range(2))
        total = (moments(a, b) + sums_ref[at]) / D
        mean, mean_tan = total[:, 0:1], total[:, 2:3]
        rstd = lax.rsqrt(total[:, 1:2] - mean * mean + norm_eps)
        cov = total[:, 3:4] - mean * mean_tan
        slope = rstd * rstd * rstd * cov
        for side, x, y in ((1 - side_ref[0], a, b), (side_ref[0], a_ref[at], b_ref[at])):
            cols = pl.ds(pl.multiple_of(side * HALF, HALF), HALF)
            centered = x - mean
            normed = centered * rstd
            normed_tan = (y - mean_tan) * rstd - centered * slope
            scale, scale_tan, shift, shift_tan = (rows_ref[i, at, cols] for i in range(4))
            ffn_ref[at, cols] = (normed * scale + shift).astype(bf16)
            ffn_tan_ref[at, cols] = (normed_tan * scale + normed * scale_tan + shift_tan).astype(bf16)
        for i in range(2):
            copies.append(pltpu.make_async_copy(held[i].at[at], outs[i].at[at], sem.at[step, i]))
            copies[-1].start()
    for copy in copies:
        copy.wait()


def norm(side, other, got_other, settled):
    outs = [jax.ShapeDtypeStruct((ROWS, D), bf16)] * 2
    return pl.pallas_call(
        norm_kernel,
        in_specs=[pl.BlockSpec(memory_space=pltpu.SMEM)] + [VMEM] * (2 * SENDS + 4),
        out_specs=[ANY] * 2,
        out_shape=outs,
        scratch_shapes=[pltpu.VMEM(x.shape, x.dtype) for x in outs] + [pltpu.SemaphoreType.DMA((ROWS // FN, 2))],
        compiler_params=params(32),
    )(side, *[in_vmem(x) for x in (*other, *got_other, *settled)])


def body(
    queries, keys, values, queries_tan, keys_tan, values_tan, segments, positions, out_weight,
    residual, residual_tan, gate, gate_tan, mod_scale, mod_scale_tan, mod_shift, mod_shift_tan,
):
    frequency = np.float32(rope_base) ** (-np.arange(HD // 2, dtype=np.float32) / np.float32(HD // 2))
    freq = np.concatenate([frequency, frequency])[None, :].astype(np.float32)
    swap = [(0, 1), (1, 0)]

    side = lax.axis_index("head").astype(i32).reshape(1)
    with jax.named_scope("pack"):
        arrays = (queries, keys, values, queries_tan, keys_tan, values_tan)
        message, seg = pack(side, arrays, freq, positions[None, :], segments[None, :])
    with jax.named_scope("spread"):
        arrived = lax.all_to_all(message, ("x", "y", "z"), 0, 0, tiled=True)
        swapped = lax.ppermute(arrived, "c", swap)
    with jax.named_scope("attend"):
        later = (out_weight, gate, gate_tan, residual, residual_tan, mod_scale, mod_scale_tan, mod_shift, mod_shift_tan)
        state, later = attend(arrived, later)
        held_weight, held_gate, held_gate_tan, held_resid, held_resid_tan, *tables = later
        answer = attend_more(arrived, swapped, state)
    with jax.named_scope("collect"):
        attended = lax.all_to_all(answer, ("x", "y", "z"), 0, 0, tiled=True)
    with jax.named_scope("project"):
        args = (attended, held_weight, seg, held_gate, held_gate_tan)
        other = [project(side, *args, (), part) for part in range(SENDS)]
        got_mine = [lax.ppermute(x, "head", swap) for x in other]
        mine = [project(side, *args, (held_resid, held_resid_tan), part) for part in range(SENDS)]
        got_other = [lax.ppermute(x, "head", swap) for x in mine[:-1]]
        last, *settled, resid, resid_tan = settle(mine, got_mine, seg, tables)
        got_other.append(lax.ppermute(last, "head", swap))
    with jax.named_scope("norm"):
        ffn, ffn_tan = norm(side, other, got_other, settled)
    return resid, resid_tan, ffn, ffn_tan


def solution(mesh):
    fine = Mesh(mesh.devices.reshape(4, 4, 2, 2, 2), ("z", "y", "x", "c", "head"))
    seq = ("z", "y", "x", "c")
    split = P(seq, "head")
    in_specs = (split,) * 6 + (P(seq), P(seq), P("head", None), split, split) + (P(),) * 6
    out_specs = (split, split, P(seq, None), P(seq, None))
    return jax.shard_map(body, mesh=fine, in_specs=in_specs, out_specs=out_specs, check_vma=False)
```
